128 devices in a mesh: row: 16 (over x, y), col: 8 (over z, core).
Axes of the slice: x: 4, y: 4, z: 4, core: 2. Of those that a mesh axis runs over, the one named last changes fastest.
Arguments:
- nodes: bfloat16 [49152, 768], P(('row', 'col')), may hold values from -6 to 6
- w_query: bfloat16 [768, 768], replicated, may hold values from -0.4375 to 0.4375
- w_key: bfloat16 [768, 768], replicated, may hold values from -0.21875 to 0.21875
- w_value: bfloat16 [768, 768], replicated, may hold values from -0.21875 to 0.21875
- w_out: bfloat16 [768, 768], replicated, may hold values from -0.21875 to 0.21875
- w_edge_gate: bfloat16 [64, 8], replicated, may hold values from -0.75 to 0.75
- w_edge_bias: bfloat16 [64, 8], replicated, may hold values from -0.75 to 0.75
- w_edge_out: float32 [8, 64], replicated, may hold values from -2 to 2
- gain_node: float32 [768], replicated, may hold values from 0.1 to 1.9
- gain_edge: float32 [64], replicated, may hold values from 0.1 to 1.9
- edges: bfloat16 [16, 8, 4, 64, 128, 128], P('row', 'col'), may hold values from -6 to 6
- tile_list: int32 [16, 8, 4], P('row', 'col'), may hold values from 0 to 1151, as said below
- tile_count: int32 [16, 8], P('row', 'col'), may hold values from 1 to 4, as said below
Outputs:
- nodes_out: bfloat16 [49152, 768], P(('row', 'col'))
- edges_out: bfloat16 [16, 8, 4, 64, 128, 128], P('row', 'col')
The draws below stay inside these ranges and needn't reach their ends.
Inputs may be any that keep to these rules, and one draw needn't show every extreme that they name: `tile_list`: the destination blocks of the 4 slots of one device are distinct. `tile_count`: some device has all 4 slots live.
All inputs are finite; a program needn't handle non-finite values.
Results may differ from the reference program's by a relative error of at most 0.0075.
Values may be sent and summed in bfloat16 or wider, within the bound.
A program may use at most 192 MiB of HBM per device.

```python
import jax
import jax.numpy as jnp
from jax import lax

D = 768
HEADS = 8
EDGE_CH = 64
BLOCK = 128
NODE_DEV = 384
CAP = 4
NODES = 49152
DEST_BLOCKS = 24
SRC_BLOCKS = 48
N_ROW = 16
N_COL = 8


def draw_tile_list(key, part):
    key = jax.random.fold_in(key, 11)
    positions = jnp.arange(N_ROW * N_COL, dtype=jnp.int32).reshape(N_ROW, N_COL)
    chosen = jax.random.randint(jax.random.fold_in(key, 3), (), 0, N_ROW * N_COL)
    is_chosen = positions == chosen
    block_ids = jnp.arange(DEST_BLOCKS, dtype=jnp.int32)
    base = jax.random.randint(jax.random.fold_in(key, 1), (N_ROW, N_COL, DEST_BLOCKS), 0, 65536)
    lift = jnp.where(is_chosen[:, :, None] & (block_ids == DEST_BLOCKS - 1)[None, None, :], 65536, 0)
    dest_scores = (base + lift) * DEST_BLOCKS + block_ids
    dest_blocks = lax.top_k(dest_scores, CAP)[1].astype(jnp.int32)
    src_blocks = jax.random.randint(jax.random.fold_in(key, 2), (N_ROW, N_COL, CAP), 0, SRC_BLOCKS)
    slot_ids = jnp.arange(CAP, dtype=jnp.int32)
    src_blocks = jnp.where(is_chosen[:, :, None] & (slot_ids == 0)[None, None, :], SRC_BLOCKS - 1, src_blocks)
    return (dest_blocks * SRC_BLOCKS + src_blocks).astype(jnp.int32)


def draw_tile_count(key, part):
    key = jax.random.fold_in(key, 23)
    coins = jax.random.randint(jax.random.fold_in(key, 1), (N_ROW, N_COL), 0, 4)
    counts = jnp.where(coins == 0, CAP, jnp.where(coins == 1, 1, min(2, CAP)))
    chosen = jax.random.randint(jax.random.fold_in(key, 2), (), 0, N_ROW * N_COL)
    positions = jnp.arange(N_ROW * N_COL, dtype=jnp.int32).reshape(N_ROW, N_COL)
    return jnp.where(positions == chosen, CAP, counts).astype(jnp.int32)


def block_levels(key, dims, cuts, least, largest):
    def one(position, parts):
        heights = jax.random.uniform(jax.random.fold_in(jax.random.fold_in(key, 6), position), (parts,), jnp.float32, least / len(cuts), largest / len(cuts))
        return jnp.repeat(jnp.exp(heights), dims[position] // parts).reshape((-1,) + (1,) * (len(dims) - position - 1))

    factor_of = one(*cuts[0])
    for cut in cuts[1:]:
        factor_of = factor_of * one(*cut)
    return factor_of


def noise(own_key, dims, scale, reach, pieces=(), kind=jnp.bfloat16):
    loudness = block_levels(own_key, dims, pieces, -0.22, 0.18) if pieces else 1.0
    array = jax.random.normal(own_key, dims, jnp.float32) * scale * loudness
    return jnp.minimum(jnp.maximum(array, -reach), reach).astype(kind)


def setup_inputs(seed: int = 0) -> dict:
    keys = jax.random.split(jax.random.key(seed), 14)
    return {
        "nodes": noise(keys[0], (NODES, D), 1.0, 6.0, ((0, 128),)),
        "w_query": noise(keys[1], (D, D), (D // 4) ** -0.5, 0.4375),
        "w_key": noise(keys[2], (D, D), D ** -0.5, 0.21875),
        "w_value": noise(keys[3], (D, D), D ** -0.5, 0.21875),
        "w_out": noise(keys[4], (D, D), D ** -0.5, 0.21875),
        "w_edge_gate": noise(keys[5], (EDGE_CH, HEADS), EDGE_CH ** -0.5, 0.75),
        "w_edge_bias": noise(keys[6], (EDGE_CH, HEADS), EDGE_CH ** -0.5, 0.75),
        "w_edge_out": noise(keys[7], (HEADS, EDGE_CH), HEADS ** -0.5, 2.0, (), jnp.float32),
        "gain_node": jnp.clip(1.0 + 0.18 * jax.random.normal(keys[8], (D,), jnp.float32), 0.1, 1.9),
        "gain_edge": jnp.clip(1.0 + 0.18 * jax.random.normal(keys[9], (EDGE_CH,), jnp.float32), 0.1, 1.9),
        "edges": noise(keys[10], (N_ROW, N_COL, CAP, EDGE_CH, BLOCK, BLOCK), 1.0, 6.0, ((0, 16), (1, 8))),
        "tile_list": draw_tile_list(jax.random.fold_in(keys[13], 71), 0),
        "tile_count": draw_tile_count(jax.random.fold_in(keys[13], 71), 0),
    }


def tile_step(query_block, pair_block, edge, w_edge_gate, w_edge_bias, w_edge_out, gain_edge, is_live):
    width = query_block.shape[1]
    head_dim = width // HEADS
    query_heads = query_block.astype(jnp.float32).reshape(BLOCK, HEADS, head_dim)
    key_heads = pair_block[:, :width].astype(jnp.float32).reshape(BLOCK, HEADS, head_dim)
    value_heads = pair_block[:, width:].astype(jnp.float32).reshape(BLOCK, HEADS, head_dim)
    raw = jnp.einsum('ihd,jhd->hij', query_heads, key_heads) * (1.0 / head_dim ** 0.5)
    edge_float = edge.astype(jnp.float32)
    bias = jnp.einsum('cij,ch->hij', edge_float, w_edge_bias.astype(jnp.float32))
    gate = jnp.einsum('cij,ch->hij', edge_float, w_edge_gate.astype(jnp.float32))
    score = jnp.clip(raw, -5.0, 5.0) + bias
    expo = jnp.exp(score) * is_live
    weight = expo * jax.nn.sigmoid(gate)
    weight_b = lax.optimization_barrier(weight.astype(jnp.bfloat16)).astype(jnp.float32)
    denom_part = lax.optimization_barrier(jnp.sum(expo, axis=2)).T
    numer_part = jnp.einsum('hij,jhd->ihd', weight_b, value_heads).reshape(BLOCK, width)
    edge_mixed = edge_float + jnp.einsum('hij,hc->cij', score, w_edge_out, precision=lax.Precision.HIGHEST)
    square_mean = lax.optimization_barrier(jnp.mean(edge_mixed * edge_mixed, axis=0, keepdims=True))
    edge_new = edge_mixed * lax.rsqrt(square_mean + 1e-05) * gain_edge[:, None, None] * is_live
    return (numer_part, denom_part, edge_new.astype(jnp.bfloat16))

def reference(nodes, w_query, w_key, w_value, w_out, w_edge_gate, w_edge_bias, w_edge_out, gain_node, gain_edge, edges, tile_list, tile_count):
    width = nodes.shape[1]
    head_dim = width // HEADS
    total_nodes = nodes.shape[0]
    queries = jnp.dot(nodes, w_query, preferred_element_type=jnp.float32).astype(jnp.bfloat16)
    pair = jnp.dot(nodes, jnp.concatenate([w_key, w_value], axis=1), preferred_element_type=jnp.float32).astype(jnp.bfloat16)
    src_blocks = NODE_DEV * N_ROW // BLOCK
    flat_edges = edges.reshape(N_ROW * N_COL * CAP, EDGE_CH, BLOCK, BLOCK)
    flat_tiles = tile_list.reshape(-1).astype(jnp.int32)
    flat_counts = tile_count.reshape(-1).astype(jnp.int32)
    indices = jnp.arange(N_ROW * N_COL * CAP, dtype=jnp.int32)

    def visit(carry, element):
        numer, denom = carry
        index, edge, tile = element
        device = index // CAP
        slot = index % CAP
        row_index = device // N_COL
        col_index = device % N_COL
        is_live = (slot < flat_counts[device]).astype(jnp.float32)
        dest_start = (row_index * N_COL * NODE_DEV + tile // src_blocks * BLOCK).astype(jnp.int32)
        local_src = tile % src_blocks * BLOCK
        src_start = ((local_src // NODE_DEV * N_COL + col_index) * NODE_DEV + local_src % NODE_DEV).astype(jnp.int32)
        query_block = lax.dynamic_slice_in_dim(queries, dest_start, BLOCK, 0)
        pair_block = lax.dynamic_slice_in_dim(pair, src_start, BLOCK, 0)
        numer_part, denom_part, edge_new = tile_step(query_block, pair_block, edge, w_edge_gate, w_edge_bias, w_edge_out, gain_edge, is_live)
        numer = lax.dynamic_update_slice_in_dim(numer, lax.dynamic_slice_in_dim(numer, dest_start, BLOCK, 0) + numer_part, dest_start, 0)
        denom = lax.dynamic_update_slice_in_dim(denom, lax.dynamic_slice_in_dim(denom, dest_start, BLOCK, 0) + denom_part, dest_start, 0)
        return ((numer, denom), edge_new)
    start_state = (jnp.zeros((total_nodes, width), jnp.float32), jnp.zeros((total_nodes, HEADS), jnp.float32))
    (numer, denom), new_edges = lax.scan(visit, start_state, (indices, flat_edges, flat_tiles))
    safe_denom = jnp.where(denom > 0.0, denom, 1.0)
    attended = (numer.reshape(total_nodes, HEADS, head_dim) / safe_denom[:, :, None]).reshape(total_nodes, width).astype(jnp.bfloat16)
    mixed = nodes.astype(jnp.float32) + jnp.dot(attended, w_out, preferred_element_type=jnp.float32)
    square_mean = lax.optimization_barrier(jnp.mean(mixed * mixed, axis=1, keepdims=True))
    nodes_out = (mixed * lax.rsqrt(square_mean + 1e-05) * gain_node).astype(jnp.bfloat16)
    return (nodes_out, new_edges.reshape(edges.shape))
```

```python
import jax
import jax.numpy as jnp
from jax import lax
from jax.experimental import pallas as pl
from jax.experimental.pallas import tpu as pltpu
from jax.sharding import PartitionSpec as P

HEADS = 8
BLOCK = 128
CH = 64
GROUP = 16
F32 = jnp.float32
BF16 = jnp.bfloat16
NT = (((1,), (1,)), ((), ()))


def iota(shape, dim):
    return lax.broadcasted_iota(jnp.int32, shape, dim)


def dot(a, b, dims=(((1,), (0,)), ((), ()))):
    return lax.dot_general(a, b, dims, preferred_element_type=F32)


def where01(mask):
    return jnp.where(mask, 1.0, 0.0).astype(BF16)


def build_maps(wb_ref, wg_ref, wo_ref, mix_map, out_map):
    rows, cols = 2 * HEADS * GROUP, CH * GROUP
    pick = iota((rows, HEADS), 0) // GROUP
    head = iota((rows, HEADS), 1)
    picked = dot(where01(pick == head), wb_ref[...], NT) + dot(
        where01(pick == head + HEADS), wg_ref[...], NT
    )
    spread = where01(iota((CH, cols), 0) == iota((CH, cols), 1) // GROUP)
    full = dot(picked.astype(BF16), spread)
    same = iota((rows, cols), 0) % GROUP == iota((rows, cols), 1) % GROUP
    mix_map[...] = jnp.where(same, full, 0.0).astype(BF16)
    narrow = HEADS * GROUP
    w_out = wo_ref[...]
    high = w_out.astype(BF16)
    low = (w_out - high.astype(F32)).astype(BF16)
    pick = where01(iota((cols, CH), 0) // GROUP == iota((cols, CH), 1))
    spread = where01(iota((HEADS, narrow), 0) == iota((HEADS, narrow), 1) // GROUP)
    same = iota((cols, narrow), 0) % GROUP == iota((cols, narrow), 1) % GROUP
    for part, w in enumerate((high, low)):
        full = dot(dot(pick, w, NT).astype(BF16), spread)
        out_map[:, part * narrow : (part + 1) * narrow] = jnp.where(same, full, 0.0).astype(BF16)


def tile_kernel(
    count_ref,
    gain_ref,
    dest_ref,
    src_ref,
    wq_ref,
    wk_ref,
    wv_ref,
    wb_ref,
    wg_ref,
    wo_ref,
    edge_ref,
    numer_ref,
    denom_ref,
    out_ref,
    q_s,
    k_s,
    v_s,
    mix_map,
    out_map,
    raw_s,
    weight_s,
    expo_s,
    mixed_s,
):
    slot = pl.program_id(0)
    width = q_s.shape[-1]
    head_dim = width // HEADS
    tiles = width // 128

    @pl.when(slot == 0)
    def _():
        build_maps(wb_ref, wg_ref, wo_ref, mix_map, out_map)
        for w_ref, x_ref, y_s in ((wq_ref, dest_ref, q_s), (wk_ref, src_ref, k_s), (wv_ref, src_ref, v_s)):
            x = x_ref[...].reshape(-1, width)
            for n in range(0, width, 256):
                y = dot(x, w_ref[:, n : n + 256]).astype(BF16)
                y_s[:, :, n : n + 256] = y.reshape(-1, BLOCK, 256)

    @pl.when(slot >= count_ref[0])
    def _():
        numer_ref[...] = jnp.zeros_like(numer_ref)
        denom_ref[...] = jnp.zeros_like(denom_ref)
        out_ref[...] = jnp.zeros_like(out_ref)

    @pl.when(slot < count_ref[0])
    def _():
        for h in range(HEADS):
            lo, hi = h * head_dim, (h + 1) * head_dim
            a, b = lo // 128 * 128, -(-hi // 128) * 128
            lane = iota((BLOCK, b - a), 1) + a
            q = q_s[slot, :, a:b]
            q = jnp.where((lane >= lo) & (lane < hi), q, jnp.zeros_like(q))
            raw = dot(q, k_s[slot, :, a:b], NT)
            raw_s[h] = jnp.clip(raw * (1.0 / head_dim**0.5), -5.0, 5.0)

        def pair(g, _):
            def rows(side):
                return pl.ds(pl.multiple_of(g * (2 * GROUP) + side * GROUP, GROUP), GROUP)

            def both(f):
                return jnp.concatenate([f(0), f(1)], axis=1)

            edge2 = both(lambda side: edge_ref[0, :, rows(side), :].reshape(CH * GROUP, BLOCK))
            mix = dot(mix_map[...], edge2)
            bias, gate = mix[: HEADS * GROUP], mix[HEADS * GROUP :]
            score = both(lambda side: raw_s[:, rows(side), :].reshape(HEADS * GROUP, BLOCK)) + bias
            expo = jnp.exp(score)
            weight = (expo / (1.0 + jnp.exp(-gate))).astype(BF16)
            expo = expo.astype(BF16)
            for side in range(2):
                part = slice(side * BLOCK, (side + 1) * BLOCK)
                weight_s[:, rows(side), :] = weight[:, part].reshape(HEADS, GROUP, BLOCK)
                expo_s[:, rows(side), :] = expo[:, part].reshape(HEADS, GROUP, BLOCK)
            score = score.astype(BF16)
            mixed_s[...] = dot(out_map[...], jnp.concatenate([score, score], axis=0))
            for side in range(2):
                part = slice(side * BLOCK, (side + 1) * BLOCK)
                total = jnp.zeros((GROUP, BLOCK), F32)
                for c in range(CH):
                    m = mixed_s[c * GROUP : (c + 1) * GROUP, part] + edge_ref[0, c, rows(side), :].astype(F32)
                    mixed_s[c * GROUP : (c + 1) * GROUP, part] = m
                    total += m * m
                scale = lax.rsqrt(total * (1.0 / CH) + 1e-5)
                for c in range(CH):
                    m = mixed_s[c * GROUP : (c + 1) * GROUP, part]
                    out_ref[0, c, rows(side), :] = (m * (scale * gain_ref[c])).astype(BF16)
            return 0

        lax.fori_loop(0, BLOCK // (2 * GROUP), pair, 0)

        for m in range(tiles):
            heads = range(m * 128 // head_dim, (m * 128 + 127) // head_dim + 1)
            v = v_s[slot, :, m * 128 : (m + 1) * 128]
            lane = iota((BLOCK, 128), 1) + m * 128
            weights = jnp.concatenate([weight_s[h] for h in heads], axis=1)
            values = jnp.concatenate(
                [jnp.where(lane // head_dim == h, v, jnp.zeros_like(v)) for h in heads], axis=0
            )
            numer_ref[0, :, m * 128 : (m + 1) * 128] = dot(weights, values).astype(BF16)
        ones = where01(iota((HEADS, HEADS * BLOCK), 0) == iota((HEADS, HEADS * BLOCK), 1) // BLOCK)
        expo_all = jnp.concatenate([expo_s[h] for h in range(HEADS)], axis=1)
        denom_ref[0] = dot(ones, expo_all, NT)


def tile_call(count, gain_edge, dest, src, w_query, w_key, w_value, w_bias, w_gate, w_out, edges):
    slots, _, width = dest.shape
    vm = pl.BlockSpec(memory_space=pltpu.VMEM)
    sm = pl.BlockSpec(memory_space=pltpu.SMEM)
    edge_spec = pl.BlockSpec((1, CH, BLOCK, BLOCK), lambda s: (s, 0, 0, 0))
    return pl.pallas_call(
        tile_kernel,
        grid=(slots,),
        in_specs=[sm, sm] + [vm] * 8 + [edge_spec],
        out_specs=[
            pl.BlockSpec((1, BLOCK, width), lambda s: (s, 0, 0)),
            pl.BlockSpec((1, HEADS, BLOCK), lambda s: (s, 0, 0)),
            edge_spec,
        ],
        out_shape=[
            jax.ShapeDtypeStruct((slots, BLOCK, width), BF16),
            jax.ShapeDtypeStruct((slots, HEADS, BLOCK), F32),
            jax.ShapeDtypeStruct(edges.shape, BF16),
        ],
        scratch_shapes=[
            pltpu.VMEM((slots, BLOCK, width), BF16),
            pltpu.VMEM((slots, BLOCK, width), BF16),
            pltpu.VMEM((slots, BLOCK, width), BF16),
            pltpu.VMEM((2 * HEADS * GROUP, CH * GROUP), BF16),
            pltpu.VMEM((CH * GROUP, 2 * HEADS * GROUP), BF16),
            pltpu.VMEM((HEADS, BLOCK, BLOCK), F32),
            pltpu.VMEM((HEADS, BLOCK, BLOCK), BF16),
            pltpu.VMEM((HEADS, BLOCK, BLOCK), BF16),
            pltpu.VMEM((CH * GROUP, 2 * BLOCK), F32),
        ],
        compiler_params=pltpu.CompilerParams(vmem_limit_bytes=48 * 1024 * 1024),
        name="tile_work",
    )(count, gain_edge, dest, src, w_query, w_key, w_value, w_bias, w_gate, w_out, edges)


def on_device(
    nodes,
    w_query,
    w_key,
    w_value,
    w_out,
    w_edge_gate,
    w_edge_bias,
    w_edge_out,
    gain_node,
    gain_edge,
    edges,
    tile_list,
    tile_count,
):
    own_rows, width = nodes.shape
    head_dim = width // HEADS
    n_col = lax.axis_size("col")
    sources = lax.all_gather(nodes, "row", axis=0, tiled=True)
    dests = lax.all_gather(nodes, "col", axis=0, tiled=True)
    src_blocks = sources.shape[0] // BLOCK
    tiles = tile_list[0, 0]
    slots = tiles.shape[0]
    dest_id = tiles // src_blocks
    src_id = tiles % src_blocks
    dest = jnp.stack([lax.dynamic_slice_in_dim(dests, dest_id[s] * BLOCK, BLOCK, 0) for s in range(slots)])
    src = jnp.stack([lax.dynamic_slice_in_dim(sources, src_id[s] * BLOCK, BLOCK, 0) for s in range(slots)])
    numer, denom, edges_out = tile_call(
        tile_count.reshape(1),
        gain_edge,
        dest,
        src,
        w_query,
        w_key,
        w_value,
        w_edge_bias,
        w_edge_gate,
        w_edge_out,
        edges[0, 0],
    )
    dest_blocks = dests.shape[0] // BLOCK
    numer_all = jnp.zeros((dest_blocks, BLOCK, width), BF16)
    denom_all = jnp.zeros((dest_blocks, HEADS, BLOCK), F32)
    for s in range(slots):
        numer_all = lax.dynamic_update_slice(numer_all, numer[s : s + 1], (dest_id[s], 0, 0))
        denom_all = lax.dynamic_update_slice(denom_all, denom[s : s + 1], (dest_id[s], 0, 0))
    numer = lax.psum_scatter(numer_all, "col", scatter_dimension=0, tiled=True).astype(F32)
    denom = lax.psum_scatter(denom_all, "col", scatter_dimension=0, tiled=True)
    denom = denom.transpose(0, 2, 1).reshape(own_rows, HEADS, 1)
    numer = numer.reshape(own_rows, HEADS, head_dim)
    attended = jnp.where(denom > 0.0, numer / jnp.where(denom > 0.0, denom, 1.0), 0.0)
    attended = attended.reshape(own_rows, width).astype(BF16)
    mixed = nodes.astype(F32) + jnp.dot(attended, w_out, preferred_element_type=F32)
    square_mean = jnp.mean(mixed * mixed, axis=1, keepdims=True)
    nodes_out = (mixed * lax.rsqrt(square_mean + 1e-05) * gain_node).astype(BF16)
    return (nodes_out, edges_out[None, None])


def solution(mesh):
    return jax.shard_map(
        on_device,
        mesh=mesh,
        in_specs=(
            P(("row", "col"), None),
            *[P()] * 9,
            P("row", "col", None, None, None, None),
            P("row", "col", None),
            P("row", "col"),
        ),
        out_specs=(P(("row", "col"), None), P("row", "col", None, None, None, None)),
        check_vma=False,
    )
```

```python
import jax
import jax.numpy as jnp
from jax import lax
from jax.experimental import pallas as pl
from jax.experimental.pallas import tpu as pltpu
from jax.sharding import PartitionSpec as P

HEADS = 8
BLOCK = 128
CH = 64
GROUP = 16
F32 = jnp.float32
BF16 = jnp.bfloat16
NT = (((1,), (1,)), ((), ()))


def iota(shape, dim):
    return lax.broadcasted_iota(jnp.int32, shape, dim)


def dot(a, b, dims=(((1,), (0,)), ((), ()))):
    return lax.dot_general(a, b, dims, preferred_element_type=F32)


def where01(mask):
    return jnp.where(mask, 1.0, 0.0).astype(BF16)


def build_maps(wb_ref, wg_ref, wo_ref, mix_map, out_map):
    rows, cols = 2 * HEADS * GROUP, CH * GROUP
    pick = iota((rows, HEADS), 0) // GROUP
    head = iota((rows, HEADS), 1)
    picked = dot(where01(pick == head), wb_ref[...], NT) + dot(
        where01(pick == head + HEADS), wg_ref[...], NT
    )
    spread = where01(iota((CH, cols), 0) == iota((CH, cols), 1) // GROUP)
    full = dot(picked.astype(BF16), spread)
    same = iota((rows, cols), 0) % GROUP == iota((rows, cols), 1) % GROUP
    mix_map[...] = jnp.where(same, full, 0.0).astype(BF16)
    narrow = HEADS * GROUP
    w_out = wo_ref[...]
    high = w_out.astype(BF16)
    low = (w_out - high.astype(F32)).astype(BF16)
    pick = where01(iota((cols, CH), 0) // GROUP == iota((cols, CH), 1))
    spread = where01(iota((HEADS, narrow), 0) == iota((HEADS, narrow), 1) // GROUP)
    same = iota((cols, narrow), 0) % GROUP == iota((cols, narrow), 1) % GROUP
    for part, w in enumerate((high, low)):
        full = dot(dot(pick, w, NT).astype(BF16), spread)
        out_map[:, part * narrow : (part + 1) * narrow] = jnp.where(same, full, 0.0).astype(BF16)


def tile_kernel(
    count_ref,
    gain_ref,
    dest_ref,
    src_ref,
    wq_ref,
    wk_ref,
    wv_ref,
    wb_ref,
    wg_ref,
    wo_ref,
    edge_ref,
    numer_ref,
    denom_ref,
    out_ref,
    q_s,
    k_s,
    v_s,
    mix_map,
    out_map,
    raw_s,
    weight_s,
    expo_s,
    mixed_s,
):
    slot = pl.program_id(0)
    width = q_s.shape[-1]
    head_dim = width // HEADS
    tiles = width // 128

    @pl.when(slot == 0)
    def _():
        build_maps(wb_ref, wg_ref, wo_ref, mix_map, out_map)
        for w_ref, x_ref, y_s in ((wq_ref, dest_ref, q_s), (wk_ref, src_ref, k_s), (wv_ref, src_ref, v_s)):
            x = x_ref[...].reshape(-1, width)
            for n in range(0, width, 256):
                y = dot(x, w_ref[:, n : n + 256]).astype(BF16)
                y_s[:, :, n : n + 256] = y.reshape(-1, BLOCK, 256)

    @pl.when(slot >= count_ref[0])
    def _():
        numer_ref[...] = jnp.zeros_like(numer_ref)
        denom_ref[...] = jnp.zeros_like(denom_ref)
        out_ref[...] = jnp.zeros_like(out_ref)

    @pl.when(slot < count_ref[0])
    def _():
        for h in range(HEADS):
            lo, hi = h * head_dim, (h + 1) * head_dim
            a, b = lo // 128 * 128, -(-hi // 128) * 128
            lane = iota((BLOCK, b - a), 1) + a
            q = q_s[slot, :, a:b]
            q = jnp.where((lane >= lo) & (lane < hi), q, jnp.zeros_like(q))
            raw = dot(q, k_s[slot, :, a:b], NT)
            raw_s[h] = jnp.clip(raw * (1.0 / head_dim**0.5), -5.0, 5.0)

        def pair(g, _):
            def rows(side):
                return pl.ds(pl.multiple_of(g * (2 * GROUP) + side * GROUP, GROUP), GROUP)

            def both(f):
                return jnp.concatenate([f(0), f(1)], axis=1)

            edge2 = both(lambda side: edge_ref[0, :, rows(side), :].reshape(CH * GROUP, BLOCK))
            mix = dot(mix_map[...], edge2)
            bias, gate = mix[: HEADS * GROUP], mix[HEADS * GROUP :]
            score = both(lambda side: raw_s[:, rows(side), :].reshape(HEADS * GROUP, BLOCK)) + bias
            expo = jnp.exp(score)
            weight = (expo / (1.0 + jnp.exp(-gate))).astype(BF16)
            expo = expo.astype(BF16)
            for side in range(2):
                part = slice(side * BLOCK, (side + 1) * BLOCK)
                weight_s[:, rows(side), :] = weight[:, part].reshape(HEADS, GROUP, BLOCK)
                expo_s[:, rows(side), :] = expo[:, part].reshape(HEADS, GROUP, BLOCK)
            score = score.astype(BF16)
            mixed_s[...] = dot(out_map[...], jnp.concatenate([score, score], axis=0))
            for side in range(2):
                part = slice(side * BLOCK, (side + 1) * BLOCK)
                total = jnp.zeros((GROUP, BLOCK), F32)
                for c in range(CH):
                    m = mixed_s[c * GROUP : (c + 1) * GROUP, part] + edge_ref[0, c, rows(side), :].astype(F32)
                    mixed_s[c * GROUP : (c + 1) * GROUP, part] = m
                    total += m * m
                scale = lax.rsqrt(total * (1.0 / CH) + 1e-5)
                for c in range(CH):
                    m = mixed_s[c * GROUP : (c + 1) * GROUP, part]
                    out_ref[0, c, rows(side), :] = (m * (scale * gain_ref[c])).astype(BF16)
            return 0

        lax.fori_loop(0, BLOCK // (2 * GROUP), pair, 0)

        for m in range(tiles):
            heads = range(m * 128 // head_dim, (m * 128 + 127) // head_dim + 1)
            v = v_s[slot, :, m * 128 : (m + 1) * 128]
            lane = iota((BLOCK, 128), 1) + m * 128
            weights = jnp.concatenate([weight_s[h] for h in heads], axis=1)
            values = jnp.concatenate(
                [jnp.where(lane // head_dim == h, v, jnp.zeros_like(v)) for h in heads], axis=0
            )
            numer_ref[0, :, m * 128 : (m + 1) * 128] = dot(weights, values).astype(BF16)
        ones = where01(iota((HEADS, HEADS * BLOCK), 0) == iota((HEADS, HEADS * BLOCK), 1) // BLOCK)
        expo_all = jnp.concatenate([expo_s[h] for h in range(HEADS)], axis=1)
        denom_ref[0] = dot(ones, expo_all, NT)


def tile_call(count, gain_edge, dest, src, w_query, w_key, w_value, w_bias, w_gate, w_out, edges):
    slots, _, width = dest.shape
    vm = pl.BlockSpec(memory_space=pltpu.VMEM)
    sm = pl.BlockSpec(memory_space=pltpu.SMEM)
    edge_spec = pl.BlockSpec((1, CH, BLOCK, BLOCK), lambda s: (s, 0, 0, 0))
    return pl.pallas_call(
        tile_kernel,
        grid=(slots,),
        in_specs=[sm, sm] + [vm] * 8 + [edge_spec],
        out_specs=[
            pl.BlockSpec((1, BLOCK, width), lambda s: (s, 0, 0)),
            pl.BlockSpec((1, HEADS, BLOCK), lambda s: (s, 0, 0)),
            edge_spec,
        ],
        out_shape=[
            jax.ShapeDtypeStruct((slots, BLOCK, width), BF16),
            jax.ShapeDtypeStruct((slots, HEADS, BLOCK), F32),
            jax.ShapeDtypeStruct(edges.shape, BF16),
        ],
        scratch_shapes=[
            pltpu.VMEM((slots, BLOCK, width), BF16),
            pltpu.VMEM((slots, BLOCK, width), BF16),
            pltpu.VMEM((slots, BLOCK, width), BF16),
            pltpu.VMEM((2 * HEADS * GROUP, CH * GROUP), BF16),
            pltpu.VMEM((CH * GROUP, 2 * HEADS * GROUP), BF16),
            pltpu.VMEM((HEADS, BLOCK, BLOCK), F32),
            pltpu.VMEM((HEADS, BLOCK, BLOCK), BF16),
            pltpu.VMEM((HEADS, BLOCK, BLOCK), BF16),
            pltpu.VMEM((CH * GROUP, 2 * BLOCK), F32),
        ],
        compiler_params=pltpu.CompilerParams(vmem_limit_bytes=48 * 1024 * 1024),
        name="tile_work",
    )(count, gain_edge, dest, src, w_query, w_key, w_value, w_bias, w_gate, w_out, edges)


NX, NY, NZ = 4, 4, 4
PIECES = 6
MESH = pl.DeviceIdType.MESH


def place():
    row, col = lax.axis_index("row"), lax.axis_index("col")
    x, y, z, core = row // NY, row % NY, col // 2, col % 2

    def on_x(k):
        return (lax.rem(x + k, NX) * NY + y, col)

    def on_y(k):
        return (x * NY + lax.rem(y + k, NY), col)

    def on_z(k):
        return (row, lax.rem(z + k, NZ) * 2 + core)

    return x, y, z, core, on_x, on_y, on_z, (row, z * 2 + 1 - core)


def greet(peers):
    barrier = pltpu.get_barrier_semaphore()
    for peer in peers:
        pl.semaphore_signal(barrier, inc=1, device_id=peer, device_id_type=MESH)
    pl.semaphore_wait(barrier, len(peers))


def remote(src, dst, send_sem, recv_sem, peer):
    return pltpu.make_async_remote_copy(
        src_ref=src, dst_ref=dst, send_sem=send_sem, recv_sem=recv_sem, device_id=peer, device_id_type=MESH
    )


def gather_kernel(
    tile_ref,
    nodes_ref,
    src_out,
    dest_out,
    sib_out,
    pool_y,
    pool_x,
    pool_z,
    fill_send,
    fill_recv,
    core_send,
    core_recv,
    meta_own,
    meta_vmem,
    meta,
    ring_send_sem,
    ring_recv_sem,
    fill_send_sem,
    fill_recv_sem,
    meta_send_sem,
    meta_recv_sem,
    core_sem,
    local_sem,
):
    x, y, z, core, on_x, on_y, on_z, sibling = place()
    width = nodes_ref.shape[-1]
    half = width // 2
    per_dev = PIECES // 2
    src_blocks = NX * NY * per_dev
    slots = src_out.shape[0]
    greet([on_x(1), on_x(3), on_x(2), on_y(1), on_y(3), on_y(2), on_z(1), on_z(3), sibling])

    lane = iota(meta_own.shape, 1)
    words = jnp.zeros(meta_own.shape, jnp.int32)
    for s in range(slots):
        words = jnp.where(lane == s, tile_ref[s] % src_blocks, words)
        words = jnp.where(lane == slots + s, tile_ref[s] // src_blocks, words)
    meta_own[...] = words
    meta_copies = []
    for k, (peer, there) in enumerate(
        [(on_x(3), 0), (on_x(1), 1), (on_x(2), 2), (on_y(3), 3), (on_y(1), 4), (on_y(2), 5), (sibling, 6)]
    ):
        copy = remote(meta_own, meta_vmem.at[there], meta_send_sem.at[there], meta_recv_sem.at[there], peer)
        copy.start()
        meta_copies.append(copy)

    rings = [
        (pool_y, y, on_y, 0, half),
        (pool_x, x, on_x, half, width),
        (pool_z, z, on_z, 0, width),
    ]
    low, high = pl.ds(0, PIECES // 2), pl.ds(PIECES // 2, PIECES // 2)
    ring_copies = []
    for r, (pool, pos, on, a, b) in enumerate(rings):
        copies = {}
        for step in range(2):
            for way, peer in ((0, on(1)), (1, on(3))):
                part = step if way == 0 else 1 - step
                copies[way, step] = remote(
                    nodes_ref.at[(low, high)[part], :, a:b],
                    pool.at[pl.ds(pos * PIECES + part * (PIECES // 2), PIECES // 2)],
                    ring_send_sem.at[r, way, step],
                    ring_recv_sem.at[r, way, step],
                    peer,
                )
        ring_copies.append(copies)
    for step in range(2):
        for r in range(3):
            for way in range(2):
                ring_copies[r][way, step].start()
    for pool, pos, on, a, b in rings:
        pool[pl.ds(pos * PIECES, PIECES)] = nodes_ref[:, :, a:b]

    for r, (pool, pos, on, a, b) in enumerate(rings):
        for way, peer, owner in ((0, on(1), lax.rem(pos + 3, 4)), (1, on(3), lax.rem(pos + 1, 4))):
            ring_copies[r][way, 0].wait_recv()
            here = pool.at[pl.ds(owner * PIECES + way * (PIECES // 2), PIECES // 2)]
            ring_copies[r][way, 2] = remote(
                here, here, ring_send_sem.at[r, way, 2], ring_recv_sem.at[r, way, 2], peer
            )
            ring_copies[r][way, 2].start()

    for copy in meta_copies:
        copy.wait_recv()
    to_smem = pltpu.make_async_copy(meta_vmem, meta, local_sem)
    to_smem.start()
    to_smem.wait()
    sib_out[...] = meta_vmem[6]

    def source(who, s):
        block = tile_ref[s] % src_blocks if who is None else meta[who, 0, s]
        t, o = block // per_dev, block % per_dev
        return t // NY, t % NY, o

    def along_x(who, s):
        bx, by, o = source(who, s)
        return bx, by * per_dev + o

    def along_y(who, s):
        bx, by, o = source(who, s)
        return by, bx * per_dev + o

    def load(pool, block):
        return pool[pl.ds(block * 2, 2)]

    fills = [(pool_y, x, on_x, along_x, (0, 1, 2)), (pool_x, y, on_y, along_y, (3, 4, 5))]
    fill_copies = []

    def send_fill(f, way, part, peer):
        copy = remote(
            fill_send.at[f, way, part],
            fill_recv.at[f, way, part],
            fill_send_sem.at[f, way, part],
            fill_recv_sem.at[f, way, part],
            peer,
        )
        copy.start()
        return copy

    for f, (pool, pos, on, along, (plus, minus, far)) in enumerate(fills):
        for way in range(2):
            for step in (1, 2):
                ring_copies[f][way, step].wait_recv()
        copies = {}
        for part, who_of in ((0, (far, far)), (1, (plus, minus))):
            for way, peer in ((0, on(1)), (1, on(3))):
                first = 2 * (way if part == 0 else 1 - way)
                for k in range(2):
                    fill_send[f, way, part, k] = load(pool, along(who_of[way], first + k)[1])
                copies[way, part] = send_fill(f, way, part, peer)
        fill_copies.append(copies)
    for f, (pool, pos, on, along, (plus, minus, far)) in enumerate(fills):
        copies = fill_copies[f]
        for way, peer, who in ((0, on(1), plus), (1, on(3), minus)):
            copies[way, 0].wait_recv()
            for k in range(2):
                at, block = along(who, 2 * way + k)
                fill_send[f, way, 2, k] = jnp.where(at == pos, load(pool, block), fill_recv[f, way, 0, k])
            copies[way, 2] = send_fill(f, way, 2, peer)

    for way in range(2):
        for step in (1, 2):
            ring_copies[2][way, step].wait_recv()

    def dest(who, s):
        block = tile_ref[s] // src_blocks if who is None else meta[who, 0, slots + s]
        owner, o = block // per_dev, block % per_dev
        return owner % 2, (owner // 2) * per_dev + o

    for s in range(slots):
        core_send[s] = load(pool_z, dest(6, s)[1])
    core_copy = remote(core_send, core_recv, core_sem.at[0], core_sem.at[1], sibling)
    core_copy.start()

    for f, (pool, pos, on, along, (plus, minus, far)) in enumerate(fills):
        copies = fill_copies[f]
        for way in range(2):
            for part in (1, 2):
                copies[way, part].wait_recv()
        for s in range(slots):
            at, block = along(None, s)
            own = load(pool, block)
            k = s % 2
            if s < 2:
                near, other = fill_recv[f, 1, 1, k], fill_recv[f, 0, 2, k]
                is_near = at == lax.rem(pos + 1, 4)
            else:
                near, other = fill_recv[f, 0, 1, k], fill_recv[f, 1, 2, k]
                is_near = at == lax.rem(pos + 3, 4)
            src_out[s, :, :, f * half : (f + 1) * half] = jnp.where(
                at == pos, own, jnp.where(is_near, near, other)
            )
    core_copy.wait_recv()
    for s in range(slots):
        at, block = dest(None, s)
        dest_out[s] = jnp.where(at == core, load(pool_z, block), core_recv[s])
    core_copy.wait_send()
    for copy in meta_copies:
        copy.wait_send()
    for copies in ring_copies + fill_copies:
        for copy in copies.values():
            copy.wait_send()


def gather_call(tiles, nodes):
    rows, width = nodes.shape
    slots = tiles.shape[0]
    piece = rows // PIECES
    half = width // 2
    vm = pl.BlockSpec(memory_space=pltpu.VMEM)
    sm = pl.BlockSpec(memory_space=pltpu.SMEM)
    dma = pltpu.SemaphoreType.DMA
    blocks = jax.ShapeDtypeStruct((slots, 2, piece, width), BF16)
    src, dest, sib = pl.pallas_call(
        gather_kernel,
        in_specs=[sm, vm],
        out_specs=[vm, vm, vm],
        out_shape=[blocks, blocks, jax.ShapeDtypeStruct((8, 128), jnp.int32)],
        scratch_shapes=[
            pltpu.VMEM((4 * PIECES, piece, half), BF16),
            pltpu.VMEM((4 * PIECES, piece, half), BF16),
            pltpu.VMEM((4 * PIECES, piece, width), BF16),
            pltpu.VMEM((2, 2, 3, 2, 2, piece, half), BF16),
            pltpu.VMEM((2, 2, 3, 2, 2, piece, half), BF16),
            pltpu.VMEM((slots, 2, piece, width), BF16),
            pltpu.VMEM((slots, 2, piece, width), BF16),
            pltpu.VMEM((8, 128), jnp.int32),
            pltpu.VMEM((7, 8, 128), jnp.int32),
            pltpu.SMEM((7, 8, 128), jnp.int32),
            dma((3, 2, 3)),
            dma((3, 2, 3)),
            dma((2, 2, 3)),
            dma((2, 2, 3)),
            dma((7,)),
            dma((7,)),
            dma((2,)),
            dma,
        ],
        compiler_params=pltpu.CompilerParams(
            collective_id=0, has_side_effects=True, vmem_limit_bytes=48 * 1024 * 1024
        ),
        name="gather_blocks",
    )(tiles, nodes.reshape(PIECES, piece, width))
    return src.reshape(slots, BLOCK, width), dest.reshape(slots, BLOCK, width), sib[0]


def reduce_kernel(
    tile_ref,
    sib_ref,
    numer_ref,
    denom_ref,
    nodes_ref,
    w_ref,
    gain_ref,
    out_ref,
    sib_numer,
    send,
    recv,
    den_send,
    den_recv,
    total,
    sib_sem,
    send_sem,
    recv_sem,
    den_send_sem,
    den_recv_sem,
):
    x, y, z, core, on_x, on_y, on_z, sibling = place()
    row, col = lax.axis_index("row"), lax.axis_index("col")
    n_col = 2 * NZ
    slots = denom_ref.shape[0]
    src_blocks = NX * NY * (PIECES // 2)
    per_dev = PIECES // 2
    piece, width = numer_ref.shape[1:]
    head_dim = width // HEADS
    others = [(row, lax.rem(col + k, n_col)) for k in range(1, n_col)]
    greet(others)
    sib_copy = remote(numer_ref, sib_numer, sib_sem.at[0], sib_sem.at[1], sibling)
    sib_copy.start()
    mine = [tile_ref[s] // src_blocks for s in range(slots)]
    theirs = [sib_ref[slots + s] for s in range(slots)]

    def find(ids, a):
        index, found = jnp.int32(0), jnp.int32(0)
        for s in range(slots):
            index = jnp.where(ids[s] == a, s, index)
            found = jnp.where(ids[s] == a, 1, found)
        return index, found

    def denom_of(owner, o):
        index, found = find(mine, owner * per_dev + o)
        d = denom_ref[index]
        return jnp.where(found > 0, d, jnp.zeros_like(d))

    den_copies = []
    for k in range(1, n_col):
        for o in range(per_dev):
            den_send[k, o] = denom_of(lax.rem(col + k, n_col), o)
        copy = remote(den_send.at[k], den_recv.at[k], den_send_sem.at[k], den_recv_sem.at[k], others[k - 1])
        copy.start()
        den_copies.append(copy)
    sib_copy.wait_recv()

    def chunk(at, p):
        a = (at * 2 + core) * per_dev + p // 2
        i, f = find(mine, a)
        j, g = find(theirs, a)
        u = numer_ref[i * 2 + p % 2].astype(F32)
        v = sib_numer[j * 2 + p % 2].astype(F32)
        return jnp.where(f > 0, u, jnp.zeros_like(u)) + jnp.where(g > 0, v, jnp.zeros_like(v))

    half = PIECES // 2
    copies = {}

    def start(way, part):
        copies[way, part] = remote(
            send.at[way, part],
            recv.at[way, part],
            send_sem.at[way, part],
            recv_sem.at[way, part],
            on_z(1 + 2 * way),
        )
        copies[way, part].start()

    for part in range(2):
        for way in range(2):
            at = lax.rem(z + (2 if part == 0 else 1 + 2 * way), NZ)
            first = half * (way if part == 0 else 1 - way)
            for k in range(half):
                send[way, part, k] = chunk(at, first + k).astype(BF16)
            start(way, part)
    for way in range(2):
        at = lax.rem(z + 1 + 2 * way, NZ)
        copies[way, 0].wait_recv()
        for k in range(half):
            send[way, 2, k] = (chunk(at, half * way + k) + recv[way, 0, k].astype(F32)).astype(BF16)
        start(way, 2)
    for p in range(PIECES):
        total[p] = chunk(z, p)
    for copy in den_copies:
        copy.wait_recv()
    expand = where01(iota((2 * HEADS, width), 0) % HEADS == iota((2 * HEADS, width), 1) // head_dim)
    scales = []
    for o in range(per_dev):
        d = denom_of(col, o)
        for k in range(1, n_col):
            d += den_recv[k, o]
        inverse = jnp.where(d > 0.0, 1.0 / jnp.where(d > 0.0, d, 1.0), 0.0)
        upper = inverse.astype(BF16)
        lower = (inverse - upper.astype(F32)).astype(BF16)
        both = jnp.concatenate([upper.astype(F32), lower.astype(F32)], axis=0).astype(BF16)
        scales.append(dot(both, expand, (((0,), (0,)), ((), ()))))
    for part in (1, 2):
        for way in range(2):
            copies[way, part].wait_recv()
    for o in range(per_dev):
        parts = []
        for p in (2 * o, 2 * o + 1):
            k = p % half
            if p < half:
                parts.append(total[p] + recv[0, 2, k].astype(F32) + recv[1, 1, k].astype(F32))
            else:
                parts.append(total[p] + recv[0, 1, k].astype(F32) + recv[1, 2, k].astype(F32))
        numer = jnp.concatenate(parts, axis=0)
        attended = (numer * scales[o]).astype(BF16)
        rows = slice(o * BLOCK, (o + 1) * BLOCK)
        mixed = nodes_ref[rows].astype(F32) + dot(attended, w_ref[...])
        mean = jnp.mean(mixed * mixed, axis=1, keepdims=True)
        out_ref[rows] = (mixed * lax.rsqrt(mean + 1e-05) * gain_ref[...]).astype(BF16)
    sib_copy.wait_send()
    for copy in den_copies + list(copies.values()):
        copy.wait_send()


def reduce_call(tiles, sib, numer, denom, nodes, w_out, gain_node):
    slots, _, width = numer.shape
    rows = nodes.shape[0]
    piece = rows // PIECES
    vm = pl.BlockSpec(memory_space=pltpu.VMEM)
    sm = pl.BlockSpec(memory_space=pltpu.SMEM)
    dma = pltpu.SemaphoreType.DMA
    per_dev = PIECES // 2
    return pl.pallas_call(
        reduce_kernel,
        in_specs=[sm, sm] + [vm] * 5,
        out_specs=vm,
        out_shape=jax.ShapeDtypeStruct((rows, width), BF16),
        scratch_shapes=[
            pltpu.VMEM((2 * slots, piece, width), BF16),
            pltpu.VMEM((2, 3, per_dev, piece, width), BF16),
            pltpu.VMEM((2, 3, per_dev, piece, width), BF16),
            pltpu.VMEM((2 * NZ, per_dev, HEADS, BLOCK), F32),
            pltpu.VMEM((2 * NZ, per_dev, HEADS, BLOCK), F32),
            pltpu.VMEM((PIECES, piece, width), F32),
            dma((2,)),
            dma((2, 3)),
            dma((2, 3)),
            dma((2 * NZ,)),
            dma((2 * NZ,)),
        ],
        compiler_params=pltpu.CompilerParams(
            collective_id=1, has_side_effects=True, vmem_limit_bytes=48 * 1024 * 1024
        ),
        name="reduce_nodes",
    )(tiles, sib, numer.reshape(2 * slots, piece, width), denom, nodes, w_out, gain_node.reshape(1, width))


def on_device(
    nodes,
    w_query,
    w_key,
    w_value,
    w_out,
    w_edge_gate,
    w_edge_bias,
    w_edge_out,
    gain_node,
    gain_edge,
    edges,
    tile_list,
    tile_count,
):
    tiles = tile_list.reshape(-1)
    src, dest, sib = gather_call(tiles, nodes)
    numer, denom, edges_out = tile_call(
        tile_count.reshape(1),
        gain_edge,
        dest,
        src,
        w_query,
        w_key,
        w_value,
        w_edge_bias,
        w_edge_gate,
        w_edge_out,
        edges[0, 0],
    )
    nodes_out = reduce_call(tiles, sib, numer, denom, nodes, w_out, gain_node)
    return (nodes_out, edges_out[None, None])


def solution(mesh):
    return jax.shard_map(
        on_device,
        mesh=mesh,
        in_specs=(
            P(("row", "col"), None),
            *[P()] * 9,
            P("row", "col", None, None, None, None),
            P("row", "col", None),
            P("row", "col"),
        ),
        out_specs=(P(("row", "col"), None), P("row", "col", None, None, None, None)),
        check_vma=False,
    )
```

```python
import jax
import jax.numpy as jnp
from jax import lax
from jax.experimental import pallas as pl
from jax.experimental.pallas import tpu as pltpu
from jax.sharding import PartitionSpec as P

HEADS = 8
BLOCK = 128
CH = 64
GROUP = 16
NX, NY, NZ = 4, 4, 4
PER_DEV = 3
PIECES = 2 * PER_DEV
HALF = PIECES // 2
SRC_BLOCKS = NX * NY * PER_DEV
N_COL = 2 * NZ
F32 = jnp.float32
BF16 = jnp.bfloat16
NT = (((1,), (1,)), ((), ()))
TN = (((0,), (0,)), ((), ()))
MESH = pl.DeviceIdType.MESH


def iota(shape, dim):
    return lax.broadcasted_iota(jnp.int32, shape, dim)


def dot(a, b, dims=(((1,), (0,)), ((), ()))):
    return lax.dot_general(a, b, dims, preferred_element_type=F32)


def where01(mask):
    return jnp.where(mask, 1.0, 0.0).astype(BF16)


def place():
    row, col = lax.axis_index("row"), lax.axis_index("col")
    x, y, z, core = row // NY, row % NY, col // 2, col % 2

    def on_x(k):
        return (lax.rem(x + k, NX) * NY + y, col)

    def on_y(k):
        return (x * NY + lax.rem(y + k, NY), col)

    def on_z(k):
        return (row, lax.rem(z + k, NZ) * 2 + core)

    return x, y, z, core, on_x, on_y, on_z, (row, z * 2 + 1 - core)


def remote(src, dst, send_sem, recv_sem, peer):
    return pltpu.make_async_remote_copy(
        src_ref=src, dst_ref=dst, send_sem=send_sem, recv_sem=recv_sem, device_id=peer, device_id_type=MESH
    )


def build_maps(wb_ref, wg_ref, wo_ref, mix_map, out_map):
    rows, cols = 2 * HEADS * GROUP, CH * GROUP
    pick = iota((rows, HEADS), 0) >> 4
    head = iota((rows, HEADS), 1)
    picked = dot(where01(pick == head), wb_ref[...]) + dot(where01(pick == head + HEADS), wg_ref[...])
    spread = where01(iota((CH, cols), 0) == iota((CH, cols), 1) >> 4)
    full = dot(picked.astype(BF16), spread)
    same = (iota((rows, cols), 0) & 15) == (iota((rows, cols), 1) & 15)
    mix_map[...] = jnp.where(same, full, 0.0).astype(BF16)
    narrow = HEADS * GROUP
    w_out = wo_ref[...]
    high = w_out.astype(BF16)
    low = (w_out - high.astype(F32)).astype(BF16)
    pick = where01(iota((cols, CH), 0) >> 4 == iota((cols, CH), 1))
    spread = where01(iota((HEADS, narrow), 0) == iota((HEADS, narrow), 1) >> 4)
    same = (iota((cols, narrow), 0) & 15) == (iota((cols, narrow), 1) & 15)
    for part, w in enumerate((high, low)):
        full = dot(dot(pick, w, NT).astype(BF16), spread)
        out_map[:, part * narrow : (part + 1) * narrow] = jnp.where(same, full, 0.0).astype(BF16)


def group_rows(g, side):
    return pl.ds(pl.multiple_of(g * (2 * GROUP) + side * GROUP, GROUP), GROUP)


def both(f):
    return jnp.concatenate([f(0), f(1)], axis=1)


def edge_terms(slot, edge_s, mix_map, bias_s, gate_s):
    def pair(g, _):
        edge2 = both(lambda side: edge_s[slot, :, group_rows(g, side), :].reshape(CH * GROUP, BLOCK))
        mix = dot(mix_map[...], edge2)
        bias, gate = mix[: HEADS * GROUP], mix[HEADS * GROUP :]
        gate = 1.0 / (1.0 + jnp.exp(-gate))
        for side in range(2):
            part = slice(side * BLOCK, (side + 1) * BLOCK)
            bias_s[slot, :, group_rows(g, side), :] = bias[:, part].reshape(HEADS, GROUP, BLOCK)
            gate_s[slot, :, group_rows(g, side), :] = gate[:, part].reshape(HEADS, GROUP, BLOCK)
        return 0

    lax.fori_loop(0, BLOCK // (2 * GROUP), pair, 0)


def project(x, w_s, y_s):
    width = w_s.shape[0]
    for n in range(0, width, 256):
        y_s[:, :, n : n + 256] = dot(x, w_s[:, n : n + 256]).astype(BF16).reshape(-1, BLOCK, 256)


def attend(slot, live, q_s, k_s, v_s, bias_s, gate_s, score_s, weight_s, expo_s, numer_s, denom_s):
    width = q_s.shape[-1]
    head_dim = width // HEADS
    for h in range(HEADS):
        lo, hi = h * head_dim, (h + 1) * head_dim
        a, b = lo // 128 * 128, -(-hi // 128) * 128
        lane = iota((BLOCK, b - a), 1) + a
        q = q_s[slot, :, a:b]
        q = jnp.where((lane >= lo) & (lane < hi), q, jnp.zeros_like(q))
        raw = dot(q, k_s[slot, :, a:b], NT)
        score = jnp.clip(raw * (1.0 / head_dim**0.5), -5.0, 5.0) + bias_s[slot, h]
        expo = jnp.exp(score)
        score_s[slot, h] = score.astype(BF16)
        weight_s[h] = (expo * gate_s[slot, h]).astype(BF16)
        expo_s[:, h * BLOCK : (h + 1) * BLOCK] = expo.astype(BF16)
    for m in range(width // 128):
        heads = range(m * 128 // head_dim, (m * 128 + 127) // head_dim + 1)
        v = v_s[slot, :, m * 128 : (m + 1) * 128]
        lane = iota((BLOCK, 128), 1) + m * 128
        weights = jnp.concatenate([weight_s[h] for h in heads], axis=1)
        values = jnp.concatenate(
            [
                jnp.where((lane >= h * head_dim) & (lane < (h + 1) * head_dim), v, jnp.zeros_like(v))
                for h in heads
            ],
            axis=0,
        )
        numer = dot(weights, values)
        numer = jnp.where(live, numer, jnp.zeros_like(numer)).astype(BF16)
        piece = BLOCK // 2
        numer_s[2 * slot, :, m * 128 : (m + 1) * 128] = numer[:piece]
        numer_s[2 * slot + 1, :, m * 128 : (m + 1) * 128] = numer[piece:]
    ones = where01(iota((HEADS, HEADS * BLOCK), 0) == iota((HEADS, HEADS * BLOCK), 1) >> 7)
    denom = dot(ones, expo_s[...], NT)
    denom_s[slot] = jnp.where(live, denom, jnp.zeros_like(denom))


def edge_output(slot, live, gain_ref, out_map, edge_s, score_s, mixed_s):
    factor = jnp.where(live, 1.0, 0.0)

    def pair(g, _):
        score = both(lambda side: score_s[slot, :, group_rows(g, side), :].reshape(HEADS * GROUP, BLOCK))
        mixed_s[...] = dot(out_map[...], jnp.concatenate([score, score], axis=0))
        for side in range(2):
            part = slice(side * BLOCK, (side + 1) * BLOCK)
            rows = group_rows(g, side)
            total = jnp.zeros((GROUP, BLOCK), F32)
            for c in range(CH):
                m = mixed_s[c * GROUP : (c + 1) * GROUP, part] + edge_s[slot, c, rows, :].astype(F32)
                mixed_s[c * GROUP : (c + 1) * GROUP, part] = m
                total += m * m
            scale = lax.rsqrt(total * (1.0 / CH) + 1e-5) * factor
            for c in range(CH):
                m = mixed_s[c * GROUP : (c + 1) * GROUP, part]
                edge_s[slot, c, rows, :] = (m * (scale * gain_ref[c])).astype(BF16)
        return 0

    lax.fori_loop(0, BLOCK // (2 * GROUP), pair, 0)


def layer_kernel(
    tile_ref,
    count_ref,
    gain_edge_ref,
    nodes_ref,
    wb_ref,
    wg_ref,
    wo_ref,
    gain_node_ref,
    wq_hbm,
    wk_hbm,
    wv_hbm,
    wout_hbm,
    edges_hbm,
    nodes_out,
    edges_out,
    pool_y,
    pool_x,
    pool_z,
    fill_send,
    fill_recv,
    core_send,
    core_recv,
    meta_own,
    meta_vmem,
    meta,
    ring_send_sem,
    ring_recv_sem,
    fill_send_sem,
    fill_recv_sem,
    meta_send_sem,
    meta_recv_sem,
    core_sem,
    local_sem,
    edge_s,
    w_s,
    src_s,
    dest_s,
    q_s,
    k_s,
    v_s,
    mix_map,
    out_map,
    bias_s,
    gate_s,
    score_s,
    weight_s,
    expo_s,
    mixed_s,
    numer_s,
    denom_s,
    edge_sem,
    w_sem,
    sib_numer,
    send,
    recv,
    den_send,
    den_recv,
    sib_send_sem,
    sib_recv_sem,
    send_sem,
    recv_sem,
    den_send_sem,
    den_recv_sem,
):
    x, y, z, core, on_x, on_y, on_z, sibling = place()
    row, col = lax.axis_index("row"), lax.axis_index("col")
    width = nodes_ref.shape[-1]
    head_dim = width // HEADS
    half = width // 2
    slots = edge_s.shape[0]
    piece = BLOCK // 2

    w_copies = []
    for i, w_hbm in enumerate((wq_hbm, wk_hbm, wv_hbm, wout_hbm)):
        w_copies.append(pltpu.make_async_copy(w_hbm, w_s.at[i], w_sem.at[i]))
    edge_copies = []
    for s in range(slots):
        edge_copies.append(pltpu.make_async_copy(edges_hbm.at[s], edge_s.at[s], edge_sem.at[s]))
        edge_copies[s].start()
    for copy in w_copies:
        copy.start()

    others = [(row, lax.rem(col + k, N_COL)) for k in range(1, N_COL)]
    peers = [on_x(1), on_x(3), on_x(2), on_y(1), on_y(3), on_y(2)] + others
    barrier = pltpu.get_barrier_semaphore()
    for peer in peers:
        pl.semaphore_signal(barrier, inc=1, device_id=peer, device_id_type=MESH)
    lane = iota(meta_own.shape, 1)
    words = jnp.zeros(meta_own.shape, jnp.int32)
    for s in range(slots):
        words = jnp.where(lane == s, tile_ref[s] % SRC_BLOCKS, words)
        words = jnp.where(lane == slots + s, tile_ref[s] // SRC_BLOCKS, words)
    meta_own[...] = words
    pl.semaphore_wait(barrier, len(peers))

    meta_copies = []
    for peer, there in (
        (on_x(3), 0),
        (on_x(1), 1),
        (on_x(2), 2),
        (on_y(3), 3),
        (on_y(1), 4),
        (on_y(2), 5),
        (sibling, 6),
    ):
        copy = remote(meta_own, meta_vmem.at[there], meta_send_sem.at[there], meta_recv_sem.at[there], peer)
        copy.start()
        meta_copies.append(copy)

    rings = [(pool_y, y, on_y, 0, half), (pool_x, x, on_x, half, width), (pool_z, z, on_z, 0, width)]
    low, high = pl.ds(0, HALF), pl.ds(HALF, HALF)
    ring_copies = []
    for r, (pool, pos, on, a, b) in enumerate(rings):
        copies = {}
        for step in range(2):
            for way in range(2):
                part = step if way == 0 else 1 - step
                copies[way, step] = remote(
                    nodes_ref.at[(low, high)[part], :, a:b],
                    pool.at[pl.ds(pos * PIECES + part * HALF, HALF)],
                    ring_send_sem.at[r, way, step],
                    ring_recv_sem.at[r, way, step],
                    on(1 + 2 * way),
                )
        ring_copies.append(copies)
    for step in range(2):
        for r in range(3):
            for way in range(2):
                ring_copies[r][way, step].start()
    for pool, pos, on, a, b in rings:
        pool[pl.ds(pos * PIECES, PIECES)] = nodes_ref[:, :, a:b]

    build_maps(wb_ref, wg_ref, wo_ref, mix_map, out_map)

    def forward(r):
        pool, pos, on, a, b = rings[r]
        for way in range(2):
            owner = lax.rem(pos + 3 - 2 * way, 4)
            ring_copies[r][way, 0].wait_recv()
            here = pool.at[pl.ds(owner * PIECES + way * HALF, HALF)]
            ring_copies[r][way, 2] = remote(
                here, here, ring_send_sem.at[r, way, 2], ring_recv_sem.at[r, way, 2], on(1 + 2 * way)
            )
            ring_copies[r][way, 2].start()

    def terms(s):
        edge_copies[s].wait()
        edge_terms(s, edge_s, mix_map, bias_s, gate_s)

    forward(0)
    forward(1)
    terms(0)
    forward(2)
    for copy in meta_copies:
        copy.wait_recv()
    to_smem = pltpu.make_async_copy(meta_vmem, meta, local_sem)
    to_smem.start()
    terms(1)
    to_smem.wait()

    def source(who, s):
        block = tile_ref[s] % SRC_BLOCKS if who is None else meta[who, 0, s]
        t, o = block // PER_DEV, block % PER_DEV
        return t // NY, t % NY, o

    def along_x(who, s):
        bx, by, o = source(who, s)
        return bx, by * PER_DEV + o

    def along_y(who, s):
        bx, by, o = source(who, s)
        return by, bx * PER_DEV + o

    def load(pool, block):
        return pool[pl.ds(block * 2, 2)]

    fills = [(pool_y, x, on_x, along_x, (0, 1, 2)), (pool_x, y, on_y, along_y, (3, 4, 5))]
    fill_copies = []

    def send_fill(f, way, part, peer):
        copy = remote(
            fill_send.at[f, way, part],
            fill_recv.at[f, way, part],
            fill_send_sem.at[f, way, part],
            fill_recv_sem.at[f, way, part],
            peer,
        )
        copy.start()
        return copy

    for f, (pool, pos, on, along, (plus, minus, far)) in enumerate(fills):
        for way in range(2):
            for step in (1, 2):
                ring_copies[f][way, step].wait_recv()
        copies = {}
        for part, who_of in ((0, (far, far)), (1, (plus, minus))):
            for way in range(2):
                first = 2 * (way if part == 0 else 1 - way)
                for k in range(2):
                    fill_send[f, way, part, k] = load(pool, along(who_of[way], first + k)[1])
                copies[way, part] = send_fill(f, way, part, on(1 + 2 * way))
        fill_copies.append(copies)
    terms(2)
    for f, (pool, pos, on, along, (plus, minus, far)) in enumerate(fills):
        copies = fill_copies[f]
        for way, who in ((0, plus), (1, minus)):
            copies[way, 0].wait_recv()
            for k in range(2):
                at, block = along(who, 2 * way + k)
                fill_send[f, way, 2, k] = jnp.where(at == pos, load(pool, block), fill_recv[f, way, 0, k])
            copies[way, 2] = send_fill(f, way, 2, on(1 + 2 * way))
    terms(3)
    for copy in w_copies:
        copy.wait()

    for way in range(2):
        for step in (1, 2):
            ring_copies[2][way, step].wait_recv()

    def dest(who, s):
        block = tile_ref[s] // SRC_BLOCKS if who is None else meta[who, 0, slots + s]
        owner, o = block // PER_DEV, block % PER_DEV
        return owner % 2, (owner // 2) * PER_DEV + o

    for s in range(slots):
        core_send[s] = load(pool_z, dest(6, s)[1])
    core_copy = remote(core_send, core_recv, core_sem.at[0], core_sem.at[1], sibling)
    core_copy.start()
    core_copy.wait_recv()
    for s in range(slots):
        at, block = dest(None, s)
        dest_s[s] = jnp.where(at == core, load(pool_z, block), core_recv[s])
    project(dest_s[...].reshape(-1, width), w_s.at[0], q_s)

    for f, (pool, pos, on, along, (plus, minus, far)) in enumerate(fills):
        copies = fill_copies[f]
        for way in range(2):
            for part in (1, 2):
                copies[way, part].wait_recv()
        for s in range(slots):
            at, block = along(None, s)
            own = load(pool, block)
            k = s % 2
            if s < 2:
                near, other = fill_recv[f, 1, 1, k], fill_recv[f, 0, 2, k]
                is_near = at == lax.rem(pos + 1, 4)
            else:
                near, other = fill_recv[f, 0, 1, k], fill_recv[f, 1, 2, k]
                is_near = at == lax.rem(pos + 3, 4)
            src_s[s, :, :, f * half : (f + 1) * half] = jnp.where(
                at == pos, own, jnp.where(is_near, near, other)
            )
    project(src_s[...].reshape(-1, width), w_s.at[1], k_s)
    project(src_s[...].reshape(-1, width), w_s.at[2], v_s)

    lives = [s < count_ref[0] for s in range(slots)]
    sib_copies = []
    for s in range(slots):
        attend(
            s, lives[s], q_s, k_s, v_s, bias_s, gate_s, score_s, weight_s, expo_s, numer_s, denom_s
        )
        here = pl.ds(2 * s, 2)
        copy = remote(numer_s.at[here], sib_numer.at[here], sib_send_sem.at[s], sib_recv_sem.at[s], sibling)
        copy.start()
        sib_copies.append(copy)

    mine = [tile_ref[s] // SRC_BLOCKS for s in range(slots)]
    theirs = [meta[6, 0, slots + s] for s in range(slots)]

    def find(ids, a):
        index, found = jnp.int32(0), jnp.int32(0)
        for s in range(slots):
            index = jnp.where(ids[s] == a, s, index)
            found = jnp.where(ids[s] == a, 1, found)
        return index, found

    def denom_of(owner, o):
        index, found = find(mine, owner * PER_DEV + o)
        d = denom_s[index]
        return jnp.where(found > 0, d, jnp.zeros_like(d))

    for copy in sib_copies:
        copy.wait_recv()

    def chunk(at, p):
        a = (at * 2 + core) * PER_DEV + p // 2
        i, f = find(mine, a)
        j, g = find(theirs, a)
        u = numer_s[i * 2 + p % 2].astype(F32)
        v = sib_numer[j * 2 + p % 2].astype(F32)
        return jnp.where(f > 0, u, jnp.zeros_like(u)) + jnp.where(g > 0, v, jnp.zeros_like(v))

    copies = {}

    def start(way, part):
        copies[way, part] = remote(
            send.at[way, part],
            recv.at[way, part],
            send_sem.at[way, part],
            recv_sem.at[way, part],
            on_z(1 + 2 * way),
        )
        copies[way, part].start()

    for part in range(2):
        for way in range(2):
            at = lax.rem(z + (2 if part == 0 else 1 + 2 * way), NZ)
            first = HALF * (way if part == 0 else 1 - way)
            for k in range(HALF):
                send[way, part, k] = chunk(at, first + k).astype(BF16)
            start(way, part)
    den_copies = []
    for k in range(1, N_COL):
        for o in range(PER_DEV):
            den_send[k, o] = denom_of(lax.rem(col + k, N_COL), o)
        copy = remote(den_send.at[k], den_recv.at[k], den_send_sem.at[k], den_recv_sem.at[k], others[k - 1])
        copy.start()
        den_copies.append(copy)

    out_copies = []

    def emit(s):
        edge_output(s, lives[s], gain_edge_ref, out_map, edge_s, score_s, mixed_s)
        copy = pltpu.make_async_copy(edge_s.at[s], edges_out.at[s], edge_sem.at[s])
        copy.start()
        out_copies.append(copy)

    emit(0)
    emit(1)
    emit(2)
    for way in range(2):
        at = lax.rem(z + 1 + 2 * way, NZ)
        copies[way, 0].wait_recv()
        for k in range(HALF):
            send[way, 2, k] = (chunk(at, HALF * way + k) + recv[way, 0, k].astype(F32)).astype(BF16)
        start(way, 2)
    emit(3)
    for copy in den_copies:
        copy.wait_recv()
    heads = iota((2 * HEADS, width), 0) & 7
    lanes = iota((2 * HEADS, width), 1)
    expand = where01((lanes >= heads * head_dim) & (lanes < (heads + 1) * head_dim))
    scales = []
    for o in range(PER_DEV):
        d = denom_of(col, o)
        for k in range(1, N_COL):
            d += den_recv[k, o]
        inverse = jnp.where(d > 0.0, 1.0 / jnp.where(d > 0.0, d, 1.0), 0.0)
        upper = inverse.astype(BF16).astype(F32)
        scales.append(dot(jnp.concatenate([upper, inverse - upper], axis=0).astype(BF16), expand, TN))
    for part in (1, 2):
        for way in range(2):
            copies[way, part].wait_recv()
    for o in range(PER_DEV):
        parts = []
        for p in (2 * o, 2 * o + 1):
            k = p % HALF
            left, right = (2, 1) if p < HALF else (1, 2)
            parts.append(chunk(z, p) + recv[0, left, k].astype(F32) + recv[1, right, k].astype(F32))
        numer = jnp.concatenate(parts, axis=0)
        attended = (numer * scales[o]).astype(BF16)
        base = nodes_ref[2 * o : 2 * o + 2].reshape(BLOCK, width).astype(F32)
        mixed = base + dot(attended, w_s[3])
        mean = jnp.mean(mixed * mixed, axis=1, keepdims=True)
        nodes_out[o * BLOCK : (o + 1) * BLOCK] = (
            mixed * lax.rsqrt(mean + 1e-05) * gain_node_ref[...]
        ).astype(BF16)

    for copy in out_copies:
        copy.wait()
    core_copy.wait_send()
    for copy in meta_copies + sib_copies + den_copies:
        copy.wait_send()
    for group in ring_copies + fill_copies + [copies]:
        for copy in group.values():
            copy.wait_send()


def on_device(
    nodes,
    w_query,
    w_key,
    w_value,
    w_out,
    w_edge_gate,
    w_edge_bias,
    w_edge_out,
    gain_node,
    gain_edge,
    edges,
    tile_list,
    tile_count,
):
    rows, width = nodes.shape
    slots = edges.shape[2]
    piece = rows // PIECES
    half = width // 2
    vm = pl.BlockSpec(memory_space=pltpu.VMEM)
    sm = pl.BlockSpec(memory_space=pltpu.SMEM)
    hbm = pl.BlockSpec(memory_space=pl.ANY)
    dma = pltpu.SemaphoreType.DMA
    v = pltpu.VMEM
    nodes_out, edges_out = pl.pallas_call(
        layer_kernel,
        in_specs=[sm, sm, sm] + [vm] * 5 + [hbm] * 5,
        out_specs=[vm, hbm],
        out_shape=[
            jax.ShapeDtypeStruct((rows, width), BF16),
            jax.ShapeDtypeStruct((slots, CH, BLOCK, BLOCK), BF16),
        ],
        scratch_shapes=[
            v((4 * PIECES, piece, half), BF16),
            v((4 * PIECES, piece, half), BF16),
            v((4 * PIECES, piece, width), BF16),
            v((2, 2, 3, 2, 2, piece, half), BF16),
            v((2, 2, 3, 2, 2, piece, half), BF16),
            v((slots, 2, piece, width), BF16),
            v((slots, 2, piece, width), BF16),
            v((8, 128), jnp.int32),
            v((7, 8, 128), jnp.int32),
            pltpu.SMEM((7, 8, 128), jnp.int32),
            dma((3, 2, 3)),
            dma((3, 2, 3)),
            dma((2, 2, 3)),
            dma((2, 2, 3)),
            dma((7,)),
            dma((7,)),
            dma((2,)),
            dma,
            v((slots, CH, BLOCK, BLOCK), BF16),
            v((4, width, width), BF16),
            v((slots, 2, piece, width), BF16),
            v((slots, 2, piece, width), BF16),
            v((slots, BLOCK, width), BF16),
            v((slots, BLOCK, width), BF16),
            v((slots, BLOCK, width), BF16),
            v((2 * HEADS * GROUP, CH * GROUP), BF16),
            v((CH * GROUP, 2 * HEADS * GROUP), BF16),
            v((slots, HEADS, BLOCK, BLOCK), F32),
            v((slots, HEADS, BLOCK, BLOCK), F32),
            v((slots, HEADS, BLOCK, BLOCK), BF16),
            v((HEADS, BLOCK, BLOCK), BF16),
            v((BLOCK, HEADS * BLOCK), BF16),
            v((CH * GROUP, 2 * BLOCK), F32),
            v((2 * slots, piece, width), BF16),
            v((slots, HEADS, BLOCK), F32),
            dma((slots,)),
            dma((4,)),
            v((2 * slots, piece, width), BF16),
            v((2, 3, HALF, piece, width), BF16),
            v((2, 3, HALF, piece, width), BF16),
            v((N_COL, PER_DEV, HEADS, BLOCK), F32),
            v((N_COL, PER_DEV, HEADS, BLOCK), F32),
            dma((slots,)),
            dma((slots,)),
            dma((2, 3)),
            dma((2, 3)),
            dma((N_COL,)),
            dma((N_COL,)),
        ],
        compiler_params=pltpu.CompilerParams(
            collective_id=0, has_side_effects=True, vmem_limit_bytes=60 * 1024 * 1024
        ),
        name="layer",
    )(
        tile_list.reshape(-1),
        tile_count.reshape(1),
        gain_edge,
        nodes.reshape(PIECES, piece, width),
        w_edge_bias.T,
        w_edge_gate.T,
        w_edge_out,
        gain_node.reshape(1, width),
        w_query,
        w_key,
        w_value,
        w_out,
        edges.reshape(slots, CH, BLOCK, BLOCK),
    )
    return (nodes_out, edges_out.reshape(edges.shape))


def solution(mesh):
    return jax.shard_map(
        on_device,
        mesh=mesh,
        in_specs=(
            P(("row", "col"), None),
            *[P()] * 9,
            P("row", "col", None, None, None, None),
            P("row", "col", None),
            P("row", "col"),
        ),
        out_specs=(P(("row", "col"), None), P("row", "col", None, None, None, None)),
        check_vma=False,
    )
```

```python
import jax
import jax.numpy as jnp
from jax import lax
from jax.experimental import pallas as pl
from jax.experimental.pallas import tpu as pltpu
from jax.sharding import PartitionSpec as P

HEADS = 8
BLOCK = 128
CH = 64
GROUP = 16
NX, NY, NZ = 4, 4, 4
PER_DEV = 3
PIECES = 2 * PER_DEV
HALF = PIECES // 2
SRC_BLOCKS = NX * NY * PER_DEV
N_COL = 2 * NZ
F32 = jnp.float32
BF16 = jnp.bfloat16
NT = (((1,), (1,)), ((), ()))
TN = (((0,), (0,)), ((), ()))
MESH = pl.DeviceIdType.MESH


def iota(shape, dim):
    return lax.broadcasted_iota(jnp.int32, shape, dim)


def dot(a, b, dims=(((1,), (0,)), ((), ()))):
    return lax.dot_general(a, b, dims, preferred_element_type=F32)


def where01(mask):
    return jnp.where(mask, 1.0, 0.0).astype(BF16)


def place():
    row, col = lax.axis_index("row"), lax.axis_index("col")
    x, y, z, core = row // NY, row % NY, col // 2, col % 2

    def on_x(k):
        return (lax.rem(x + k, NX) * NY + y, col)

    def on_y(k):
        return (x * NY + lax.rem(y + k, NY), col)

    def on_z(k):
        return (row, lax.rem(z + k, NZ) * 2 + core)

    return x, y, z, core, on_x, on_y, on_z, (row, z * 2 + 1 - core)


def remote(src, dst, send_sem, recv_sem, peer):
    return pltpu.make_async_remote_copy(
        src_ref=src, dst_ref=dst, send_sem=send_sem, recv_sem=recv_sem, device_id=peer, device_id_type=MESH
    )


def build_maps(wb_ref, wg_ref, wo_ref, mix_map, out_map):
    rows, cols = 2 * HEADS * GROUP, CH * GROUP
    pick = iota((rows, HEADS), 0) >> 4
    head = iota((rows, HEADS), 1)
    picked = dot(where01(pick == head), wb_ref[...]) + dot(where01(pick == head + HEADS), wg_ref[...])
    spread = where01(iota((CH, cols), 0) == iota((CH, cols), 1) >> 4)
    full = dot(picked.astype(BF16), spread)
    same = (iota((rows, cols), 0) & 15) == (iota((rows, cols), 1) & 15)
    mix_map[...] = jnp.where(same, full, 0.0).astype(BF16)
    narrow = HEADS * GROUP
    w_out = wo_ref[...]
    high = w_out.astype(BF16)
    low = (w_out - high.astype(F32)).astype(BF16)
    pick = where01(iota((cols, CH), 0) >> 4 == iota((cols, CH), 1))
    spread = where01(iota((HEADS, narrow), 0) == iota((HEADS, narrow), 1) >> 4)
    same = (iota((cols, narrow), 0) & 15) == (iota((cols, narrow), 1) & 15)
    for part, w in enumerate((high, low)):
        full = dot(dot(pick, w, NT).astype(BF16), spread)
        out_map[:, part * narrow : (part + 1) * narrow] = jnp.where(same, full, 0.0).astype(BF16)


def group_rows(g, side):
    return pl.ds(pl.multiple_of(g * (2 * GROUP) + side * GROUP, GROUP), GROUP)


def both(f):
    return jnp.concatenate([f(0), f(1)], axis=1)


def edge_terms(slot, edge_s, mix_map, bias_s, gate_s):
    def pair(g, _):
        edge2 = both(lambda side: edge_s[slot, :, group_rows(g, side), :].reshape(CH * GROUP, BLOCK))
        mix = dot(mix_map[...], edge2)
        bias, gate = mix[: HEADS * GROUP], mix[HEADS * GROUP :]
        gate = 1.0 / (1.0 + jnp.exp(-gate))
        for side in range(2):
            part = slice(side * BLOCK, (side + 1) * BLOCK)
            bias_s[slot, :, group_rows(g, side), :] = bias[:, part].reshape(HEADS, GROUP, BLOCK)
            gate_s[slot, :, group_rows(g, side), :] = gate[:, part].reshape(HEADS, GROUP, BLOCK)
        return 0

    lax.fori_loop(0, BLOCK // (2 * GROUP), pair, 0)


def project(x, w_s, y_s):
    width = w_s.shape[0]
    for n in range(0, width, 256):
        y_s[:, :, n : n + 256] = dot(x, w_s[:, n : n + 256]).astype(BF16).reshape(-1, BLOCK, 256)


def attend(slot, live, q_s, k_s, v_s, bias_s, gate_s, score_s, weight_s, expo_s, numer_s, denom_s):
    width = q_s.shape[-1]
    head_dim = width // HEADS
    for h in range(HEADS):
        lo, hi = h * head_dim, (h + 1) * head_dim
        a, b = lo // 128 * 128, -(-hi // 128) * 128
        lane = iota((BLOCK, b - a), 1) + a
        q = q_s[slot, :, a:b]
        q = jnp.where((lane >= lo) & (lane < hi), q, jnp.zeros_like(q))
        raw = dot(q, k_s[slot, :, a:b], NT)
        score = jnp.clip(raw * (1.0 / head_dim**0.5), -5.0, 5.0) + bias_s[slot, h]
        expo = jnp.exp(score)
        score_s[slot, h] = score.astype(BF16)
        weight_s[h] = (expo * gate_s[slot, h]).astype(BF16)
        expo_s[:, h * BLOCK : (h + 1) * BLOCK] = expo.astype(BF16)
    for m in range(width // 128):
        heads = range(m * 128 // head_dim, (m * 128 + 127) // head_dim + 1)
        v = v_s[slot, :, m * 128 : (m + 1) * 128]
        lane = iota((BLOCK, 128), 1) + m * 128
        weights = jnp.concatenate([weight_s[h] for h in heads], axis=1)
        values = jnp.concatenate(
            [
                jnp.where((lane >= h * head_dim) & (lane < (h + 1) * head_dim), v, jnp.zeros_like(v))
                for h in heads
            ],
            axis=0,
        )
        numer = dot(weights, values)
        numer = jnp.where(live, numer, jnp.zeros_like(numer)).astype(BF16)
        piece = BLOCK // 2
        numer_s[2 * slot, :, m * 128 : (m + 1) * 128] = numer[:piece]
        numer_s[2 * slot + 1, :, m * 128 : (m + 1) * 128] = numer[piece:]
    ones = where01(iota((HEADS, HEADS * BLOCK), 0) == iota((HEADS, HEADS * BLOCK), 1) >> 7)
    denom = dot(ones, expo_s[...], NT)
    denom_s[slot] = jnp.where(live, denom, jnp.zeros_like(denom))


def edge_output(slot, live, gain_ref, out_map, edge_s, score_s, mixed_s):
    factor = jnp.where(live, 1.0, 0.0)

    def pair(g, _):
        score = both(lambda side: score_s[slot, :, group_rows(g, side), :].reshape(HEADS * GROUP, BLOCK))
        mixed_s[...] = dot(out_map[...], jnp.concatenate([score, score], axis=0))
        for side in range(2):
            part = slice(side * BLOCK, (side + 1) * BLOCK)
            rows = group_rows(g, side)
            total = jnp.zeros((GROUP, BLOCK), F32)
            for c in range(CH):
                m = mixed_s[c * GROUP : (c + 1) * GROUP, part] + edge_s[slot, c, rows, :].astype(F32)
                mixed_s[c * GROUP : (c + 1) * GROUP, part] = m
                total += m * m
            scale = lax.rsqrt(total * (1.0 / CH) + 1e-5) * factor
            for c in range(CH):
                m = mixed_s[c * GROUP : (c + 1) * GROUP, part]
                edge_s[slot, c, rows, :] = (m * (scale * gain_ref[c])).astype(BF16)
        return 0

    lax.fori_loop(0, BLOCK // (2 * GROUP), pair, 0)


def layer_kernel(
    tile_ref,
    count_ref,
    gain_edge_ref,
    nodes_ref,
    wb_ref,
    wg_ref,
    wo_ref,
    gain_node_ref,
    wq_hbm,
    wk_hbm,
    wv_hbm,
    wout_hbm,
    edges_hbm,
    nodes_out,
    edge_s,
    pool_y,
    pool_x,
    pool_z,
    fill_send,
    fill_recv,
    core_send,
    core_recv,
    meta_own,
    meta_vmem,
    meta,
    ring_send_sem,
    ring_recv_sem,
    fill_send_sem,
    fill_recv_sem,
    meta_send_sem,
    meta_recv_sem,
    core_sem,
    local_sem,
    w_s,
    src_s,
    dest_s,
    q_s,
    k_s,
    v_s,
    mix_map,
    out_map,
    bias_s,
    gate_s,
    score_s,
    weight_s,
    expo_s,
    mixed_s,
    numer_s,
    denom_s,
    edge_sem,
    w_sem,
    sib_numer,
    send,
    recv,
    den_send,
    den_recv,
    sib_send_sem,
    sib_recv_sem,
    send_sem,
    recv_sem,
    den_send_sem,
    den_recv_sem,
):
    x, y, z, core, on_x, on_y, on_z, sibling = place()
    row, col = lax.axis_index("row"), lax.axis_index("col")
    width = nodes_ref.shape[-1]
    head_dim = width // HEADS
    half = width // 2
    slots = edge_s.shape[0]
    piece = BLOCK // 2

    w_copies = []
    for i, w_hbm in enumerate((wq_hbm, wk_hbm, wv_hbm, wout_hbm)):
        w_copies.append(pltpu.make_async_copy(w_hbm, w_s.at[i], w_sem.at[i]))
    edge_copies = []
    for s in range(slots):
        edge_copies.append(pltpu.make_async_copy(edges_hbm.at[s], edge_s.at[s], edge_sem.at[s]))
        edge_copies[s].start()
    for copy in w_copies:
        copy.start()

    others = [(row, lax.rem(col + k, N_COL)) for k in range(1, N_COL)]
    peers = [on_x(1), on_x(3), on_x(2), on_y(1), on_y(3), on_y(2)] + others
    barrier = pltpu.get_barrier_semaphore()
    for peer in peers:
        pl.semaphore_signal(barrier, inc=1, device_id=peer, device_id_type=MESH)
    lane = iota(meta_own.shape, 1)
    words = jnp.zeros(meta_own.shape, jnp.int32)
    for s in range(slots):
        words = jnp.where(lane == s, tile_ref[s] % SRC_BLOCKS, words)
        words = jnp.where(lane == slots + s, tile_ref[s] // SRC_BLOCKS, words)
    meta_own[...] = words
    pl.semaphore_wait(barrier, len(peers))

    meta_copies = []
    for peer, there in (
        (on_x(3), 0),
        (on_x(1), 1),
        (on_x(2), 2),
        (on_y(3), 3),
        (on_y(1), 4),
        (on_y(2), 5),
        (sibling, 6),
    ):
        copy = remote(meta_own, meta_vmem.at[there], meta_send_sem.at[there], meta_recv_sem.at[there], peer)
        copy.start()
        meta_copies.append(copy)

    rings = [(pool_y, y, on_y, 0, half), (pool_x, x, on_x, half, width), (pool_z, z, on_z, 0, width)]
    low, high = pl.ds(0, HALF), pl.ds(HALF, HALF)
    ring_copies = []
    for r, (pool, pos, on, a, b) in enumerate(rings):
        copies = {}
        for step in range(2):
            for way in range(2):
                part = step if way == 0 else 1 - step
                copies[way, step] = remote(
                    nodes_ref.at[(low, high)[part], :, a:b],
                    pool.at[pl.ds(pos * PIECES + part * HALF, HALF)],
                    ring_send_sem.at[r, way, step],
                    ring_recv_sem.at[r, way, step],
                    on(1 + 2 * way),
                )
        ring_copies.append(copies)
    for step in range(2):
        for r in range(3):
            for way in range(2):
                ring_copies[r][way, step].start()
    for pool, pos, on, a, b in rings:
        pool[pl.ds(pos * PIECES, PIECES)] = nodes_ref[:, :, a:b]

    build_maps(wb_ref, wg_ref, wo_ref, mix_map, out_map)

    def forward(r):
        pool, pos, on, a, b = rings[r]
        for way in range(2):
            owner = lax.rem(pos + 3 - 2 * way, 4)
            ring_copies[r][way, 0].wait_recv()
            here = pool.at[pl.ds(owner * PIECES + way * HALF, HALF)]
            ring_copies[r][way, 2] = remote(
                here, here, ring_send_sem.at[r, way, 2], ring_recv_sem.at[r, way, 2], on(1 + 2 * way)
            )
            ring_copies[r][way, 2].start()

    def terms(s):
        edge_copies[s].wait()
        edge_terms(s, edge_s, mix_map, bias_s, gate_s)

    forward(0)
    forward(1)
    terms(0)
    forward(2)
    for copy in meta_copies:
        copy.wait_recv()
    to_smem = pltpu.make_async_copy(meta_vmem, meta, local_sem)
    to_smem.start()
    terms(1)
    to_smem.wait()

    def source(who, s):
        block = tile_ref[s] % SRC_BLOCKS if who is None else meta[who, 0, s]
        t, o = block // PER_DEV, block % PER_DEV
        return t // NY, t % NY, o

    def along_x(who, s):
        bx, by, o = source(who, s)
        return bx, by * PER_DEV + o

    def along_y(who, s):
        bx, by, o = source(who, s)
        return by, bx * PER_DEV + o

    def load(pool, block):
        return pool[pl.ds(block * 2, 2)]

    fills = [(pool_y, x, on_x, along_x, (0, 1, 2)), (pool_x, y, on_y, along_y, (3, 4, 5))]
    fill_copies = []

    def send_fill(f, way, part, peer):
        copy = remote(
            fill_send.at[f, way, part],
            fill_recv.at[f, way, part],
            fill_send_sem.at[f, way, part],
            fill_recv_sem.at[f, way, part],
            peer,
        )
        copy.start()
        return copy

    for f, (pool, pos, on, along, (plus, minus, far)) in enumerate(fills):
        for way in range(2):
            for step in (1, 2):
                ring_copies[f][way, step].wait_recv()
        copies = {}
        for part, who_of in ((0, (far, far)), (1, (plus, minus))):
            for way in range(2):
                first = 2 * (way if part == 0 else 1 - way)
                for k in range(2):
                    fill_send[f, way, part, k] = load(pool, along(who_of[way], first + k)[1])
                copies[way, part] = send_fill(f, way, part, on(1 + 2 * way))
        fill_copies.append(copies)
    terms(2)
    for f, (pool, pos, on, along, (plus, minus, far)) in enumerate(fills):
        copies = fill_copies[f]
        for way, who in ((0, plus), (1, minus)):
            copies[way, 0].wait_recv()
            for k in range(2):
                at, block = along(who, 2 * way + k)
                fill_send[f, way, 2, k] = jnp.where(at == pos, load(pool, block), fill_recv[f, way, 0, k])
            copies[way, 2] = send_fill(f, way, 2, on(1 + 2 * way))
    terms(3)
    for copy in w_copies:
        copy.wait()

    for way in range(2):
        for step in (1, 2):
            ring_copies[2][way, step].wait_recv()

    def dest(who, s):
        block = tile_ref[s] // SRC_BLOCKS if who is None else meta[who, 0, slots + s]
        owner, o = block // PER_DEV, block % PER_DEV
        return owner % 2, (owner // 2) * PER_DEV + o

    for s in range(slots):
        core_send[s] = load(pool_z, dest(6, s)[1])
    core_copy = remote(core_send, core_recv, core_sem.at[0], core_sem.at[1], sibling)
    core_copy.start()
    core_copy.wait_recv()
    for s in range(slots):
        at, block = dest(None, s)
        dest_s[s] = jnp.where(at == core, load(pool_z, block), core_recv[s])
    project(dest_s[...].reshape(-1, width), w_s.at[0], q_s)

    for f, (pool, pos, on, along, (plus, minus, far)) in enumerate(fills):
        copies = fill_copies[f]
        for way in range(2):
            for part in (1, 2):
                copies[way, part].wait_recv()
        for s in range(slots):
            at, block = along(None, s)
            own = load(pool, block)
            k = s % 2
            if s < 2:
                near, other = fill_recv[f, 1, 1, k], fill_recv[f, 0, 2, k]
                is_near = at == lax.rem(pos + 1, 4)
            else:
                near, other = fill_recv[f, 0, 1, k], fill_recv[f, 1, 2, k]
                is_near = at == lax.rem(pos + 3, 4)
            src_s[s, :, :, f * half : (f + 1) * half] = jnp.where(
                at == pos, own, jnp.where(is_near, near, other)
            )
    project(src_s[...].reshape(-1, width), w_s.at[1], k_s)
    project(src_s[...].reshape(-1, width), w_s.at[2], v_s)

    lives = [s < count_ref[0] for s in range(slots)]
    sib_copies = []
    for s in range(slots):
        attend(
            s, lives[s], q_s, k_s, v_s, bias_s, gate_s, score_s, weight_s, expo_s, numer_s, denom_s
        )
        here = pl.ds(2 * s, 2)
        copy = remote(numer_s.at[here], sib_numer.at[here], sib_send_sem.at[s], sib_recv_sem.at[s], sibling)
        copy.start()
        sib_copies.append(copy)

    mine = [tile_ref[s] // SRC_BLOCKS for s in range(slots)]
    theirs = [meta[6, 0, slots + s] for s in range(slots)]

    def find(ids, a):
        index, found = jnp.int32(0), jnp.int32(0)
        for s in range(slots):
            index = jnp.where(ids[s] == a, s, index)
            found = jnp.where(ids[s] == a, 1, found)
        return index, found

    def denom_of(owner, o):
        index, found = find(mine, owner * PER_DEV + o)
        d = denom_s[index]
        return jnp.where(found > 0, d, jnp.zeros_like(d))

    for copy in sib_copies:
        copy.wait_recv()

    def chunk(at, p):
        a = (at * 2 + core) * PER_DEV + p // 2
        i, f = find(mine, a)
        j, g = find(theirs, a)
        u = numer_s[i * 2 + p % 2].astype(F32)
        v = sib_numer[j * 2 + p % 2].astype(F32)
        return jnp.where(f > 0, u, jnp.zeros_like(u)) + jnp.where(g > 0, v, jnp.zeros_like(v))

    copies = {}

    def start(way, part):
        copies[way, part] = remote(
            send.at[way, part],
            recv.at[way, part],
            send_sem.at[way, part],
            recv_sem.at[way, part],
            on_z(1 + 2 * way),
        )
        copies[way, part].start()

    for part in range(2):
        for way in range(2):
            at = lax.rem(z + (2 if part == 0 else 1 + 2 * way), NZ)
            first = HALF * (way if part == 0 else 1 - way)
            for k in range(HALF):
                send[way, part, k] = chunk(at, first + k).astype(BF16)
            start(way, part)
    den_copies = []
    for k in range(1, N_COL):
        for o in range(PER_DEV):
            den_send[k, o] = denom_of(lax.rem(col + k, N_COL), o)
        copy = remote(den_send.at[k], den_recv.at[k], den_send_sem.at[k], den_recv_sem.at[k], others[k - 1])
        copy.start()
        den_copies.append(copy)

    def emit(s):
        edge_output(s, lives[s], gain_edge_ref, out_map, edge_s, score_s, mixed_s)

    emit(0)
    emit(1)
    emit(2)
    for way in range(2):
        at = lax.rem(z + 1 + 2 * way, NZ)
        copies[way, 0].wait_recv()
        for k in range(HALF):
            send[way, 2, k] = (chunk(at, HALF * way + k) + recv[way, 0, k].astype(F32)).astype(BF16)
        start(way, 2)
    emit(3)
    for copy in den_copies:
        copy.wait_recv()
    heads = iota((2 * HEADS, width), 0) & 7
    lanes = iota((2 * HEADS, width), 1)
    expand = where01((lanes >= heads * head_dim) & (lanes < (heads + 1) * head_dim))
    scales = []
    for o in range(PER_DEV):
        d = denom_of(col, o)
        for k in range(1, N_COL):
            d += den_recv[k, o]
        inverse = jnp.where(d > 0.0, 1.0 / jnp.where(d > 0.0, d, 1.0), 0.0)
        upper = inverse.astype(BF16).astype(F32)
        scales.append(dot(jnp.concatenate([upper, inverse - upper], axis=0).astype(BF16), expand, TN))
    for part in (1, 2):
        for way in range(2):
            copies[way, part].wait_recv()
    for o in range(PER_DEV):
        parts = []
        for p in (2 * o, 2 * o + 1):
            k = p % HALF
            left, right = (2, 1) if p < HALF else (1, 2)
            parts.append(chunk(z, p) + recv[0, left, k].astype(F32) + recv[1, right, k].astype(F32))
        numer = jnp.concatenate(parts, axis=0)
        attended = (numer * scales[o]).astype(BF16)
        base = nodes_ref[2 * o : 2 * o + 2].reshape(BLOCK, width).astype(F32)
        mixed = base + dot(attended, w_s[3])
        mean = jnp.mean(mixed * mixed, axis=1, keepdims=True)
        nodes_out[o * BLOCK : (o + 1) * BLOCK] = (
            mixed * lax.rsqrt(mean + 1e-05) * gain_node_ref[...][None]
        ).astype(BF16)

    core_copy.wait_send()
    for copy in meta_copies + sib_copies + den_copies:
        copy.wait_send()
    for group in ring_copies + fill_copies + [copies]:
        for copy in group.values():
            copy.wait_send()


def on_device(
    nodes,
    w_query,
    w_key,
    w_value,
    w_out,
    w_edge_gate,
    w_edge_bias,
    w_edge_out,
    gain_node,
    gain_edge,
    edges,
    tile_list,
    tile_count,
):
    rows, width = nodes.shape
    slots = edges.shape[2]
    piece = rows // PIECES
    half = width // 2
    vm = pl.BlockSpec(memory_space=pltpu.VMEM)
    sm = pl.BlockSpec(memory_space=pltpu.SMEM)
    hbm = pl.BlockSpec(memory_space=pl.ANY)
    dma = pltpu.SemaphoreType.DMA
    v = pltpu.VMEM
    nodes_out, edges_out = pl.pallas_call(
        layer_kernel,
        in_specs=[sm, sm, sm] + [vm] * 5 + [hbm] * 5,
        out_specs=[vm, vm],
        out_shape=[v((rows, width), BF16), v((slots, CH, BLOCK, BLOCK), BF16)],
        scratch_shapes=[
            v((4 * PIECES, piece, half), BF16),
            v((4 * PIECES, piece, half), BF16),
            v((4 * PIECES, piece, width), BF16),
            v((2, 2, 3, 2, 2, piece, half), BF16),
            v((2, 2, 3, 2, 2, piece, half), BF16),
            v((slots, 2, piece, width), BF16),
            v((slots, 2, piece, width), BF16),
            v((8, 128), jnp.int32),
            v((7, 8, 128), jnp.int32),
            pltpu.SMEM((7, 8, 128), jnp.int32),
            dma((3, 2, 3)),
            dma((3, 2, 3)),
            dma((2, 2, 3)),
            dma((2, 2, 3)),
            dma((7,)),
            dma((7,)),
            dma((2,)),
            dma,
            v((4, width, width), BF16),
            v((slots, 2, piece, width), BF16),
            v((slots, 2, piece, width), BF16),
            v((slots, BLOCK, width), BF16),
            v((slots, BLOCK, width), BF16),
            v((slots, BLOCK, width), BF16),
            v((2 * HEADS * GROUP, CH * GROUP), BF16),
            v((CH * GROUP, 2 * HEADS * GROUP), BF16),
            v((slots, HEADS, BLOCK, BLOCK), F32),
            v((slots, HEADS, BLOCK, BLOCK), F32),
            v((slots, HEADS, BLOCK, BLOCK), BF16),
            v((HEADS, BLOCK, BLOCK), BF16),
            v((BLOCK, HEADS * BLOCK), BF16),
            v((CH * GROUP, 2 * BLOCK), F32),
            v((2 * slots, piece, width), BF16),
            v((slots, HEADS, BLOCK), F32),
            dma((slots,)),
            dma((4,)),
            v((2 * slots, piece, width), BF16),
            v((2, 3, HALF, piece, width), BF16),
            v((2, 3, HALF, piece, width), BF16),
            v((N_COL, PER_DEV, HEADS, BLOCK), F32),
            v((N_COL, PER_DEV, HEADS, BLOCK), F32),
            dma((slots,)),
            dma((slots,)),
            dma((2, 3)),
            dma((2, 3)),
            dma((N_COL,)),
            dma((N_COL,)),
        ],
        compiler_params=pltpu.CompilerParams(
            collective_id=0, has_side_effects=True, vmem_limit_bytes=50 * 1024 * 1024
        ),
        name="layer",
    )(
        tile_list.reshape(-1),
        tile_count.reshape(1),
        gain_edge,
        nodes.reshape(PIECES, piece, width),
        w_edge_bias.T,
        w_edge_gate.T,
        w_edge_out,
        gain_node,
        w_query,
        w_key,
        w_value,
        w_out,
        edges.reshape(slots, CH, BLOCK, BLOCK),
    )

    return (nodes_out, edges_out.reshape(edges.shape))


def solution(mesh):
    return jax.shard_map(
        on_device,
        mesh=mesh,
        in_specs=(
            P(("row", "col"), None),
            *[P()] * 9,
            P("row", "col", None, None, None, None),
            P("row", "col", None),
            P("row", "col"),
        ),
        out_specs=(P(("row", "col"), None), P("row", "col", None, None, None, None)),
        check_vma=False,
    )
```

```python
import jax
import jax.numpy as jnp
from jax import lax
from jax.experimental import pallas as pl
from jax.experimental.pallas import tpu as pltpu
from jax.sharding import PartitionSpec as P

HEADS = 8
BLOCK = 128
CH = 64
GROUP = 16
NX, NY, NZ = 4, 4, 4
PER_DEV = 3
PIECES = 2 * PER_DEV
HALF = PIECES // 2
SRC_BLOCKS = NX * NY * PER_DEV
N_COL = 2 * NZ
F32 = jnp.float32
BF16 = jnp.bfloat16
NT = (((1,), (1,)), ((), ()))
TN = (((0,), (0,)), ((), ()))
MESH = pl.DeviceIdType.MESH


def iota(shape, dim):
    return lax.broadcasted_iota(jnp.int32, shape, dim)


def dot(a, b, dims=(((1,), (0,)), ((), ()))):
    return lax.dot_general(a, b, dims, preferred_element_type=F32)


def where01(mask):
    return jnp.where(mask, 1.0, 0.0).astype(BF16)


def place():
    row, col = lax.axis_index("row"), lax.axis_index("col")
    x, y, z, core = row // NY, row % NY, col // 2, col % 2

    def on_x(k):
        return (lax.rem(x + k, NX) * NY + y, col)

    def on_y(k):
        return (x * NY + lax.rem(y + k, NY), col)

    def on_z(k):
        return (row, lax.rem(z + k, NZ) * 2 + core)

    return x, y, z, core, on_x, on_y, on_z, (row, z * 2 + 1 - core)


def remote(src, dst, send_sem, recv_sem, peer):
    return pltpu.make_async_remote_copy(
        src_ref=src, dst_ref=dst, send_sem=send_sem, recv_sem=recv_sem, device_id=peer, device_id_type=MESH
    )


def build_maps(wb_ref, wg_ref, wo_ref, mix_map, out_map):
    rows, cols = 2 * HEADS * GROUP, CH * GROUP
    pick = iota((rows, HEADS), 0) >> 4
    head = iota((rows, HEADS), 1)
    picked = dot(where01(pick == head), wb_ref[...]) + dot(where01(pick == head + HEADS), wg_ref[...])
    spread = where01(iota((CH, cols), 0) == iota((CH, cols), 1) >> 4)
    full = dot(picked.astype(BF16), spread)
    same = (iota((rows, cols), 0) & 15) == (iota((rows, cols), 1) & 15)
    mix_map[...] = jnp.where(same, full, 0.0).astype(BF16)
    narrow = HEADS * GROUP
    w_out = wo_ref[...]
    high = w_out.astype(BF16)
    low = (w_out - high.astype(F32)).astype(BF16)
    pick = where01(iota((cols, CH), 0) >> 4 == iota((cols, CH), 1))
    spread = where01(iota((HEADS, narrow), 0) == iota((HEADS, narrow), 1) >> 4)
    same = (iota((cols, narrow), 0) & 15) == (iota((cols, narrow), 1) & 15)
    for part, w in enumerate((high, low)):
        full = dot(dot(pick, w, NT).astype(BF16), spread)
        out_map[:, part * narrow : (part + 1) * narrow] = jnp.where(same, full, 0.0).astype(BF16)


def group_rows(g, side):
    return pl.ds(pl.multiple_of(g * (2 * GROUP) + side * GROUP, GROUP), GROUP)


def both(f):
    return jnp.concatenate([f(0), f(1)], axis=1)


def edge_terms(slot, edge_s, mix_map, bias_s, gate_s):
    def pair(g, _):
        edge2 = both(lambda side: edge_s[slot, :, group_rows(g, side), :].reshape(CH * GROUP, BLOCK))
        mix = dot(mix_map[...], edge2)
        bias, gate = mix[: HEADS * GROUP], mix[HEADS * GROUP :]
        gate = 1.0 / (1.0 + jnp.exp(-gate))
        for side in range(2):
            part = slice(side * BLOCK, (side + 1) * BLOCK)
            bias_s[slot, :, group_rows(g, side), :] = bias[:, part].reshape(HEADS, GROUP, BLOCK)
            gate_s[slot, :, group_rows(g, side), :] = gate[:, part].reshape(HEADS, GROUP, BLOCK)
        return 0

    lax.fori_loop(0, BLOCK // (2 * GROUP), pair, 0)


def project(x_s, batch, w_s, y_s):
    width = w_s.shape[0]
    slots = slice(2 * batch, 2 * batch + 2)
    x = jnp.concatenate([x_s[side, slots].reshape(2 * BLOCK, width // 2) for side in range(2)], axis=1)
    for n in range(0, width, 256):
        y_s[slots, :, n : n + 256] = dot(x, w_s[:, n : n + 256]).astype(BF16).reshape(2, BLOCK, 256)


def attend(slot, live, q_s, k_s, v_s, bias_s, gate_s, score_s, weight_s, expo_s, numer_s, denom_s):
    width = q_s.shape[-1]
    head_dim = width // HEADS
    for h in range(HEADS):
        lo, hi = h * head_dim, (h + 1) * head_dim
        a, b = lo // 128 * 128, -(-hi // 128) * 128
        lane = iota((BLOCK, b - a), 1) + a
        q = q_s[slot, :, a:b]
        q = jnp.where((lane >= lo) & (lane < hi), q, jnp.zeros_like(q))
        raw = dot(q, k_s[slot, :, a:b], NT)
        score = jnp.clip(raw * (1.0 / head_dim**0.5), -5.0, 5.0) + bias_s[slot, h]
        expo = jnp.exp(score)
        score_s[slot, h] = score.astype(BF16)
        weight_s[h] = (expo * gate_s[slot, h]).astype(BF16)
        expo_s[:, h * BLOCK : (h + 1) * BLOCK] = expo.astype(BF16)
    for m in range(width // 128):
        heads = range(m * 128 // head_dim, (m * 128 + 127) // head_dim + 1)
        v = v_s[slot, :, m * 128 : (m + 1) * 128]
        lane = iota((BLOCK, 128), 1) + m * 128
        weights = jnp.concatenate([weight_s[h] for h in heads], axis=1)
        values = jnp.concatenate(
            [
                jnp.where((lane >= h * head_dim) & (lane < (h + 1) * head_dim), v, jnp.zeros_like(v))
                for h in heads
            ],
            axis=0,
        )
        numer = dot(weights, values)
        numer = jnp.where(live, numer, jnp.zeros_like(numer)).astype(BF16)
        side, first = divmod(m * 128, width // 2)
        numer_s[side, 2 * slot : 2 * slot + 2, :, first : first + 128] = numer.reshape(2, BLOCK // 2, 128)
    ones = where01(iota((HEADS, HEADS * BLOCK), 0) == iota((HEADS, HEADS * BLOCK), 1) >> 7)
    denom = dot(ones, expo_s[...], NT)
    denom_s[slot] = jnp.where(live, denom, jnp.zeros_like(denom))


def edge_output(slot, live, gain_ref, out_map, edge_s, score_s, mixed_s):
    factor = jnp.where(live, 1.0, 0.0)

    def pair(g, _):
        score = both(lambda side: score_s[slot, :, group_rows(g, side), :].reshape(HEADS * GROUP, BLOCK))
        mixed_s[...] = dot(out_map[...], jnp.concatenate([score, score], axis=0))
        for side in range(2):
            part = slice(side * BLOCK, (side + 1) * BLOCK)
            rows = group_rows(g, side)
            total = jnp.zeros((GROUP, BLOCK), F32)
            for c in range(CH):
                m = mixed_s[c * GROUP : (c + 1) * GROUP, part] + edge_s[slot, c, rows, :].astype(F32)
                mixed_s[c * GROUP : (c + 1) * GROUP, part] = m
                total += m * m
            scale = lax.rsqrt(total * (1.0 / CH) + 1e-5) * factor
            for c in range(CH):
                m = mixed_s[c * GROUP : (c + 1) * GROUP, part]
                edge_s[slot, c, rows, :] = (m * (scale * gain_ref[c])).astype(BF16)
        return 0

    lax.fori_loop(0, BLOCK // (2 * GROUP), pair, 0)


def layer_kernel(
    tile_ref,
    count_ref,
    gain_edge_ref,
    nodes_ref,
    wb_ref,
    wg_ref,
    wo_ref,
    gain_node_ref,
    wq_hbm,
    wk_hbm,
    wv_hbm,
    wout_hbm,
    edges_hbm,
    nodes_out,
    edge_s,
    nodes_h,
    pool_y,
    pool_x,
    pool_z,
    fill_send,
    fill_recv,
    wish_send,
    wish_recv,
    core_send,
    meta_own,
    meta_vmem,
    meta,
    ring_send_sem,
    ring_recv_sem,
    pair_send_sem,
    pair_recv_sem,
    fill_send_sem,
    fill_recv_sem,
    wish_send_sem,
    wish_recv_sem,
    meta_send_sem,
    meta_recv_sem,
    core_send_sem,
    core_recv_sem,
    local_sem,
    w_s,
    src_s,
    dest_s,
    q_s,
    k_s,
    v_s,
    mix_map,
    out_map,
    bias_s,
    gate_s,
    score_s,
    weight_s,
    expo_s,
    mixed_s,
    numer_s,
    denom_s,
    edge_sem,
    w_sem,
    sib_numer,
    pair_numer,
    sum_send,
    sum_recv,
    last_send,
    last_s,
    den_send,
    den_recv,
    sib_send_sem,
    sib_recv_sem,
    first_send_sem,
    first_recv_sem,
    sum_send_sem,
    sum_recv_sem,
    last_sem,
    den_send_sem,
    den_recv_sem,
):
    x, y, z, core, on_x, on_y, on_z, sibling = place()
    row, col = lax.axis_index("row"), lax.axis_index("col")
    width = gain_node_ref.shape[0]
    head_dim = width // HEADS
    half = width // 2
    slots = edge_s.shape[0]
    batches = slots // 2
    other = 1 - core
    flip, mirror = z + 1 - 2 * (z % 2), NZ - 1 - z
    near_z = flip * other + mirror * core
    far_z = mirror * other + flip * core
    near, far_pair = (row, near_z * 2 + core), (row, far_z * 2 + core)
    sends = []

    def push(src, dst, send_sem, recv_sem, peer):
        copy = remote(src, dst, send_sem, recv_sem, peer)
        copy.start()
        sends.append(copy)
        return copy

    w_copies = []
    for i, w_hbm in enumerate((wq_hbm, wk_hbm, wv_hbm, wout_hbm)):
        w_copies.append(pltpu.make_async_copy(w_hbm, w_s.at[i], w_sem.at[i]))
    edge_copies = []
    for s in range(slots):
        edge_copies.append(pltpu.make_async_copy(edges_hbm.at[s], edge_s.at[s], edge_sem.at[s]))
        edge_copies[s].start()
    for copy in w_copies:
        copy.start()

    others = [(row, lax.rem(col + k, N_COL)) for k in range(1, N_COL)]
    peers = [on_x(1), on_x(3), on_x(2), on_y(1), on_y(3), on_y(2)] + others
    barrier = pltpu.get_barrier_semaphore()
    for peer in peers:
        pl.semaphore_signal(barrier, inc=1, device_id=peer, device_id_type=MESH)

    lane = iota(meta_own.shape, 1)
    words = jnp.zeros(meta_own.shape, jnp.int32)
    own_words = []
    for s in range(slots):
        tile = tile_ref[s]
        to, at = tile // SRC_BLOCKS, tile % SRC_BLOCKS
        t, o = at // PER_DEV, at % PER_DEV
        bx, by = t // NY, t % NY
        owner, p = to // PER_DEV, to % PER_DEV
        fields = [bx, by * PER_DEV + o, by, bx * PER_DEV + o, owner // 2, owner % 2 * PIECES + 2 * p, to]
        own_words.append(fields)
        for f, value in enumerate(fields):
            words = jnp.where(lane == f * slots + s, value, words)
    meta_own[...] = words
    for side in range(2):
        nodes_h[side] = nodes_ref[:, :, side * half : (side + 1) * half]

    def word(who, f, s):
        return own_words[s][f] if who is None else meta[who, 0, f * slots + s]

    pl.semaphore_wait(barrier, len(peers))

    sib_shard = push(
        nodes_h.at[other], pool_z.at[pl.ds(core * PIECES, PIECES)], pair_send_sem.at[0], pair_recv_sem.at[0], sibling
    )
    for i, (peer, there) in enumerate(
        (
            (on_x(3), 0),
            (on_x(1), 1),
            (on_x(2), 2),
            (on_y(3), 3),
            (on_y(1), 4),
            (on_y(2), 5),
            (sibling, 6),
            ((row, flip * 2 + 1), 7 + core),
            ((row, mirror * 2), 7 + core),
        )
    ):
        push(meta_own, meta_vmem.at[there], meta_send_sem.at[i], meta_recv_sem.at[there], peer)

    rings = [(pool_y, y, on_y, 0), (pool_x, x, on_x, 1)]
    low, high = pl.ds(0, HALF), pl.ds(HALF, HALF)
    ring_copies = [{}, {}]
    for step in range(2):
        for r, (pool, pos, on, side) in enumerate(rings):
            for way in range(2):
                part = step if way == 0 else 1 - step
                ring_copies[r][way, step] = push(
                    nodes_h.at[side, (low, high)[part]],
                    pool.at[pl.ds(pos * PIECES + part * HALF, HALF)],
                    ring_send_sem.at[r, way, step],
                    ring_recv_sem.at[r, way, step],
                    on(1 + 2 * way),
                )
        if step == 0:
            pair_own = push(
                nodes_h.at[core],
                pool_z.at[pl.ds((2 + core) * PIECES, PIECES)],
                pair_send_sem.at[1],
                pair_recv_sem.at[1],
                near,
            )
    for pool, pos, on, side in rings:
        pool[pl.ds(pos * PIECES, PIECES)] = nodes_h[side]
    pool_z[pl.ds(core * PIECES, PIECES)] = nodes_h[core]
    sib_shard.wait_recv()
    pair_sib = push(
        pool_z.at[pl.ds(other * PIECES, PIECES)],
        pool_z.at[pl.ds((2 + other) * PIECES, PIECES)],
        pair_send_sem.at[2],
        pair_recv_sem.at[2],
        near,
    )

    build_maps(wb_ref, wg_ref, wo_ref, mix_map, out_map)

    for r, (pool, pos, on, side) in enumerate(rings):
        for way in range(2):
            owner = lax.rem(pos + 3 - 2 * way, 4)
            ring_copies[r][way, 0].wait_recv()
            here = pool.at[pl.ds(owner * PIECES + way * HALF, HALF)]
            ring_copies[r][way, 2] = push(
                here, here, ring_send_sem.at[r, way, 2], ring_recv_sem.at[r, way, 2], on(1 + 2 * way)
            )

    def terms(s):
        edge_copies[s].wait()
        edge_terms(s, edge_s, mix_map, bias_s, gate_s)

    for i in range(9):
        remote(meta_own, meta_vmem.at[i], meta_send_sem.at[i], meta_recv_sem.at[i], sibling).wait_recv()
    to_smem = pltpu.make_async_copy(meta_vmem, meta, local_sem)
    to_smem.start()
    terms(0)
    to_smem.wait()

    def load(pool, block):
        return pool[pl.ds(block * 2, 2)]

    def load_z(who, s):
        group = jnp.where(word(who, 4, s) == near_z, 2 * PIECES, 0)
        return pool_z[pl.ds(group + word(who, 5, s), 2)]

    pair_own.wait_recv()
    pair_sib.wait_recv()
    wishes = []
    for b in range(batches):
        for d in range(2):
            for k in range(2):
                wish_send[b, d, k] = load_z(7 + d, 2 * b + k)
        wishes.append(
            push(wish_send.at[b], wish_recv.at[b], wish_send_sem.at[b], wish_recv_sem.at[b], far_pair)
        )

    fills = [(pool_y, x, on_x, 0, (0, 1, 2)), (pool_x, y, on_y, 2, (3, 4, 5))]
    fill_copies = {}

    def send_fill(f, way, b, part, value):
        fill_send[f, way, b, part] = value
        fill_copies[f, way, b, part] = push(
            fill_send.at[f, way, b, part],
            fill_recv.at[f, way, b, part],
            fill_send_sem.at[f, way, b, part],
            fill_recv_sem.at[f, way, b, part],
            fills[f][2](1 + 2 * way),
        )

    def fill_start(f, b):
        pool, pos, on, at, (plus, minus, far) = fills[f]
        for part in range(2):
            for way in range(2):
                who = far if part == 0 else (plus, minus)[way]
                s = 2 * b + (way if part == 0 else 1 - way)
                send_fill(f, way, b, part, load(pool, word(who, at + 1, s)))

    def fill_end(f, b):
        pool, pos, on, at, (plus, minus, far) = fills[f]
        for way in range(2):
            who, s = (plus, minus)[way], 2 * b + way
            fill_copies[f, way, b, 0].wait_recv()
            mine = load(pool, word(who, at + 1, s))
            send_fill(
                f, way, b, 2, jnp.where(word(who, at, s) == pos, mine, fill_recv[f, way, b, 0])
            )

    def dest_batch(b):
        wishes[b].wait_recv()
        for k in range(2):
            s = 2 * b + k
            for who, d in ((6, other), (None, core)):
                at = word(who, 4, s)
                inside = jnp.where(at == z, 1, jnp.where(at == near_z, 1, 0))
                value = jnp.where(inside == 1, load_z(who, s), wish_recv[b, d, k])
                if who is None:
                    dest_s[core, s] = value
                else:
                    core_send[s] = value
        here = pl.ds(2 * b, 2)
        return push(
            core_send.at[here], dest_s.at[core, here], core_send_sem.at[b], core_recv_sem.at[b], sibling
        )

    def source_batch(b):
        for f, (pool, pos, on, at, who) in enumerate(fills):
            for way in range(2):
                for part in (1, 2):
                    fill_copies[f, way, b, part].wait_recv()
            for k in range(2):
                s = 2 * b + k
                p = word(None, at, s)
                mine = load(pool, word(None, at + 1, s))
                direct, passed = fill_recv[f, 1 - k, b, 1], fill_recv[f, k, b, 2]
                beside = p == lax.rem(pos + 1 + 2 * k, 4)
                src_s[f, s] = jnp.where(p == pos, mine, jnp.where(beside, direct, passed))

    for f in range(2):
        for way in range(2):
            for step in (1, 2):
                ring_copies[f][way, step].wait_recv()
        fill_start(f, 0)
    dest_copies = [dest_batch(0)]
    for f in range(2):
        fill_end(f, 0)
        fill_start(f, 1)
    terms(1)
    dest_copies.append(dest_batch(1))
    for copy in w_copies:
        copy.wait()
    dest_copies[0].wait_recv()
    project(dest_s, 0, w_s.at[0], q_s)

    lives = [s < count_ref[0] for s in range(slots)]
    sib_copies, first_copies = [], []

    def attend_batch(b):
        for s in (2 * b, 2 * b + 1):
            attend(
                s, lives[s], q_s, k_s, v_s, bias_s, gate_s, score_s, weight_s, expo_s, numer_s, denom_s
            )
            here = pl.ds(2 * s, 2)
            sib_copies.append(
                push(numer_s.at[other, here], sib_numer.at[here], sib_send_sem.at[s], sib_recv_sem.at[s], sibling)
            )
        here = pl.ds(4 * b, 4)
        first_copies.append(
            push(
                numer_s.at[core, here],
                pair_numer.at[core, here],
                first_send_sem.at[b, 0],
                first_recv_sem.at[b, 0],
                far_pair,
            )
        )

    def pass_sibling(b):
        for s in (2 * b, 2 * b + 1):
            sib_copies[s].wait_recv()
        here = pl.ds(4 * b, 4)
        first_copies.append(
            push(
                sib_numer.at[here],
                pair_numer.at[other, here],
                first_send_sem.at[b, 1],
                first_recv_sem.at[b, 1],
                far_pair,
            )
        )

    def emit(s):
        edge_output(s, lives[s], gain_edge_ref, out_map, edge_s, score_s, mixed_s)

    source_batch(0)
    project(src_s, 0, w_s.at[1], k_s)
    project(src_s, 0, w_s.at[2], v_s)
    for f in range(2):
        fill_end(f, 1)
    attend_batch(0)
    pass_sibling(0)
    dest_copies[1].wait_recv()
    project(dest_s, 1, w_s.at[0], q_s)
    terms(2)
    terms(3)
    source_batch(1)
    project(src_s, 1, w_s.at[1], k_s)
    project(src_s, 1, w_s.at[2], v_s)
    attend_batch(1)
    pass_sibling(1)

    mine = [word(None, 6, s) for s in range(slots)]
    ids = [mine, [word(6, 6, s) for s in range(slots)]]
    ids += [[word(7 + d, 6, s) for s in range(slots)] for d in range(2)]

    def find(of, a):
        index, found = jnp.int32(0), jnp.int32(0)
        for s in range(slots):
            index = jnp.where(of[s] == a, s, index)
            found = jnp.where(of[s] == a, 1, found)
        return index, found

    def denom_of(owner, o):
        index, found = find(mine, owner * PER_DEV + o)
        d = denom_s[index]
        return jnp.where(found > 0, d, jnp.zeros_like(d))

    den_copies = []
    for k in range(1, N_COL):
        for o in range(PER_DEV):
            den_send[k, o] = denom_of(lax.rem(col + k, N_COL), o)
        den_copies.append(
            push(den_send.at[k], den_recv.at[k], den_send_sem.at[k], den_recv_sem.at[k], others[k - 1])
        )

    emit(0)
    for copy in first_copies:
        copy.wait_recv()

    def block_sum(at_z, at_core, o):
        a = (at_z * 2 + at_core) * PER_DEV + o
        total = jnp.zeros((2, BLOCK // 2, half), F32)
        for i, of in enumerate(ids):
            index, found = find(of, a)
            here = pl.ds(2 * index, 2)
            part = (numer_s[core, here] if i == 0 else sib_numer[here] if i == 1 else pair_numer[i - 2, here])
            total += jnp.where(found > 0, part, jnp.zeros_like(part)).astype(F32)
        return total

    sum_copies = []
    for i, at_core in enumerate((other, core)):
        for o in range(PER_DEV):
            sum_send[i, 2 * o : 2 * o + 2] = block_sum(near_z, at_core, o).astype(BF16)
        sum_copies.append(
            push(sum_send.at[i], sum_recv.at[i], sum_send_sem.at[i], sum_recv_sem.at[i], near)
        )
    emit(1)
    emit(2)
    sum_copies[0].wait_recv()
    for o in range(PER_DEV):
        here = slice(2 * o, 2 * o + 2)
        last_send[here] = (block_sum(z, other, o) + sum_recv[0, here].astype(F32)).astype(BF16)
    last_copy = push(last_send, last_s.at[core], last_sem.at[0], last_sem.at[1], sibling)
    emit(3)
    for copy in den_copies:
        copy.wait_recv()
    heads = iota((2 * HEADS, width), 0) & 7
    lanes = iota((2 * HEADS, width), 1)
    expand = where01((lanes >= heads * head_dim) & (lanes < (heads + 1) * head_dim))
    scales = []
    for o in range(PER_DEV):
        d = denom_of(col, o)
        for k in range(1, N_COL):
            d += den_recv[k, o]
        inverse = jnp.where(d > 0.0, 1.0 / jnp.where(d > 0.0, d, 1.0), 0.0)
        upper = inverse.astype(BF16).astype(F32)
        scales.append(dot(jnp.concatenate([upper, inverse - upper], axis=0).astype(BF16), expand, TN))
    sum_copies[1].wait_recv()
    for o in range(PER_DEV):
        here = slice(2 * o, 2 * o + 2)
        last_s[core, here] = (block_sum(z, core, o) + sum_recv[1, here].astype(F32)).astype(BF16)
    last_copy.wait_recv()
    for o in range(PER_DEV):
        here = slice(2 * o, 2 * o + 2)
        numer = jnp.concatenate([last_s[side, here].reshape(BLOCK, half) for side in range(2)], axis=1)
        attended = (numer.astype(F32) * scales[o]).astype(BF16)
        base = nodes_ref[here].reshape(BLOCK, width).astype(F32)
        mixed = base + dot(attended, w_s[3])
        mean = jnp.mean(mixed * mixed, axis=1, keepdims=True)
        nodes_out[o * BLOCK : (o + 1) * BLOCK] = (
            mixed * lax.rsqrt(mean + 1e-05) * gain_node_ref[...][None]
        ).astype(BF16)
    for copy in sends:
        copy.wait_send()


def on_device(
    nodes,
    w_query,
    w_key,
    w_value,
    w_out,
    w_edge_gate,
    w_edge_bias,
    w_edge_out,
    gain_node,
    gain_edge,
    edges,
    tile_list,
    tile_count,
):
    rows, width = nodes.shape
    slots = edges.shape[2]
    batches = slots // 2
    piece = rows // PIECES
    half = width // 2
    vm = pl.BlockSpec(memory_space=pltpu.VMEM)
    sm = pl.BlockSpec(memory_space=pltpu.SMEM)
    hbm = pl.BlockSpec(memory_space=pl.ANY)
    dma = pltpu.SemaphoreType.DMA
    v = pltpu.VMEM
    nodes_out, edges_out = pl.pallas_call(
        layer_kernel,
        in_specs=[sm, sm, sm] + [vm] * 5 + [hbm] * 5,
        out_specs=[vm, vm],
        out_shape=[v((rows, width), BF16), v((slots, CH, BLOCK, BLOCK), BF16)],
        scratch_shapes=[
            v((2, PIECES, piece, half), BF16),
            v((NY * PIECES, piece, half), BF16),
            v((NX * PIECES, piece, half), BF16),
            v((4 * PIECES, piece, half), BF16),
            v((2, 2, batches, 3, 2, piece, half), BF16),
            v((2, 2, batches, 3, 2, piece, half), BF16),
            v((batches, 2, 2, 2, piece, half), BF16),
            v((batches, 2, 2, 2, piece, half), BF16),
            v((slots, 2, piece, half), BF16),
            v((8, 128), jnp.int32),
            v((9, 8, 128), jnp.int32),
            pltpu.SMEM((9, 8, 128), jnp.int32),
            dma((2, 2, 3)),
            dma((2, 2, 3)),
            dma((3,)),
            dma((3,)),
            dma((2, 2, batches, 3)),
            dma((2, 2, batches, 3)),
            dma((batches,)),
            dma((batches,)),
            dma((9,)),
            dma((9,)),
            dma((batches,)),
            dma((batches,)),
            dma,
            v((4, width, width), BF16),
            v((2, slots, 2, piece, half), BF16),
            v((2, slots, 2, piece, half), BF16),
            v((slots, BLOCK, width), BF16),
            v((slots, BLOCK, width), BF16),
            v((slots, BLOCK, width), BF16),
            v((2 * HEADS * GROUP, CH * GROUP), BF16),
            v((CH * GROUP, 2 * HEADS * GROUP), BF16),
            v((slots, HEADS, BLOCK, BLOCK), F32),
            v((slots, HEADS, BLOCK, BLOCK), F32),
            v((slots, HEADS, BLOCK, BLOCK), BF16),
            v((HEADS, BLOCK, BLOCK), BF16),
            v((BLOCK, HEADS * BLOCK), BF16),
            v((CH * GROUP, 2 * BLOCK), F32),
            v((2, 2 * slots, piece, half), BF16),
            v((slots, HEADS, BLOCK), F32),
            dma((slots,)),
            dma((4,)),
            v((2 * slots, piece, half), BF16),
            v((2, 2 * slots, piece, half), BF16),
            v((2, PIECES, piece, half), BF16),
            v((2, PIECES, piece, half), BF16),
            v((PIECES, piece, half), BF16),
            v((2, PIECES, piece, half), BF16),
            v((N_COL, PER_DEV, HEADS, BLOCK), F32),
            v((N_COL, PER_DEV, HEADS, BLOCK), F32),
            dma((slots,)),
            dma((slots,)),
            dma((batches, 2)),
            dma((batches, 2)),
            dma((2,)),
            dma((2,)),
            dma((2,)),
            dma((N_COL,)),
            dma((N_COL,)),
        ],
        compiler_params=pltpu.CompilerParams(
            collective_id=0, has_side_effects=True, vmem_limit_bytes=50 * 1024 * 1024
        ),
        name="layer",
    )(
        tile_list.reshape(-1),
        tile_count.reshape(1),
        gain_edge,
        nodes.reshape(PIECES, piece, width),
        w_edge_bias.T,
        w_edge_gate.T,
        w_edge_out,
        gain_node,
        w_query,
        w_key,
        w_value,
        w_out,
        edges.reshape(slots, CH, BLOCK, BLOCK),
    )

    return (nodes_out, edges_out.reshape(edges.shape))


def solution(mesh):
    return jax.shard_map(
        on_device,
        mesh=mesh,
        in_specs=(
            P(("row", "col"), None),
            *[P()] * 9,
            P("row", "col", None, None, None, None),
            P("row", "col", None),
            P("row", "col"),
        ),
        out_specs=(P(("row", "col"), None), P("row", "col", None, None, None, None)),
        check_vma=False,
    )
```

```python
import jax
import jax.numpy as jnp
from jax import lax
from jax.experimental import pallas as pl
from jax.experimental.pallas import tpu as pltpu
from jax.sharding import PartitionSpec as P

HEADS = 8
BLOCK = 128
CH = 64
GROUP = 16
NX, NY, NZ = 4, 4, 4
PER_DEV = 3
PIECES = 2 * PER_DEV
HALF = PIECES // 2
SRC_BLOCKS = NX * NY * PER_DEV
N_COL = 2 * NZ
F32 = jnp.float32
BF16 = jnp.bfloat16
NT = (((1,), (1,)), ((), ()))
TN = (((0,), (0,)), ((), ()))
MESH = pl.DeviceIdType.MESH


def iota(shape, dim):
    return lax.broadcasted_iota(jnp.int32, shape, dim)


def dot(a, b, dims=(((1,), (0,)), ((), ()))):
    return lax.dot_general(a, b, dims, preferred_element_type=F32)


def where01(mask):
    return jnp.where(mask, 1.0, 0.0).astype(BF16)


def place():
    row, col = lax.axis_index("row"), lax.axis_index("col")
    x, y, z, core = row // NY, row % NY, col // 2, col % 2

    def on_x(k):
        return (lax.rem(x + k, NX) * NY + y, col)

    def on_y(k):
        return (x * NY + lax.rem(y + k, NY), col)

    def on_z(k):
        return (row, lax.rem(z + k, NZ) * 2 + core)

    return x, y, z, core, on_x, on_y, on_z, (row, z * 2 + 1 - core)


def remote(src, dst, send_sem, recv_sem, peer):
    return pltpu.make_async_remote_copy(
        src_ref=src, dst_ref=dst, send_sem=send_sem, recv_sem=recv_sem, device_id=peer, device_id_type=MESH
    )


def build_maps(wb_ref, wg_ref, wo_ref, mix_map, out_map):
    rows, cols = 2 * HEADS * GROUP, CH * GROUP
    pick = iota((rows, HEADS), 0) >> 4
    head = iota((rows, HEADS), 1)
    picked = dot(where01(pick == head), wb_ref[...]) + dot(where01(pick == head + HEADS), wg_ref[...])
    spread = where01(iota((CH, cols), 0) == iota((CH, cols), 1) >> 4)
    full = dot(picked.astype(BF16), spread)
    same = (iota((rows, cols), 0) & 15) == (iota((rows, cols), 1) & 15)
    mix_map[...] = jnp.where(same, full, 0.0).astype(BF16)
    narrow = HEADS * GROUP
    w_out = wo_ref[...]
    high = w_out.astype(BF16)
    low = (w_out - high.astype(F32)).astype(BF16)
    pick = where01(iota((cols, CH), 0) >> 4 == iota((cols, CH), 1))
    spread = where01(iota((HEADS, narrow), 0) == iota((HEADS, narrow), 1) >> 4)
    same = (iota((cols, narrow), 0) & 15) == (iota((cols, narrow), 1) & 15)
    for part, w in enumerate((high, low)):
        full = dot(dot(pick, w, NT).astype(BF16), spread)
        out_map[:, part * narrow : (part + 1) * narrow] = jnp.where(same, full, 0.0).astype(BF16)


def group_rows(g, side):
    return pl.ds(pl.multiple_of(g * (2 * GROUP) + side * GROUP, GROUP), GROUP)


def both(f):
    return jnp.concatenate([f(0), f(1)], axis=1)


def edge_terms(slot, edge_s, mix_map, bias_s, gate_s):
    def pair(g, _):
        edge2 = both(lambda side: edge_s[slot, :, group_rows(g, side), :].reshape(CH * GROUP, BLOCK))
        mix = dot(mix_map[...], edge2)
        bias, gate = mix[: HEADS * GROUP], mix[HEADS * GROUP :]
        gate = 1.0 / (1.0 + jnp.exp(-gate))
        for side in range(2):
            part = slice(side * BLOCK, (side + 1) * BLOCK)
            bias_s[slot, :, group_rows(g, side), :] = bias[:, part].reshape(HEADS, GROUP, BLOCK)
            gate_s[slot, :, group_rows(g, side), :] = gate[:, part].reshape(HEADS, GROUP, BLOCK)
        return 0

    lax.fori_loop(0, BLOCK // (2 * GROUP), pair, 0)


def project(x_s, slot, w_s, y_s):
    width = w_s.shape[0]
    x = jnp.concatenate([x_s[side, slot].reshape(BLOCK, width // 2) for side in range(2)], axis=1)
    for n in range(0, width, 256):
        y_s[slot, :, n : n + 256] = dot(x, w_s[:, n : n + 256]).astype(BF16)


def attend(slot, live, q_s, k_s, v_s, bias_s, gate_s, score_s, weight_s, expo_s, numer_s, denom_s):
    width = q_s.shape[-1]
    head_dim = width // HEADS
    for h in range(HEADS):
        lo, hi = h * head_dim, (h + 1) * head_dim
        a, b = lo // 128 * 128, -(-hi // 128) * 128
        lane = iota((BLOCK, b - a), 1) + a
        q = q_s[slot, :, a:b]
        q = jnp.where((lane >= lo) & (lane < hi), q, jnp.zeros_like(q))
        raw = dot(q, k_s[slot, :, a:b], NT)
        score = jnp.clip(raw * (1.0 / head_dim**0.5), -5.0, 5.0) + bias_s[slot, h]
        expo = jnp.exp(score)
        score_s[slot, h] = score.astype(BF16)
        weight_s[h] = (expo * gate_s[slot, h]).astype(BF16)
        expo_s[:, h * BLOCK : (h + 1) * BLOCK] = expo.astype(BF16)
    for m in range(width // 128):
        heads = range(m * 128 // head_dim, (m * 128 + 127) // head_dim + 1)
        v = v_s[slot, :, m * 128 : (m + 1) * 128]
        lane = iota((BLOCK, 128), 1) + m * 128
        weights = jnp.concatenate([weight_s[h] for h in heads], axis=1)
        values = jnp.concatenate(
            [
                jnp.where((lane >= h * head_dim) & (lane < (h + 1) * head_dim), v, jnp.zeros_like(v))
                for h in heads
            ],
            axis=0,
        )
        numer = dot(weights, values)
        numer = jnp.where(live, numer, jnp.zeros_like(numer)).astype(BF16)
        side, first = divmod(m * 128, width // 2)
        numer_s[side, 2 * slot : 2 * slot + 2, :, first : first + 128] = numer.reshape(2, BLOCK // 2, 128)
    ones = where01(iota((HEADS, HEADS * BLOCK), 0) == iota((HEADS, HEADS * BLOCK), 1) >> 7)
    denom = dot(ones, expo_s[...], NT)
    denom_s[slot] = jnp.where(live, denom, jnp.zeros_like(denom))


def edge_output(slot, live, gain_ref, out_map, edge_s, score_s, mixed_s):
    factor = jnp.where(live, 1.0, 0.0)

    def pair(g, _):
        score = both(lambda side: score_s[slot, :, group_rows(g, side), :].reshape(HEADS * GROUP, BLOCK))
        mixed_s[...] = dot(out_map[...], jnp.concatenate([score, score], axis=0))
        for side in range(2):
            part = slice(side * BLOCK, (side + 1) * BLOCK)
            rows = group_rows(g, side)
            total = jnp.zeros((GROUP, BLOCK), F32)
            for c in range(CH):
                m = mixed_s[c * GROUP : (c + 1) * GROUP, part] + edge_s[slot, c, rows, :].astype(F32)
                mixed_s[c * GROUP : (c + 1) * GROUP, part] = m
                total += m * m
            scale = lax.rsqrt(total * (1.0 / CH) + 1e-5) * factor
            for c in range(CH):
                m = mixed_s[c * GROUP : (c + 1) * GROUP, part]
                edge_s[slot, c, rows, :] = (m * (scale * gain_ref[c])).astype(BF16)
        return 0

    lax.fori_loop(0, BLOCK // (2 * GROUP), pair, 0)


def layer_kernel(
    tile_ref,
    count_ref,
    gain_edge_ref,
    nodes_ref,
    wb_ref,
    wg_ref,
    wo_ref,
    gain_node_ref,
    wq_hbm,
    wk_hbm,
    wv_hbm,
    wout_hbm,
    edges_hbm,
    nodes_out,
    edge_s,
    nodes_h,
    pool_y,
    pool_x,
    pool_z,
    fill_send,
    fill_recv,
    pass_send,
    pass_recv,
    wish_send,
    wish_recv,
    core_send,
    meta_own,
    meta_vmem,
    meta,
    ring_send_sem,
    ring_recv_sem,
    pair_send_sem,
    pair_recv_sem,
    fill_send_sem,
    fill_recv_sem,
    pass_send_sem,
    pass_recv_sem,
    wish_send_sem,
    wish_recv_sem,
    meta_send_sem,
    meta_recv_sem,
    core_send_sem,
    core_recv_sem,
    local_sem,
    w_s,
    src_s,
    dest_s,
    q_s,
    k_s,
    v_s,
    mix_map,
    out_map,
    bias_s,
    gate_s,
    score_s,
    weight_s,
    expo_s,
    mixed_s,
    numer_s,
    denom_s,
    edge_sem,
    w_sem,
    sib_numer,
    pair_numer,
    sum_send,
    sum_recv,
    last_send,
    last_s,
    den_send,
    den_recv,
    sib_send_sem,
    sib_recv_sem,
    first_send_sem,
    first_recv_sem,
    sum_send_sem,
    sum_recv_sem,
    last_sem,
    den_send_sem,
    den_recv_sem,
):
    x, y, z, core, on_x, on_y, on_z, sibling = place()
    row, col = lax.axis_index("row"), lax.axis_index("col")
    width = gain_node_ref.shape[0]
    head_dim = width // HEADS
    half = width // 2
    slots = edge_s.shape[0]
    other = 1 - core
    flip, mirror = z + 1 - 2 * (z % 2), NZ - 1 - z
    near_z = flip * other + mirror * core
    far_z = mirror * other + flip * core
    near, far_pair = (row, near_z * 2 + core), (row, far_z * 2 + core)
    sends = []

    def push(src, dst, send_sem, recv_sem, peer):
        copy = remote(src, dst, send_sem, recv_sem, peer)
        copy.start()
        sends.append(copy)
        return copy

    w_copies = []
    for i, w_hbm in enumerate((wq_hbm, wk_hbm, wv_hbm, wout_hbm)):
        w_copies.append(pltpu.make_async_copy(w_hbm, w_s.at[i], w_sem.at[i]))
    edge_copies = []
    for s in range(slots):
        edge_copies.append(pltpu.make_async_copy(edges_hbm.at[s], edge_s.at[s], edge_sem.at[s]))
        edge_copies[s].start()
    for copy in w_copies:
        copy.start()

    others = [(row, lax.rem(col + k, N_COL)) for k in range(1, N_COL)]
    peers = [on_x(1), on_x(3), on_x(2), on_y(1), on_y(3), on_y(2)] + others
    barrier = pltpu.get_barrier_semaphore()
    for peer in peers:
        pl.semaphore_signal(barrier, inc=1, device_id=peer, device_id_type=MESH)

    lane = iota(meta_own.shape, 1)
    words = jnp.zeros(meta_own.shape, jnp.int32)
    own_words = []
    for s in range(slots):
        tile = tile_ref[s]
        to, at = tile // SRC_BLOCKS, tile % SRC_BLOCKS
        t, o = at // PER_DEV, at % PER_DEV
        bx, by = t // NY, t % NY
        owner, p = to // PER_DEV, to % PER_DEV
        fields = [bx, by * PER_DEV + o, by, bx * PER_DEV + o, owner // 2, owner % 2 * PIECES + 2 * p, to]
        own_words.append(fields)
        for f, value in enumerate(fields):
            words = jnp.where(lane == f * slots + s, value, words)
    meta_own[...] = words
    for side in range(2):
        nodes_h[side] = nodes_ref[:, :, side * half : (side + 1) * half]

    def word(who, f, s):
        return own_words[s][f] if who is None else meta[who, 0, f * slots + s]

    pl.semaphore_wait(barrier, len(peers))

    rings = [(pool_y, y, on_y, 0), (pool_x, x, on_x, 1)]
    low, high = pl.ds(0, HALF), pl.ds(HALF, HALF)
    ring_copies = [{}, {}]

    def ring_start(step):
        for r, (pool, pos, on, side) in enumerate(rings):
            for way in range(2):
                part = step if way == 0 else 1 - step
                ring_copies[r][way, step] = push(
                    nodes_h.at[side, (low, high)[part]],
                    pool.at[pl.ds(pos * PIECES + part * HALF, HALF)],
                    ring_send_sem.at[r, way, step],
                    ring_recv_sem.at[r, way, step],
                    on(1 + 2 * way),
                )

    ring_start(0)
    sib_shard = push(
        nodes_h.at[other], pool_z.at[pl.ds(core * PIECES, PIECES)], pair_send_sem.at[0], pair_recv_sem.at[0], sibling
    )
    pair_own = push(
        nodes_h.at[core],
        pool_z.at[pl.ds((2 + core) * PIECES, PIECES)],
        pair_send_sem.at[1],
        pair_recv_sem.at[1],
        near,
    )
    for i, (peer, there) in enumerate(
        (
            (on_x(3), 0),
            (on_x(1), 1),
            (on_x(2), 2),
            (on_y(3), 3),
            (on_y(1), 4),
            (on_y(2), 5),
            (sibling, 6),
            ((row, flip * 2 + 1), 7 + core),
            ((row, mirror * 2), 7 + core),
        )
    ):
        push(meta_own, meta_vmem.at[there], meta_send_sem.at[i], meta_recv_sem.at[there], peer)
    ring_start(1)
    for pool, pos, on, side in rings:
        pool[pl.ds(pos * PIECES, PIECES)] = nodes_h[side]
    pool_z[pl.ds(core * PIECES, PIECES)] = nodes_h[core]
    sib_shard.wait_recv()
    pair_sib = push(
        pool_z.at[pl.ds(other * PIECES, PIECES)],
        pool_z.at[pl.ds((2 + other) * PIECES, PIECES)],
        pair_send_sem.at[2],
        pair_recv_sem.at[2],
        near,
    )

    def terms(s):
        edge_copies[s].wait()
        edge_terms(s, edge_s, mix_map, bias_s, gate_s)

    build_maps(wb_ref, wg_ref, wo_ref, mix_map, out_map)
    terms(0)

    for r, (pool, pos, on, side) in enumerate(rings):
        for way in range(2):
            owner = lax.rem(pos + 3 - 2 * way, 4)
            ring_copies[r][way, 0].wait_recv()
            here = pool.at[pl.ds(owner * PIECES + way * HALF, HALF)]
            ring_copies[r][way, 2] = push(
                here, here, ring_send_sem.at[r, way, 2], ring_recv_sem.at[r, way, 2], on(1 + 2 * way)
            )

    for i in range(9):
        remote(meta_own, meta_vmem.at[i], meta_send_sem.at[i], meta_recv_sem.at[i], sibling).wait_recv()
    to_smem = pltpu.make_async_copy(meta_vmem, meta, local_sem)
    to_smem.start()
    terms(1)
    to_smem.wait()

    def load_z(who, s):
        group = jnp.where(word(who, 4, s) == near_z, 2 * PIECES, 0)
        return pool_z[pl.ds(group + word(who, 5, s), 2)]

    pair_own.wait_recv()
    pair_sib.wait_recv()
    wishes = []
    for s in range(slots):
        for d in range(2):
            wish_send[s, d] = load_z(7 + d, s)
        wishes.append(
            push(wish_send.at[s], wish_recv.at[s], wish_send_sem.at[s], wish_recv_sem.at[s], far_pair)
        )
    terms(2)
    terms(3)

    fills = [(pool_y, x, on_x, 0, (0, 1, 2)), (pool_x, y, on_y, 2, (3, 4, 5))]
    fill_copies, pass_copies = {}, {}

    def fill_start(j):
        for f, (pool, pos, on, at, (plus, minus, far)) in enumerate(fills):
            for way in range(2):
                who = (plus, minus)[way]
                if j > 0:
                    fill_send[f, way, j, 0] = pool[word(who, at + 1, j - 1) * 2 + 1 - way]
                if j < slots:
                    fill_send[f, way, j, 1] = pool[word(far, at + 1, j) * 2 + way]
                part = pl.ds(1, 1) if j == 0 else pl.ds(0, 1) if j == slots else pl.ds(0, 2)
                fill_copies[f, way, j] = push(
                    fill_send.at[f, way, j, part],
                    fill_recv.at[f, way, j, part],
                    fill_send_sem.at[f, way, j],
                    fill_recv_sem.at[f, way, j],
                    on(1 + 2 * way),
                )

    def fill_pass(s):
        for f, (pool, pos, on, at, (plus, minus, far)) in enumerate(fills):
            for way in range(2):
                who = (plus, minus)[way]
                fill_copies[f, way, s].wait_recv()
                mine = pool[word(who, at + 1, s) * 2 + way]
                pass_send[f, way, s] = jnp.where(word(who, at, s) == pos, mine, fill_recv[f, way, s, 1])
                pass_copies[f, way, s] = push(
                    pass_send.at[f, way, s],
                    pass_recv.at[f, way, s],
                    pass_send_sem.at[f, way, s],
                    pass_recv_sem.at[f, way, s],
                    on(1 + 2 * way),
                )
        if s + 2 <= slots:
            fill_start(s + 2)

    def dest_start(s):
        wishes[s].wait_recv()
        for who, d in ((6, other), (None, core)):
            at = word(who, 4, s)
            inside = jnp.where(at == z, 1, jnp.where(at == near_z, 1, 0))
            value = jnp.where(inside == 1, load_z(who, s), wish_recv[s, d])
            if who is None:
                dest_s[core, s] = value
            else:
                core_send[s] = value
        return push(
            core_send.at[s], dest_s.at[core, s], core_send_sem.at[s], core_recv_sem.at[s], sibling
        )

    def source(s):
        if s == slots - 1:
            for f in range(2):
                for way in range(2):
                    fill_copies[f, way, slots].wait_recv()
        for f, (pool, pos, on, at, who) in enumerate(fills):
            p = word(None, at, s)
            for way in range(2):
                pass_copies[f, way, s].wait_recv()
            for k in range(2):
                mine = pool[word(None, at + 1, s) * 2 + k]
                direct, passed = fill_recv[f, 1 - k, s + 1, 0], pass_recv[f, k, s]
                beside = p == lax.rem(pos + 1 + 2 * k, 4)
                src_s[f, s, k] = jnp.where(p == pos, mine, jnp.where(beside, direct, passed))

    lives = [s < count_ref[0] for s in range(slots)]
    sib_copies, first_copies, dest_copies = [], [], []

    def tile(s):
        dest_copies[s].wait_recv()
        project(dest_s, s, w_s.at[0], q_s)
        source(s)
        project(src_s, s, w_s.at[1], k_s)
        project(src_s, s, w_s.at[2], v_s)
        attend(s, lives[s], q_s, k_s, v_s, bias_s, gate_s, score_s, weight_s, expo_s, numer_s, denom_s)
        here = pl.ds(2 * s, 2)
        sib_copies.append(
            push(numer_s.at[other, here], sib_numer.at[here], sib_send_sem.at[s], sib_recv_sem.at[s], sibling)
        )
        first_copies.append(
            push(
                numer_s.at[core, here],
                pair_numer.at[core, here],
                first_send_sem.at[s, 0],
                first_recv_sem.at[s, 0],
                far_pair,
            )
        )

    def pass_sibling(s):
        sib_copies[s].wait_recv()
        here = pl.ds(2 * s, 2)
        first_copies.append(
            push(
                sib_numer.at[here],
                pair_numer.at[other, here],
                first_send_sem.at[s, 1],
                first_recv_sem.at[s, 1],
                far_pair,
            )
        )

    def emit(s):
        edge_output(s, lives[s], gain_edge_ref, out_map, edge_s, score_s, mixed_s)

    for f in range(2):
        for way in range(2):
            for step in (1, 2):
                ring_copies[f][way, step].wait_recv()
    fill_start(0)
    fill_start(1)
    for copy in w_copies:
        copy.wait()
    dest_copies.append(dest_start(0))
    fill_pass(0)
    dest_copies.append(dest_start(1))
    fill_pass(1)
    tile(0)
    dest_copies.append(dest_start(2))
    fill_pass(2)
    pass_sibling(0)
    tile(1)
    dest_copies.append(dest_start(3))
    fill_pass(3)
    pass_sibling(1)
    tile(2)
    pass_sibling(2)
    tile(3)
    pass_sibling(3)

    mine = [word(None, 6, s) for s in range(slots)]
    ids = [mine, [word(6, 6, s) for s in range(slots)]]
    ids += [[word(7 + d, 6, s) for s in range(slots)] for d in range(2)]

    def find(of, a):
        index, found = jnp.int32(0), jnp.int32(0)
        for s in range(slots):
            index = jnp.where(of[s] == a, s, index)
            found = jnp.where(of[s] == a, 1, found)
        return index, found

    def denom_of(owner, o):
        index, found = find(mine, owner * PER_DEV + o)
        d = denom_s[index]
        return jnp.where(found > 0, d, jnp.zeros_like(d))

    den_copies = []
    for k in range(1, N_COL):
        for o in range(PER_DEV):
            den_send[k, o] = denom_of(lax.rem(col + k, N_COL), o)
        den_copies.append(
            push(den_send.at[k], den_recv.at[k], den_send_sem.at[k], den_recv_sem.at[k], others[k - 1])
        )

    emit(0)
    for copy in first_copies:
        copy.wait_recv()

    def block_sum(at_z, at_core, o):
        a = (at_z * 2 + at_core) * PER_DEV + o
        total = jnp.zeros((2, BLOCK // 2, half), F32)
        for i, of in enumerate(ids):
            index, found = find(of, a)
            here = pl.ds(2 * index, 2)
            part = (numer_s[core, here] if i == 0 else sib_numer[here] if i == 1 else pair_numer[i - 2, here])
            total += jnp.where(found > 0, part, jnp.zeros_like(part)).astype(F32)
        return total

    sum_copies = []
    for i, at_core in enumerate((other, core)):
        for o in range(PER_DEV):
            sum_send[i, 2 * o : 2 * o + 2] = block_sum(near_z, at_core, o).astype(BF16)
        sum_copies.append(
            push(sum_send.at[i], sum_recv.at[i], sum_send_sem.at[i], sum_recv_sem.at[i], near)
        )
    emit(1)
    emit(2)
    sum_copies[0].wait_recv()
    for o in range(PER_DEV):
        here = slice(2 * o, 2 * o + 2)
        last_send[here] = (block_sum(z, other, o) + sum_recv[0, here].astype(F32)).astype(BF16)
    last_copy = push(last_send, last_s.at[core], last_sem.at[0], last_sem.at[1], sibling)
    emit(3)
    for copy in den_copies:
        copy.wait_recv()
    heads = iota((2 * HEADS, width), 0) & 7
    lanes = iota((2 * HEADS, width), 1)
    expand = where01((lanes >= heads * head_dim) & (lanes < (heads + 1) * head_dim))
    scales = []
    for o in range(PER_DEV):
        d = denom_of(col, o)
        for k in range(1, N_COL):
            d += den_recv[k, o]
        inverse = jnp.where(d > 0.0, 1.0 / jnp.where(d > 0.0, d, 1.0), 0.0)
        upper = inverse.astype(BF16).astype(F32)
        scales.append(dot(jnp.concatenate([upper, inverse - upper], axis=0).astype(BF16), expand, TN))
    sum_copies[1].wait_recv()
    for o in range(PER_DEV):
        here = slice(2 * o, 2 * o + 2)
        last_s[core, here] = (block_sum(z, core, o) + sum_recv[1, here].astype(F32)).astype(BF16)
    last_copy.wait_recv()
    for o in range(PER_DEV):
        here = slice(2 * o, 2 * o + 2)
        numer = jnp.concatenate([last_s[side, here].reshape(BLOCK, half) for side in range(2)], axis=1)
        attended = (numer.astype(F32) * scales[o]).astype(BF16)
        base = nodes_ref[here].reshape(BLOCK, width).astype(F32)
        mixed = base + dot(attended, w_s[3])
        mean = jnp.mean(mixed * mixed, axis=1, keepdims=True)
        nodes_out[o * BLOCK : (o + 1) * BLOCK] = (
            mixed * lax.rsqrt(mean + 1e-05) * gain_node_ref[...][None]
        ).astype(BF16)
    for copy in sends:
        copy.wait_send()


def on_device(
    nodes,
    w_query,
    w_key,
    w_value,
    w_out,
    w_edge_gate,
    w_edge_bias,
    w_edge_out,
    gain_node,
    gain_edge,
    edges,
    tile_list,
    tile_count,
):
    rows, width = nodes.shape
    slots = edges.shape[2]
    piece = rows // PIECES
    half = width // 2
    vm = pl.BlockSpec(memory_space=pltpu.VMEM)
    sm = pl.BlockSpec(memory_space=pltpu.SMEM)
    hbm = pl.BlockSpec(memory_space=pl.ANY)
    dma = pltpu.SemaphoreType.DMA
    v = pltpu.VMEM
    nodes_out, edges_out = pl.pallas_call(
        layer_kernel,
        in_specs=[sm, sm, sm] + [vm] * 5 + [hbm] * 5,
        out_specs=[vm, vm],
        out_shape=[v((rows, width), BF16), v((slots, CH, BLOCK, BLOCK), BF16)],
        scratch_shapes=[
            v((2, PIECES, piece, half), BF16),
            v((NY * PIECES, piece, half), BF16),
            v((NX * PIECES, piece, half), BF16),
            v((4 * PIECES, piece, half), BF16),
            v((2, 2, slots + 1, 2, piece, half), BF16),
            v((2, 2, slots + 1, 2, piece, half), BF16),
            v((2, 2, slots, piece, half), BF16),
            v((2, 2, slots, piece, half), BF16),
            v((slots, 2, 2, piece, half), BF16),
            v((slots, 2, 2, piece, half), BF16),
            v((slots, 2, piece, half), BF16),
            v((8, 128), jnp.int32),
            v((9, 8, 128), jnp.int32),
            pltpu.SMEM((9, 8, 128), jnp.int32),
            dma((2, 2, 3)),
            dma((2, 2, 3)),
            dma((3,)),
            dma((3,)),
            dma((2, 2, slots + 1)),
            dma((2, 2, slots + 1)),
            dma((2, 2, slots)),
            dma((2, 2, slots)),
            dma((slots,)),
            dma((slots,)),
            dma((9,)),
            dma((9,)),
            dma((slots,)),
            dma((slots,)),
            dma,
            v((4, width, width), BF16),
            v((2, slots, 2, piece, half), BF16),
            v((2, slots, 2, piece, half), BF16),
            v((slots, BLOCK, width), BF16),
            v((slots, BLOCK, width), BF16),
            v((slots, BLOCK, width), BF16),
            v((2 * HEADS * GROUP, CH * GROUP), BF16),
            v((CH * GROUP, 2 * HEADS * GROUP), BF16),
            v((slots, HEADS, BLOCK, BLOCK), F32),
            v((slots, HEADS, BLOCK, BLOCK), F32),
            v((slots, HEADS, BLOCK, BLOCK), BF16),
            v((HEADS, BLOCK, BLOCK), BF16),
            v((BLOCK, HEADS * BLOCK), BF16),
            v((CH * GROUP, 2 * BLOCK), F32),
            v((2, 2 * slots, piece, half), BF16),
            v((slots, HEADS, BLOCK), F32),
            dma((slots,)),
            dma((4,)),
            v((2 * slots, piece, half), BF16),
            v((2, 2 * slots, piece, half), BF16),
            v((2, PIECES, piece, half), BF16),
            v((2, PIECES, piece, half), BF16),
            v((PIECES, piece, half), BF16),
            v((2, PIECES, piece, half), BF16),
            v((N_COL, PER_DEV, HEADS, BLOCK), F32),
            v((N_COL, PER_DEV, HEADS, BLOCK), F32),
            dma((slots,)),
            dma((slots,)),
            dma((slots, 2)),
            dma((slots, 2)),
            dma((2,)),
            dma((2,)),
            dma((2,)),
            dma((N_COL,)),
            dma((N_COL,)),
        ],
        compiler_params=pltpu.CompilerParams(
            collective_id=0, has_side_effects=True, vmem_limit_bytes=50 * 1024 * 1024
        ),
        name="layer",
    )(
        tile_list.reshape(-1),
        tile_count.reshape(1),
        gain_edge,
        nodes.reshape(PIECES, piece, width),
        w_edge_bias.T,
        w_edge_gate.T,
        w_edge_out,
        gain_node,
        w_query,
        w_key,
        w_value,
        w_out,
        edges.reshape(slots, CH, BLOCK, BLOCK),
    )

    return (nodes_out, edges_out.reshape(edges.shape))


def solution(mesh):
    return jax.shard_map(
        on_device,
        mesh=mesh,
        in_specs=(
            P(("row", "col"), None),
            *[P()] * 9,
            P("row", "col", None, None, None, None),
            P("row", "col", None),
            P("row", "col"),
        ),
        out_specs=(P(("row", "col"), None), P("row", "col", None, None, None, None)),
        check_vma=False,
    )
```

```python
import jax
import jax.numpy as jnp
from jax import lax
from jax.experimental import pallas as pl
from jax.experimental.pallas import tpu as pltpu
from jax.sharding import PartitionSpec as P

HEADS = 8
BLOCK = 128
CH = 64
GROUP = 16
NX, NY, NZ = 4, 4, 4
PER_DEV = 3
PIECES = 2 * PER_DEV
HALF = PIECES // 2
SRC_BLOCKS = NX * NY * PER_DEV
N_COL = 2 * NZ
F32 = jnp.float32
BF16 = jnp.bfloat16
NT = (((1,), (1,)), ((), ()))
TN = (((0,), (0,)), ((), ()))
MESH = pl.DeviceIdType.MESH


def iota(shape, dim):
    return lax.broadcasted_iota(jnp.int32, shape, dim)


def dot(a, b, dims=(((1,), (0,)), ((), ()))):
    return lax.dot_general(a, b, dims, preferred_element_type=F32)


def where01(mask):
    return jnp.where(mask, 1.0, 0.0).astype(BF16)


def place():
    row, col = lax.axis_index("row"), lax.axis_index("col")
    x, y, z, core = row // NY, row % NY, col // 2, col % 2

    def on_x(k):
        return (lax.rem(x + k, NX) * NY + y, col)

    def on_y(k):
        return (x * NY + lax.rem(y + k, NY), col)

    def on_z(k):
        return (row, lax.rem(z + k, NZ) * 2 + core)

    return x, y, z, core, on_x, on_y, on_z, (row, z * 2 + 1 - core)


def remote(src, dst, send_sem, recv_sem, peer):
    return pltpu.make_async_remote_copy(
        src_ref=src, dst_ref=dst, send_sem=send_sem, recv_sem=recv_sem, device_id=peer, device_id_type=MESH
    )


def build_maps(wb_ref, wg_ref, wo_ref, mix_map, out_map):
    rows, cols = 2 * HEADS * GROUP, CH * GROUP
    pick = iota((rows, HEADS), 0) >> 4
    head = iota((rows, HEADS), 1)
    picked = dot(where01(pick == head), wb_ref[...]) + dot(where01(pick == head + HEADS), wg_ref[...])
    spread = where01(iota((CH, cols), 0) == iota((CH, cols), 1) >> 4)
    full = dot(picked.astype(BF16), spread)
    same = (iota((rows, cols), 0) & 15) == (iota((rows, cols), 1) & 15)
    mix_map[...] = jnp.where(same, full, 0.0).astype(BF16)
    narrow = HEADS * GROUP
    w_out = wo_ref[...]
    high = w_out.astype(BF16)
    low = (w_out - high.astype(F32)).astype(BF16)
    pick = where01(iota((cols, CH), 0) >> 4 == iota((cols, CH), 1))
    spread = where01(iota((HEADS, narrow), 0) == iota((HEADS, narrow), 1) >> 4)
    same = (iota((cols, narrow), 0) & 15) == (iota((cols, narrow), 1) & 15)
    for part, w in enumerate((high, low)):
        full = dot(dot(pick, w, NT).astype(BF16), spread)
        out_map[:, part * narrow : (part + 1) * narrow] = jnp.where(same, full, 0.0).astype(BF16)


def group_rows(g, side):
    return pl.ds(pl.multiple_of(g * (2 * GROUP) + side * GROUP, GROUP), GROUP)


def both(f):
    return jnp.concatenate([f(0), f(1)], axis=1)


def edge_terms(slot, edge_s, mix_map, bias_s, gate_s):
    def pair(g, _):
        edge2 = both(lambda side: edge_s[slot, :, group_rows(g, side), :].reshape(CH * GROUP, BLOCK))
        mix = dot(mix_map[...], edge2)
        bias, gate = mix[: HEADS * GROUP], mix[HEADS * GROUP :]
        gate = 1.0 / (1.0 + jnp.exp(-gate))
        for side in range(2):
            part = slice(side * BLOCK, (side + 1) * BLOCK)
            bias_s[slot, :, group_rows(g, side), :] = bias[:, part].reshape(HEADS, GROUP, BLOCK)
            gate_s[slot, :, group_rows(g, side), :] = gate[:, part].reshape(HEADS, GROUP, BLOCK)
        return 0

    lax.fori_loop(0, BLOCK // (2 * GROUP), pair, 0)


def project(x_s, slot, w_s, y_s):
    width = w_s.shape[0]
    x = jnp.concatenate([x_s[side, slot].reshape(BLOCK, width // 2) for side in range(2)], axis=1)
    for n in range(0, width, 256):
        y_s[slot, :, n : n + 256] = dot(x, w_s[:, n : n + 256]).astype(BF16)


def attend(slot, live, q_s, k_s, v_s, bias_s, gate_s, score_s, weight_s, expo_s, numer_s, denom_s):
    width = q_s.shape[-1]
    head_dim = width // HEADS
    for h in range(HEADS):
        lo, hi = h * head_dim, (h + 1) * head_dim
        a, b = lo // 128 * 128, -(-hi // 128) * 128
        lane = iota((BLOCK, b - a), 1) + a
        q = q_s[slot, :, a:b]
        q = jnp.where((lane >= lo) & (lane < hi), q, jnp.zeros_like(q))
        raw = dot(q, k_s[slot, :, a:b], NT)
        score = jnp.clip(raw * (1.0 / head_dim**0.5), -5.0, 5.0) + bias_s[slot, h]
        expo = jnp.exp(score)
        score_s[slot, h] = score.astype(BF16)
        weight_s[h] = (expo * gate_s[slot, h]).astype(BF16)
        expo_s[:, h * BLOCK : (h + 1) * BLOCK] = expo.astype(BF16)
    for m in range(width // 128):
        heads = range(m * 128 // head_dim, (m * 128 + 127) // head_dim + 1)
        v = v_s[slot, :, m * 128 : (m + 1) * 128]
        lane = iota((BLOCK, 128), 1) + m * 128
        weights = jnp.concatenate([weight_s[h] for h in heads], axis=1)
        values = jnp.concatenate(
            [
                jnp.where((lane >= h * head_dim) & (lane < (h + 1) * head_dim), v, jnp.zeros_like(v))
                for h in heads
            ],
            axis=0,
        )
        numer = dot(weights, values)
        numer = jnp.where(live, numer, jnp.zeros_like(numer)).astype(BF16)
        side, first = divmod(m * 128, width // 2)
        numer_s[side, 2 * slot : 2 * slot + 2, :, first : first + 128] = numer.reshape(2, BLOCK // 2, 128)
    ones = where01(iota((HEADS, HEADS * BLOCK), 0) == iota((HEADS, HEADS * BLOCK), 1) >> 7)
    denom = dot(ones, expo_s[...], NT)
    denom_s[slot] = jnp.where(live, denom, jnp.zeros_like(denom))


def edge_output(slot, live, gain_ref, out_map, edge_s, score_s, mixed_s):
    factor = jnp.where(live, 1.0, 0.0)

    def pair(g, _):
        score = both(lambda side: score_s[slot, :, group_rows(g, side), :].reshape(HEADS * GROUP, BLOCK))
        mixed_s[...] = dot(out_map[...], jnp.concatenate([score, score], axis=0))
        for side in range(2):
            part = slice(side * BLOCK, (side + 1) * BLOCK)
            rows = group_rows(g, side)
            total = jnp.zeros((GROUP, BLOCK), F32)
            for c in range(CH):
                m = mixed_s[c * GROUP : (c + 1) * GROUP, part] + edge_s[slot, c, rows, :].astype(F32)
                mixed_s[c * GROUP : (c + 1) * GROUP, part] = m
                total += m * m
            scale = lax.rsqrt(total * (1.0 / CH) + 1e-5) * factor
            for c in range(CH):
                m = mixed_s[c * GROUP : (c + 1) * GROUP, part]
                edge_s[slot, c, rows, :] = (m * (scale * gain_ref[c])).astype(BF16)
        return 0

    lax.fori_loop(0, BLOCK // (2 * GROUP), pair, 0)


def layer_kernel(
    tile_ref,
    count_ref,
    gain_edge_ref,
    nodes_hbm,
    wb_hbm,
    wg_hbm,
    wo_hbm,
    gain_node_hbm,
    wq_hbm,
    wk_hbm,
    wv_hbm,
    wout_hbm,
    edges_hbm,
    nodes_out,
    edge_s,
    nodes_h,
    wb_ref,
    wg_ref,
    wo_ref,
    gain_node_ref,
    total_s,
    early_sem,
    pool_y,
    pool_x,
    pool_z,
    fill_send,
    fill_recv,
    pass_send,
    pass_recv,
    wish_send,
    wish_recv,
    core_send,
    meta_own,
    meta_vmem,
    meta,
    ring_send_sem,
    ring_recv_sem,
    pair_send_sem,
    pair_recv_sem,
    fill_send_sem,
    fill_recv_sem,
    pass_send_sem,
    pass_recv_sem,
    wish_send_sem,
    wish_recv_sem,
    meta_send_sem,
    meta_recv_sem,
    core_send_sem,
    core_recv_sem,
    local_sem,
    w_s,
    src_s,
    dest_s,
    q_s,
    k_s,
    v_s,
    mix_map,
    out_map,
    bias_s,
    gate_s,
    score_s,
    weight_s,
    expo_s,
    mixed_s,
    numer_s,
    denom_s,
    edge_sem,
    w_sem,
    sib_numer,
    pair_numer,
    sum_send,
    sum_recv,
    last_send,
    last_s,
    den_send,
    den_recv,
    sib_send_sem,
    sib_recv_sem,
    first_send_sem,
    first_recv_sem,
    sum_send_sem,
    sum_recv_sem,
    last_sem,
    den_send_sem,
    den_recv_sem,
):
    x, y, z, core, on_x, on_y, on_z, sibling = place()
    row, col = lax.axis_index("row"), lax.axis_index("col")
    width = gain_node_ref.shape[0]
    head_dim = width // HEADS
    half = width // 2
    slots = edge_s.shape[0]
    other = 1 - core
    flip, mirror = z + 1 - 2 * (z % 2), NZ - 1 - z
    near_z = flip * other + mirror * core
    far_z = mirror * other + flip * core
    near, far_pair = (row, near_z * 2 + core), (row, far_z * 2 + core)
    sends = []

    def push(src, dst, send_sem, recv_sem, peer):
        copy = remote(src, dst, send_sem, recv_sem, peer)
        copy.start()
        sends.append(copy)
        return copy

    early = []
    for side in range(2):
        early.append(
            pltpu.make_async_copy(
                nodes_hbm.at[:, :, side * half : (side + 1) * half], nodes_h.at[side], early_sem.at[side]
            )
        )
    for i, (a, b) in enumerate(
        ((wb_hbm, wb_ref), (wg_hbm, wg_ref), (wo_hbm, wo_ref), (gain_node_hbm, gain_node_ref))
    ):
        early.append(pltpu.make_async_copy(a, b, early_sem.at[2 + i]))
    for copy in early:
        copy.start()

    others = [(row, lax.rem(col + k, N_COL)) for k in range(1, N_COL)]
    peers = [on_x(1), on_x(3), on_x(2), on_y(1), on_y(3), on_y(2)] + others
    barrier = pltpu.get_barrier_semaphore()
    for peer in peers:
        pl.semaphore_signal(barrier, inc=1, device_id=peer, device_id_type=MESH)

    w_copies = []
    for i, w_hbm in enumerate((wq_hbm, wk_hbm, wv_hbm, wout_hbm)):
        w_copies.append(pltpu.make_async_copy(w_hbm, w_s.at[i], w_sem.at[i]))
    edge_copies = []
    for s in range(slots):
        edge_copies.append(pltpu.make_async_copy(edges_hbm.at[s], edge_s.at[s], edge_sem.at[s]))
        edge_copies[s].start()
    for copy in w_copies:
        copy.start()

    lane = iota(meta_own.shape, 1)
    words = jnp.zeros(meta_own.shape, jnp.int32)
    own_words = []
    for s in range(slots):
        tile = tile_ref[s]
        to, at = tile // SRC_BLOCKS, tile % SRC_BLOCKS
        t, o = at // PER_DEV, at % PER_DEV
        bx, by = t // NY, t % NY
        owner, p = to // PER_DEV, to % PER_DEV
        fields = [bx, by * PER_DEV + o, by, bx * PER_DEV + o, owner // 2, owner % 2 * PIECES + 2 * p, to]
        own_words.append(fields)
        for f, value in enumerate(fields):
            words = jnp.where(lane == f * slots + s, value, words)
    meta_own[...] = words
    for copy in early[:2]:
        copy.wait()

    def word(who, f, s):
        return own_words[s][f] if who is None else meta[who, 0, f * slots + s]

    pl.semaphore_wait(barrier, len(peers))

    rings = [(pool_y, y, on_y, 0), (pool_x, x, on_x, 1)]
    low, high = pl.ds(0, HALF), pl.ds(HALF, HALF)
    ring_copies = [{}, {}]

    def ring_start(step):
        for r, (pool, pos, on, side) in enumerate(rings):
            for way in range(2):
                part = step if way == 0 else 1 - step
                ring_copies[r][way, step] = push(
                    nodes_h.at[side, (low, high)[part]],
                    pool.at[pl.ds(pos * PIECES + part * HALF, HALF)],
                    ring_send_sem.at[r, way, step],
                    ring_recv_sem.at[r, way, step],
                    on(1 + 2 * way),
                )

    ring_start(0)
    sib_shard = push(
        nodes_h.at[other], pool_z.at[pl.ds(core * PIECES, PIECES)], pair_send_sem.at[0], pair_recv_sem.at[0], sibling
    )
    pair_own = push(
        nodes_h.at[core],
        pool_z.at[pl.ds((2 + core) * PIECES, PIECES)],
        pair_send_sem.at[1],
        pair_recv_sem.at[1],
        near,
    )
    for i, (peer, there) in enumerate(
        (
            (on_x(3), 0),
            (on_x(1), 1),
            (on_x(2), 2),
            (on_y(3), 3),
            (on_y(1), 4),
            (on_y(2), 5),
            (sibling, 6),
            ((row, flip * 2 + 1), 7 + core),
            ((row, mirror * 2), 7 + core),
        )
    ):
        push(meta_own, meta_vmem.at[there], meta_send_sem.at[i], meta_recv_sem.at[there], peer)
    ring_start(1)
    for pool, pos, on, side in rings:
        pool[pl.ds(pos * PIECES, PIECES)] = nodes_h[side]
    pool_z[pl.ds(core * PIECES, PIECES)] = nodes_h[core]
    sib_shard.wait_recv()
    pair_sib = push(
        pool_z.at[pl.ds(other * PIECES, PIECES)],
        pool_z.at[pl.ds((2 + other) * PIECES, PIECES)],
        pair_send_sem.at[2],
        pair_recv_sem.at[2],
        near,
    )

    def terms(s):
        edge_copies[s].wait()
        edge_terms(s, edge_s, mix_map, bias_s, gate_s)

    for copy in early[2:]:
        copy.wait()
    build_maps(wb_ref, wg_ref, wo_ref, mix_map, out_map)
    terms(0)

    for r, (pool, pos, on, side) in enumerate(rings):
        for way in range(2):
            owner = lax.rem(pos + 3 - 2 * way, 4)
            ring_copies[r][way, 0].wait_recv()
            here = pool.at[pl.ds(owner * PIECES + way * HALF, HALF)]
            ring_copies[r][way, 2] = push(
                here, here, ring_send_sem.at[r, way, 2], ring_recv_sem.at[r, way, 2], on(1 + 2 * way)
            )

    for i in range(9):
        remote(meta_own, meta_vmem.at[i], meta_send_sem.at[i], meta_recv_sem.at[i], sibling).wait_recv()
    to_smem = pltpu.make_async_copy(meta_vmem, meta, local_sem)
    to_smem.start()
    terms(1)
    to_smem.wait()

    def load_z(who, s):
        group = jnp.where(word(who, 4, s) == near_z, 2 * PIECES, 0)
        return pool_z[pl.ds(group + word(who, 5, s), 2)]

    pair_own.wait_recv()
    pair_sib.wait_recv()
    wishes = []
    for s in range(slots):
        for d in range(2):
            wish_send[s, d] = load_z(7 + d, s)
        wishes.append(
            push(wish_send.at[s], wish_recv.at[s], wish_send_sem.at[s], wish_recv_sem.at[s], far_pair)
        )
    terms(2)
    terms(3)

    fills = [(pool_y, x, on_x, 0, (0, 1, 2)), (pool_x, y, on_y, 2, (3, 4, 5))]
    fill_copies, pass_copies = {}, {}

    def fill_start(j):
        for f, (pool, pos, on, at, (plus, minus, far)) in enumerate(fills):
            for way in range(2):
                who = (plus, minus)[way]
                if j > 0:
                    fill_send[f, way, j, 0] = pool[word(who, at + 1, j - 1) * 2 + 1 - way]
                if j < slots:
                    fill_send[f, way, j, 1] = pool[word(far, at + 1, j) * 2 + way]
                part = pl.ds(1, 1) if j == 0 else pl.ds(0, 1) if j == slots else pl.ds(0, 2)
                fill_copies[f, way, j] = push(
                    fill_send.at[f, way, j, part],
                    fill_recv.at[f, way, j, part],
                    fill_send_sem.at[f, way, j],
                    fill_recv_sem.at[f, way, j],
                    on(1 + 2 * way),
                )

    def fill_pass(s):
        for f, (pool, pos, on, at, (plus, minus, far)) in enumerate(fills):
            for way in range(2):
                who = (plus, minus)[way]
                fill_copies[f, way, s].wait_recv()
                mine = pool[word(who, at + 1, s) * 2 + way]
                pass_send[f, way, s] = jnp.where(word(who, at, s) == pos, mine, fill_recv[f, way, s, 1])
                pass_copies[f, way, s] = push(
                    pass_send.at[f, way, s],
                    pass_recv.at[f, way, s],
                    pass_send_sem.at[f, way, s],
                    pass_recv_sem.at[f, way, s],
                    on(1 + 2 * way),
                )
        if s + 2 <= slots:
            fill_start(s + 2)

    def dest_start(s):
        wishes[s].wait_recv()
        for who, d in ((6, other), (None, core)):
            at = word(who, 4, s)
            inside = jnp.where(at == z, 1, jnp.where(at == near_z, 1, 0))
            value = jnp.where(inside == 1, load_z(who, s), wish_recv[s, d])
            if who is None:
                dest_s[core, s] = value
            else:
                core_send[s] = value
        return push(
            core_send.at[s], dest_s.at[core, s], core_send_sem.at[s], core_recv_sem.at[s], sibling
        )

    def source(s):
        if s == slots - 1:
            for f in range(2):
                for way in range(2):
                    fill_copies[f, way, slots].wait_recv()
        for f, (pool, pos, on, at, who) in enumerate(fills):
            p = word(None, at, s)
            for way in range(2):
                pass_copies[f, way, s].wait_recv()
            for k in range(2):
                mine = pool[word(None, at + 1, s) * 2 + k]
                direct, passed = fill_recv[f, 1 - k, s + 1, 0], pass_recv[f, k, s]
                beside = p == lax.rem(pos + 1 + 2 * k, 4)
                src_s[f, s, k] = jnp.where(p == pos, mine, jnp.where(beside, direct, passed))

    lives = [s < count_ref[0] for s in range(slots)]
    sib_copies, first_copies, dest_copies = [], [], []

    def tile(s):
        dest_copies[s].wait_recv()
        project(dest_s, s, w_s.at[0], q_s)
        source(s)
        project(src_s, s, w_s.at[1], k_s)
        project(src_s, s, w_s.at[2], v_s)
        attend(s, lives[s], q_s, k_s, v_s, bias_s, gate_s, score_s, weight_s, expo_s, numer_s, denom_s)
        here = pl.ds(2 * s, 2)
        sib_copies.append(
            push(numer_s.at[other, here], sib_numer.at[here], sib_send_sem.at[s], sib_recv_sem.at[s], sibling)
        )
        first_copies.append(
            push(
                numer_s.at[core, here],
                pair_numer.at[core, here],
                first_send_sem.at[s, 0],
                first_recv_sem.at[s, 0],
                far_pair,
            )
        )

    def pass_sibling(s):
        sib_copies[s].wait_recv()
        here = pl.ds(2 * s, 2)
        first_copies.append(
            push(
                sib_numer.at[here],
                pair_numer.at[other, here],
                first_send_sem.at[s, 1],
                first_recv_sem.at[s, 1],
                far_pair,
            )
        )

    def emit(s):
        edge_output(s, lives[s], gain_edge_ref, out_map, edge_s, score_s, mixed_s)

    for f in range(2):
        for way in range(2):
            for step in (1, 2):
                ring_copies[f][way, step].wait_recv()
    fill_start(0)
    fill_start(1)
    for copy in w_copies:
        copy.wait()
    dest_copies.append(dest_start(0))
    fill_pass(0)
    dest_copies.append(dest_start(1))
    fill_pass(1)
    tile(0)
    dest_copies.append(dest_start(2))
    fill_pass(2)
    pass_sibling(0)
    tile(1)
    dest_copies.append(dest_start(3))
    fill_pass(3)
    pass_sibling(1)
    tile(2)
    pass_sibling(2)
    tile(3)
    pass_sibling(3)

    mine = [word(None, 6, s) for s in range(slots)]
    ids = [mine, [word(6, 6, s) for s in range(slots)]]
    ids += [[word(7 + d, 6, s) for s in range(slots)] for d in range(2)]

    def find(of, a):
        index, found = jnp.int32(0), jnp.int32(0)
        for s in range(slots):
            index = jnp.where(of[s] == a, s, index)
            found = jnp.where(of[s] == a, 1, found)
        return index, found

    def denom_of(owner, o):
        index, found = find(mine, owner * PER_DEV + o)
        d = denom_s[index]
        return jnp.where(found > 0, d, jnp.zeros_like(d))

    den_copies = []
    for k in range(1, N_COL):
        for o in range(PER_DEV):
            den_send[k, o] = denom_of(lax.rem(col + k, N_COL), o)
        den_copies.append(
            push(den_send.at[k], den_recv.at[k], den_send_sem.at[k], den_recv_sem.at[k], others[k - 1])
        )

    emit(0)
    for copy in first_copies:
        copy.wait_recv()

    def block_sum(at_z, at_core, o):
        a = (at_z * 2 + at_core) * PER_DEV + o
        total = jnp.zeros((2, BLOCK // 2, half), F32)
        for i, of in enumerate(ids):
            index, found = find(of, a)
            here = pl.ds(2 * index, 2)
            part = (numer_s[core, here] if i == 0 else sib_numer[here] if i == 1 else pair_numer[i - 2, here])
            total += jnp.where(found > 0, part, jnp.zeros_like(part)).astype(F32)
        return total

    sum_copies = []
    for i, at_core in enumerate((other, core)):
        for o in range(PER_DEV):
            sum_send[i, 2 * o : 2 * o + 2] = block_sum(near_z, at_core, o).astype(BF16)
        sum_copies.append(
            push(sum_send.at[i], sum_recv.at[i], sum_send_sem.at[i], sum_recv_sem.at[i], near)
        )
    for i, at_core in enumerate((other, core)):
        for o in range(PER_DEV):
            total_s[i, 2 * o : 2 * o + 2] = block_sum(z, at_core, o)
    emit(1)
    emit(2)
    sum_copies[0].wait_recv()
    for o in range(PER_DEV):
        here = slice(2 * o, 2 * o + 2)
        last_send[here] = (total_s[0, here] + sum_recv[0, here].astype(F32)).astype(BF16)
    last_copy = push(last_send, last_s.at[core], last_sem.at[0], last_sem.at[1], sibling)
    emit(3)
    for copy in den_copies:
        copy.wait_recv()
    heads = iota((2 * HEADS, width), 0) & 7
    lanes = iota((2 * HEADS, width), 1)
    expand = where01((lanes >= heads * head_dim) & (lanes < (heads + 1) * head_dim))
    scales = []
    for o in range(PER_DEV):
        d = denom_of(col, o)
        for k in range(1, N_COL):
            d += den_recv[k, o]
        inverse = jnp.where(d > 0.0, 1.0 / jnp.where(d > 0.0, d, 1.0), 0.0)
        upper = inverse.astype(BF16).astype(F32)
        scales.append(dot(jnp.concatenate([upper, inverse - upper], axis=0).astype(BF16), expand, TN))
    sum_copies[1].wait_recv()
    for o in range(PER_DEV):
        here = slice(2 * o, 2 * o + 2)
        last_s[core, here] = (total_s[1, here] + sum_recv[1, here].astype(F32)).astype(BF16)
    last_copy.wait_recv()
    for o in range(PER_DEV):
        here = slice(2 * o, 2 * o + 2)
        numer = jnp.concatenate([last_s[side, here].reshape(BLOCK, half) for side in range(2)], axis=1)
        attended = (numer.astype(F32) * scales[o]).astype(BF16)
        base = jnp.concatenate([nodes_h[side, here].reshape(BLOCK, half) for side in range(2)], axis=1)
        mixed = base.astype(F32) + dot(attended, w_s[3])
        mean = jnp.mean(mixed * mixed, axis=1, keepdims=True)
        nodes_out[o * BLOCK : (o + 1) * BLOCK] = (
            mixed * lax.rsqrt(mean + 1e-05) * gain_node_ref[...][None]
        ).astype(BF16)
    for copy in sends:
        copy.wait_send()


def store_kernel(nodes_ref, edge_ref, nodes_out, edges_out, sem):
    slots = edge_ref.shape[0]
    copies = [pltpu.make_async_copy(nodes_ref, nodes_out, sem.at[slots])]
    for s in range(slots):
        copies.append(pltpu.make_async_copy(edge_ref.at[s], edges_out.at[s], sem.at[s]))
    for copy in copies:
        copy.start()
    for copy in copies:
        copy.wait()


def store_call(nodes_new, edges_new):
    vm = pl.BlockSpec(memory_space=pltpu.VMEM)
    hbm = pl.BlockSpec(memory_space=pl.ANY)
    return pl.pallas_call(
        store_kernel,
        in_specs=[vm, vm],
        out_specs=[hbm, hbm],
        out_shape=[
            jax.ShapeDtypeStruct(nodes_new.shape, BF16),
            jax.ShapeDtypeStruct(edges_new.shape, BF16),
        ],
        scratch_shapes=[pltpu.SemaphoreType.DMA((edges_new.shape[0] + 1,))],
        compiler_params=pltpu.CompilerParams(vmem_limit_bytes=1 * 1024 * 1024),
        name="store",
    )(
        pltpu.with_memory_space_constraint(nodes_new, pltpu.VMEM),
        pltpu.with_memory_space_constraint(edges_new, pltpu.VMEM),
    )


def on_device(
    nodes,
    w_query,
    w_key,
    w_value,
    w_out,
    w_edge_gate,
    w_edge_bias,
    w_edge_out,
    gain_node,
    gain_edge,
    edges,
    tile_list,
    tile_count,
):
    rows, width = nodes.shape
    slots = edges.shape[2]
    piece = rows // PIECES
    half = width // 2
    vm = pl.BlockSpec(memory_space=pltpu.VMEM)
    sm = pl.BlockSpec(memory_space=pltpu.SMEM)
    hbm = pl.BlockSpec(memory_space=pl.ANY)
    dma = pltpu.SemaphoreType.DMA
    v = pltpu.VMEM
    nodes_out, edges_out = pl.pallas_call(
        layer_kernel,
        in_specs=[sm, sm, sm] + [hbm] * 10,
        out_specs=[vm, vm],
        out_shape=[v((rows, width), BF16), v((slots, CH, BLOCK, BLOCK), BF16)],
        scratch_shapes=[
            v((2, PIECES, piece, half), BF16),
            v((HEADS, CH), BF16),
            v((HEADS, CH), BF16),
            v((HEADS, CH), F32),
            v((width,), F32),
            v((2, PIECES, piece, half), F32),
            dma((6,)),
            v((NY * PIECES, piece, half), BF16),
            v((NX * PIECES, piece, half), BF16),
            v((4 * PIECES, piece, half), BF16),
            v((2, 2, slots + 1, 2, piece, half), BF16),
            v((2, 2, slots + 1, 2, piece, half), BF16),
            v((2, 2, slots, piece, half), BF16),
            v((2, 2, slots, piece, half), BF16),
            v((slots, 2, 2, piece, half), BF16),
            v((slots, 2, 2, piece, half), BF16),
            v((slots, 2, piece, half), BF16),
            v((8, 128), jnp.int32),
            v((9, 8, 128), jnp.int32),
            pltpu.SMEM((9, 8, 128), jnp.int32),
            dma((2, 2, 3)),
            dma((2, 2, 3)),
            dma((3,)),
            dma((3,)),
            dma((2, 2, slots + 1)),
            dma((2, 2, slots + 1)),
            dma((2, 2, slots)),
            dma((2, 2, slots)),
            dma((slots,)),
            dma((slots,)),
            dma((9,)),
            dma((9,)),
            dma((slots,)),
            dma((slots,)),
            dma,
            v((4, width, width), BF16),
            v((2, slots, 2, piece, half), BF16),
            v((2, slots, 2, piece, half), BF16),
            v((slots, BLOCK, width), BF16),
            v((slots, BLOCK, width), BF16),
            v((slots, BLOCK, width), BF16),
            v((2 * HEADS * GROUP, CH * GROUP), BF16),
            v((CH * GROUP, 2 * HEADS * GROUP), BF16),
            v((slots, HEADS, BLOCK, BLOCK), F32),
            v((slots, HEADS, BLOCK, BLOCK), F32),
            v((slots, HEADS, BLOCK, BLOCK), BF16),
            v((HEADS, BLOCK, BLOCK), BF16),
            v((BLOCK, HEADS * BLOCK), BF16),
            v((CH * GROUP, 2 * BLOCK), F32),
            v((2, 2 * slots, piece, half), BF16),
            v((slots, HEADS, BLOCK), F32),
            dma((slots,)),
            dma((4,)),
            v((2 * slots, piece, half), BF16),
            v((2, 2 * slots, piece, half), BF16),
            v((2, PIECES, piece, half), BF16),
            v((2, PIECES, piece, half), BF16),
            v((PIECES, piece, half), BF16),
            v((2, PIECES, piece, half), BF16),
            v((N_COL, PER_DEV, HEADS, BLOCK), F32),
            v((N_COL, PER_DEV, HEADS, BLOCK), F32),
            dma((slots,)),
            dma((slots,)),
            dma((slots, 2)),
            dma((slots, 2)),
            dma((2,)),
            dma((2,)),
            dma((2,)),
            dma((N_COL,)),
            dma((N_COL,)),
        ],
        compiler_params=pltpu.CompilerParams(
            collective_id=0, has_side_effects=True, vmem_limit_bytes=48 * 1024 * 1024
        ),
        name="layer",
    )(
        tile_list.reshape(-1),
        tile_count.reshape(1),
        gain_edge,
        nodes.reshape(PIECES, piece, width),
        w_edge_bias.T,
        w_edge_gate.T,
        w_edge_out,
        gain_node,
        w_query,
        w_key,
        w_value,
        w_out,
        edges.reshape(slots, CH, BLOCK, BLOCK),
    )

    nodes_out, edges_out = store_call(nodes_out, edges_out)
    return (nodes_out, edges_out.reshape(edges.shape))


def solution(mesh):
    return jax.shard_map(
        on_device,
        mesh=mesh,
        in_specs=(
            P(("row", "col"), None),
            *[P()] * 9,
            P("row", "col", None, None, None, None),
            P("row", "col", None),
            P("row", "col"),
        ),
        out_specs=(P(("row", "col"), None), P("row", "col", None, None, None, None)),
        check_vma=False,
    )
```

```python
import jax
import jax.numpy as jnp
from jax import lax
from jax.experimental import pallas as pl
from jax.experimental.pallas import tpu as pltpu
from jax.sharding import PartitionSpec as P

HEADS = 8
BLOCK = 128
CH = 64
GROUP = 16
NX, NY, NZ = 4, 4, 4
PER_DEV = 3
PIECES = 2 * PER_DEV
HALF = PIECES // 2
SRC_BLOCKS = NX * NY * PER_DEV
N_COL = 2 * NZ
F32 = jnp.float32
BF16 = jnp.bfloat16
NT = (((1,), (1,)), ((), ()))
TN = (((0,), (0,)), ((), ()))
MESH = pl.DeviceIdType.MESH


def iota(shape, dim):
    return lax.broadcasted_iota(jnp.int32, shape, dim)


def dot(a, b, dims=(((1,), (0,)), ((), ()))):
    return lax.dot_general(a, b, dims, preferred_element_type=F32)


def where01(mask):
    return jnp.where(mask, 1.0, 0.0).astype(BF16)


def place():
    row, col = lax.axis_index("row"), lax.axis_index("col")
    x, y, z, core = row // NY, row % NY, col // 2, col % 2

    def on_x(k):
        return (lax.rem(x + k, NX) * NY + y, col)

    def on_y(k):
        return (x * NY + lax.rem(y + k, NY), col)

    def on_z(k):
        return (row, lax.rem(z + k, NZ) * 2 + core)

    return x, y, z, core, on_x, on_y, on_z, (row, z * 2 + 1 - core)


def remote(src, dst, send_sem, recv_sem, peer):
    return pltpu.make_async_remote_copy(
        src_ref=src, dst_ref=dst, send_sem=send_sem, recv_sem=recv_sem, device_id=peer, device_id_type=MESH
    )


def build_maps(wb_ref, wg_ref, wo_ref, mix_map, out_map):
    rows, cols = 2 * HEADS * GROUP, CH * GROUP
    pick = iota((rows, HEADS), 0) >> 4
    head = iota((rows, HEADS), 1)
    picked = dot(where01(pick == head), wb_ref[...]) + dot(where01(pick == head + HEADS), wg_ref[...])
    spread = where01(iota((CH, cols), 0) == iota((CH, cols), 1) >> 4)
    full = dot(picked.astype(BF16), spread)
    same = (iota((rows, cols), 0) & 15) == (iota((rows, cols), 1) & 15)
    mix_map[...] = jnp.where(same, full, 0.0).astype(BF16)
    narrow = HEADS * GROUP
    w_out = wo_ref[...]
    high = w_out.astype(BF16)
    low = (w_out - high.astype(F32)).astype(BF16)
    pick = where01(iota((cols, CH), 0) >> 4 == iota((cols, CH), 1))
    spread = where01(iota((HEADS, narrow), 0) == iota((HEADS, narrow), 1) >> 4)
    same = (iota((cols, narrow), 0) & 15) == (iota((cols, narrow), 1) & 15)
    for part, w in enumerate((high, low)):
        full = dot(dot(pick, w, NT).astype(BF16), spread)
        out_map[:, part * narrow : (part + 1) * narrow] = jnp.where(same, full, 0.0).astype(BF16)


def group_rows(g, side):
    return pl.ds(pl.multiple_of(g * (2 * GROUP) + side * GROUP, GROUP), GROUP)


def both(f):
    return jnp.concatenate([f(0), f(1)], axis=1)


def edge_terms(slot, edge_s, mix_map, bias_s, gate_s):
    def pair(g, _):
        edge2 = both(lambda side: edge_s[slot, :, group_rows(g, side), :].reshape(CH * GROUP, BLOCK))
        mix = dot(mix_map[...], edge2)
        bias, gate = mix[: HEADS * GROUP], mix[HEADS * GROUP :]
        gate = 1.0 / (1.0 + jnp.exp(-gate))
        for side in range(2):
            part = slice(side * BLOCK, (side + 1) * BLOCK)
            bias_s[slot, :, group_rows(g, side), :] = bias[:, part].reshape(HEADS, GROUP, BLOCK)
            gate_s[slot, :, group_rows(g, side), :] = gate[:, part].reshape(HEADS, GROUP, BLOCK)
        return 0

    lax.fori_loop(0, BLOCK // (2 * GROUP), pair, 0)


def project(x_s, slot, w_s, y_s):
    width = w_s.shape[0]
    x = jnp.concatenate([x_s[side, slot].reshape(BLOCK, width // 2) for side in range(2)], axis=1)
    for n in range(0, width, 256):
        y_s[slot, :, n : n + 256] = dot(x, w_s[:, n : n + 256]).astype(BF16)


def attend(slot, live, q_s, k_s, v_s, bias_s, gate_s, score_s, weight_s, expo_s, numer_s, denom_s):
    width = q_s.shape[-1]
    head_dim = width // HEADS
    for h in range(HEADS):
        lo, hi = h * head_dim, (h + 1) * head_dim
        a, b = lo // 128 * 128, -(-hi // 128) * 128
        lane = iota((BLOCK, b - a), 1) + a
        q = q_s[slot, :, a:b]
        q = jnp.where((lane >= lo) & (lane < hi), q, jnp.zeros_like(q))
        raw = dot(q, k_s[slot, :, a:b], NT)
        score = jnp.clip(raw * (1.0 / head_dim**0.5), -5.0, 5.0) + bias_s[slot, h]
        expo = jnp.exp(score)
        score_s[slot, h] = score.astype(BF16)
        weight_s[h] = (expo * gate_s[slot, h]).astype(BF16)
        expo_s[:, h * BLOCK : (h + 1) * BLOCK] = expo.astype(BF16)
    for m in range(width // 128):
        heads = range(m * 128 // head_dim, (m * 128 + 127) // head_dim + 1)
        v = v_s[slot, :, m * 128 : (m + 1) * 128]
        lane = iota((BLOCK, 128), 1) + m * 128
        weights = jnp.concatenate([weight_s[h] for h in heads], axis=1)
        values = jnp.concatenate(
            [
                jnp.where((lane >= h * head_dim) & (lane < (h + 1) * head_dim), v, jnp.zeros_like(v))
                for h in heads
            ],
            axis=0,
        )
        numer = dot(weights, values)
        numer = jnp.where(live, numer, jnp.zeros_like(numer)).astype(BF16)
        side, first = divmod(m * 128, width // 2)
        numer_s[side, 2 * slot : 2 * slot + 2, :, first : first + 128] = numer.reshape(2, BLOCK // 2, 128)
    ones = where01(iota((HEADS, HEADS * BLOCK), 0) == iota((HEADS, HEADS * BLOCK), 1) >> 7)
    denom = dot(ones, expo_s[...], NT)
    denom_s[slot] = jnp.where(live, denom, jnp.zeros_like(denom))


def edge_output(slot, live, gain_ref, out_map, edge_s, score_s, mixed_s):
    factor = jnp.where(live, 1.0, 0.0)

    def pair(g, _):
        score = both(lambda side: score_s[slot, :, group_rows(g, side), :].reshape(HEADS * GROUP, BLOCK))
        mixed_s[...] = dot(out_map[...], jnp.concatenate([score, score], axis=0))
        for side in range(2):
            part = slice(side * BLOCK, (side + 1) * BLOCK)
            rows = group_rows(g, side)
            total = jnp.zeros((GROUP, BLOCK), F32)
            for c in range(CH):
                m = mixed_s[c * GROUP : (c + 1) * GROUP, part] + edge_s[slot, c, rows, :].astype(F32)
                mixed_s[c * GROUP : (c + 1) * GROUP, part] = m
                total += m * m
            scale = lax.rsqrt(total * (1.0 / CH) + 1e-5) * factor
            for c in range(CH):
                m = mixed_s[c * GROUP : (c + 1) * GROUP, part]
                edge_s[slot, c, rows, :] = (m * (scale * gain_ref[c])).astype(BF16)
        return 0

    lax.fori_loop(0, BLOCK // (2 * GROUP), pair, 0)


def layer_kernel(
    tile_ref,
    count_ref,
    gain_edge_ref,
    nodes_hbm,
    wb_hbm,
    wg_hbm,
    wo_hbm,
    gain_node_hbm,
    wq_hbm,
    wk_hbm,
    wv_hbm,
    wout_hbm,
    edges_hbm,
    nodes_out,
    edge_s,
    nodes_h,
    wb_ref,
    wg_ref,
    wo_ref,
    gain_node_ref,
    total_s,
    early_sem,
    pool_y,
    pool_x,
    pool_z,
    fill_send,
    fill_recv,
    pass_send,
    pass_recv,
    wish_send,
    wish_recv,
    core_send,
    meta_own,
    meta_vmem,
    meta,
    ring_send_sem,
    ring_recv_sem,
    pair_send_sem,
    pair_recv_sem,
    fill_send_sem,
    fill_recv_sem,
    pass_send_sem,
    pass_recv_sem,
    wish_send_sem,
    wish_recv_sem,
    meta_send_sem,
    meta_recv_sem,
    core_send_sem,
    core_recv_sem,
    local_sem,
    w_s,
    src_s,
    dest_s,
    q_s,
    k_s,
    v_s,
    mix_map,
    out_map,
    bias_s,
    gate_s,
    score_s,
    weight_s,
    expo_s,
    mixed_s,
    numer_s,
    denom_s,
    edge_sem,
    w_sem,
    sib_numer,
    pair_numer,
    sum_send,
    sum_recv,
    last_send,
    last_s,
    den_send,
    den_recv,
    sib_send_sem,
    sib_recv_sem,
    first_send_sem,
    first_recv_sem,
    sum_send_sem,
    sum_recv_sem,
    last_sem,
    den_send_sem,
    den_recv_sem,
):
    x, y, z, core, on_x, on_y, on_z, sibling = place()
    row, col = lax.axis_index("row"), lax.axis_index("col")
    width = gain_node_ref.shape[0]
    head_dim = width // HEADS
    half = width // 2
    slots = edge_s.shape[0]
    other = 1 - core
    flip, mirror = z + 1 - 2 * (z % 2), NZ - 1 - z
    near_z = flip * other + mirror * core
    far_z = mirror * other + flip * core
    near, far_pair = (row, near_z * 2 + core), (row, far_z * 2 + core)
    sends = []

    def push(src, dst, send_sem, recv_sem, peer):
        copy = remote(src, dst, send_sem, recv_sem, peer)
        copy.start()
        sends.append(copy)
        return copy

    early = []
    for side in range(2):
        early.append(
            pltpu.make_async_copy(
                nodes_hbm.at[:, :, side * half : (side + 1) * half], nodes_h.at[side], early_sem.at[side]
            )
        )
    for i, (a, b) in enumerate(
        ((wb_hbm, wb_ref), (wg_hbm, wg_ref), (wo_hbm, wo_ref), (gain_node_hbm, gain_node_ref))
    ):
        early.append(pltpu.make_async_copy(a, b, early_sem.at[2 + i]))
    for copy in early:
        copy.start()

    others = [(row, lax.rem(col + k, N_COL)) for k in range(1, N_COL)]
    peers = [on_x(1), on_x(3), on_x(2), on_y(1), on_y(3), on_y(2)] + others
    barrier = pltpu.get_barrier_semaphore()
    for peer in peers:
        pl.semaphore_signal(barrier, inc=1, device_id=peer, device_id_type=MESH)

    w_copies = []
    for i, w_hbm in enumerate((wq_hbm, wk_hbm, wv_hbm, wout_hbm)):
        w_copies.append(pltpu.make_async_copy(w_hbm, w_s.at[i], w_sem.at[i]))
    edge_copies = []
    for s in range(slots):
        edge_copies.append(pltpu.make_async_copy(edges_hbm.at[s], edge_s.at[s], edge_sem.at[s]))
        edge_copies[s].start()
    for copy in w_copies:
        copy.start()

    lane = iota(meta_own.shape, 1)
    words = jnp.zeros(meta_own.shape, jnp.int32)
    own_words = []
    for s in range(slots):
        tile = tile_ref[s]
        to, at = tile // SRC_BLOCKS, tile % SRC_BLOCKS
        t, o = at // PER_DEV, at % PER_DEV
        bx, by = t // NY, t % NY
        owner, p = to // PER_DEV, to % PER_DEV
        fields = [bx, by * PER_DEV + o, by, bx * PER_DEV + o, owner // 2, owner % 2 * PIECES + 2 * p, to]
        own_words.append(fields)
        for f, value in enumerate(fields):
            words = jnp.where(lane == f * slots + s, value, words)
    meta_own[...] = words
    for copy in early[:2]:
        copy.wait()

    def word(who, f, s):
        return own_words[s][f] if who is None else meta[who, 0, f * slots + s]

    pl.semaphore_wait(barrier, len(peers))

    rings = [(pool_y, y, on_y, 0), (pool_x, x, on_x, 1)]
    low, high = pl.ds(0, HALF), pl.ds(HALF, HALF)
    ring_copies = [{}, {}]

    def ring_start(step):
        for r, (pool, pos, on, side) in enumerate(rings):
            for way in range(2):
                part = step if way == 0 else 1 - step
                ring_copies[r][way, step] = push(
                    nodes_h.at[side, (low, high)[part]],
                    pool.at[pl.ds(pos * PIECES + part * HALF, HALF)],
                    ring_send_sem.at[r, way, step],
                    ring_recv_sem.at[r, way, step],
                    on(1 + 2 * way),
                )

    ring_start(0)
    sib_shard = push(
        nodes_h.at[other], pool_z.at[pl.ds(core * PIECES, PIECES)], pair_send_sem.at[0], pair_recv_sem.at[0], sibling
    )
    pair_own = push(
        nodes_h.at[core],
        pool_z.at[pl.ds((2 + core) * PIECES, PIECES)],
        pair_send_sem.at[1],
        pair_recv_sem.at[1],
        near,
    )
    for i, (peer, there) in enumerate(
        (
            (on_x(3), 0),
            (on_x(1), 1),
            (on_x(2), 2),
            (on_y(3), 3),
            (on_y(1), 4),
            (on_y(2), 5),
            (sibling, 6),
            ((row, flip * 2 + 1), 7 + core),
            ((row, mirror * 2), 7 + core),
        )
    ):
        push(meta_own, meta_vmem.at[there], meta_send_sem.at[i], meta_recv_sem.at[there], peer)
    ring_start(1)
    for pool, pos, on, side in rings:
        pool[pl.ds(pos * PIECES, PIECES)] = nodes_h[side]
    pool_z[pl.ds(core * PIECES, PIECES)] = nodes_h[core]
    sib_shard.wait_recv()
    pair_sib = push(
        pool_z.at[pl.ds(other * PIECES, PIECES)],
        pool_z.at[pl.ds((2 + other) * PIECES, PIECES)],
        pair_send_sem.at[2],
        pair_recv_sem.at[2],
        near,
    )

    def terms(s):
        edge_copies[s].wait()
        edge_terms(s, edge_s, mix_map, bias_s, gate_s)

    for copy in early[2:]:
        copy.wait()
    build_maps(wb_ref, wg_ref, wo_ref, mix_map, out_map)
    terms(0)

    for r, (pool, pos, on, side) in enumerate(rings):
        for way in range(2):
            owner = lax.rem(pos + 3 - 2 * way, 4)
            ring_copies[r][way, 0].wait_recv()
            here = pool.at[pl.ds(owner * PIECES + way * HALF, HALF)]
            ring_copies[r][way, 2] = push(
                here, here, ring_send_sem.at[r, way, 2], ring_recv_sem.at[r, way, 2], on(1 + 2 * way)
            )

    for i in range(9):
        remote(meta_own, meta_vmem.at[i], meta_send_sem.at[i], meta_recv_sem.at[i], sibling).wait_recv()
    to_smem = pltpu.make_async_copy(meta_vmem, meta, local_sem)
    to_smem.start()
    terms(1)
    to_smem.wait()

    def load_z(who, s):
        group = jnp.where(word(who, 4, s) == near_z, 2 * PIECES, 0)
        return pool_z[pl.ds(group + word(who, 5, s), 2)]

    pair_own.wait_recv()
    pair_sib.wait_recv()
    wishes = []
    for s in range(slots):
        for d in range(2):
            wish_send[s, d] = load_z(7 + d, s)
        wishes.append(
            push(wish_send.at[s], wish_recv.at[s], wish_send_sem.at[s], wish_recv_sem.at[s], far_pair)
        )
    terms(2)

    fills = [(pool_y, x, on_x, 0, (0, 1, 2)), (pool_x, y, on_y, 2, (3, 4, 5))]
    fill_copies, pass_copies = {}, {}

    def fill_start(j):
        for f, (pool, pos, on, at, (plus, minus, far)) in enumerate(fills):
            for way in range(2):
                who = (plus, minus)[way]
                if j > 0:
                    fill_send[f, way, j, 0] = pool[word(who, at + 1, j - 1) * 2 + 1 - way]
                if j < slots:
                    fill_send[f, way, j, 1] = pool[word(far, at + 1, j) * 2 + way]
                part = pl.ds(1, 1) if j == 0 else pl.ds(0, 1) if j == slots else pl.ds(0, 2)
                fill_copies[f, way, j] = push(
                    fill_send.at[f, way, j, part],
                    fill_recv.at[f, way, j, part],
                    fill_send_sem.at[f, way, j],
                    fill_recv_sem.at[f, way, j],
                    on(1 + 2 * way),
                )

    def fill_pass(s):
        for f, (pool, pos, on, at, (plus, minus, far)) in enumerate(fills):
            for way in range(2):
                who = (plus, minus)[way]
                fill_copies[f, way, s].wait_recv()
                mine = pool[word(who, at + 1, s) * 2 + way]
                pass_send[f, way, s] = jnp.where(word(who, at, s) == pos, mine, fill_recv[f, way, s, 1])
                pass_copies[f, way, s] = push(
                    pass_send.at[f, way, s],
                    pass_recv.at[f, way, s],
                    pass_send_sem.at[f, way, s],
                    pass_recv_sem.at[f, way, s],
                    on(1 + 2 * way),
                )
        if s + 2 <= slots:
            fill_start(s + 2)

    def dest_start(s):
        wishes[s].wait_recv()
        for who, d in ((6, other), (None, core)):
            at = word(who, 4, s)
            inside = jnp.where(at == z, 1, jnp.where(at == near_z, 1, 0))
            value = jnp.where(inside == 1, load_z(who, s), wish_recv[s, d])
            if who is None:
                dest_s[core, s] = value
            else:
                core_send[s] = value
        return push(
            core_send.at[s], dest_s.at[core, s], core_send_sem.at[s], core_recv_sem.at[s], sibling
        )

    def source(s):
        if s == slots - 1:
            for f in range(2):
                for way in range(2):
                    fill_copies[f, way, slots].wait_recv()
        for f, (pool, pos, on, at, who) in enumerate(fills):
            p = word(None, at, s)
            for way in range(2):
                pass_copies[f, way, s].wait_recv()
            for k in range(2):
                mine = pool[word(None, at + 1, s) * 2 + k]
                direct, passed = fill_recv[f, 1 - k, s + 1, 0], pass_recv[f, k, s]
                beside = p == lax.rem(pos + 1 + 2 * k, 4)
                src_s[f, s, k] = jnp.where(p == pos, mine, jnp.where(beside, direct, passed))

    lives = [s < count_ref[0] for s in range(slots)]
    sib_copies, first_copies, dest_copies = [], [], []

    def tile(s):
        dest_copies[s].wait_recv()
        project(dest_s, s, w_s.at[0], q_s)
        source(s)
        project(src_s, s, w_s.at[1], k_s)
        project(src_s, s, w_s.at[2], v_s)
        attend(s, lives[s], q_s, k_s, v_s, bias_s, gate_s, score_s, weight_s, expo_s, numer_s, denom_s)
        here = pl.ds(2 * s, 2)
        sib_copies.append(
            push(numer_s.at[other, here], sib_numer.at[here], sib_send_sem.at[s], sib_recv_sem.at[s], sibling)
        )
        first_copies.append(
            push(
                numer_s.at[core, here],
                pair_numer.at[core, here],
                first_send_sem.at[s, 0],
                first_recv_sem.at[s, 0],
                far_pair,
            )
        )

    def pass_sibling(s):
        sib_copies[s].wait_recv()
        here = pl.ds(2 * s, 2)
        first_copies.append(
            push(
                sib_numer.at[here],
                pair_numer.at[other, here],
                first_send_sem.at[s, 1],
                first_recv_sem.at[s, 1],
                far_pair,
            )
        )

    def emit(s):
        edge_output(s, lives[s], gain_edge_ref, out_map, edge_s, score_s, mixed_s)

    for f in range(2):
        for way in range(2):
            for step in (1, 2):
                ring_copies[f][way, step].wait_recv()
    fill_start(0)
    fill_start(1)
    terms(3)
    for copy in w_copies:
        copy.wait()
    dest_copies.append(dest_start(0))
    fill_pass(0)
    dest_copies.append(dest_start(1))
    fill_pass(1)
    tile(0)
    dest_copies.append(dest_start(2))
    fill_pass(2)
    pass_sibling(0)
    tile(1)
    dest_copies.append(dest_start(3))
    fill_pass(3)
    pass_sibling(1)
    tile(2)
    pass_sibling(2)
    tile(3)
    pass_sibling(3)

    mine = [word(None, 6, s) for s in range(slots)]
    ids = [mine, [word(6, 6, s) for s in range(slots)]]
    ids += [[word(7 + d, 6, s) for s in range(slots)] for d in range(2)]

    def find(of, a):
        index, found = jnp.int32(0), jnp.int32(0)
        for s in range(slots):
            index = jnp.where(of[s] == a, s, index)
            found = jnp.where(of[s] == a, 1, found)
        return index, found

    def denom_of(owner, o):
        index, found = find(mine, owner * PER_DEV + o)
        d = denom_s[index]
        return jnp.where(found > 0, d, jnp.zeros_like(d))

    den_copies = []
    for k in range(1, N_COL):
        for o in range(PER_DEV):
            den_send[k, o] = denom_of(lax.rem(col + k, N_COL), o)
        den_copies.append(
            push(den_send.at[k], den_recv.at[k], den_send_sem.at[k], den_recv_sem.at[k], others[k - 1])
        )

    emit(0)
    for copy in first_copies:
        copy.wait_recv()

    def block_sum(at_z, at_core, o):
        a = (at_z * 2 + at_core) * PER_DEV + o
        total = jnp.zeros((2, BLOCK // 2, half), F32)
        for i, of in enumerate(ids):
            index, found = find(of, a)
            here = pl.ds(2 * index, 2)
            part = (numer_s[core, here] if i == 0 else sib_numer[here] if i == 1 else pair_numer[i - 2, here])
            total += jnp.where(found > 0, part, jnp.zeros_like(part)).astype(F32)
        return total

    sum_copies = []
    for i, at_core in enumerate((other, core)):
        for o in range(PER_DEV):
            sum_send[i, 2 * o : 2 * o + 2] = block_sum(near_z, at_core, o).astype(BF16)
        sum_copies.append(
            push(sum_send.at[i], sum_recv.at[i], sum_send_sem.at[i], sum_recv_sem.at[i], near)
        )
    for i, at_core in enumerate((other, core)):
        for o in range(PER_DEV):
            total_s[i, 2 * o : 2 * o + 2] = block_sum(z, at_core, o)
    emit(1)
    emit(2)
    sum_copies[0].wait_recv()
    for o in range(PER_DEV):
        here = slice(2 * o, 2 * o + 2)
        last_send[here] = (total_s[0, here] + sum_recv[0, here].astype(F32)).astype(BF16)
    last_copy = push(last_send, last_s.at[core], last_sem.at[0], last_sem.at[1], sibling)
    emit(3)
    for copy in den_copies:
        copy.wait_recv()
    heads = iota((2 * HEADS, width), 0) & 7
    lanes = iota((2 * HEADS, width), 1)
    expand = where01((lanes >= heads * head_dim) & (lanes < (heads + 1) * head_dim))
    scales = []
    for o in range(PER_DEV):
        d = denom_of(col, o)
        for k in range(1, N_COL):
            d += den_recv[k, o]
        inverse = jnp.where(d > 0.0, 1.0 / jnp.where(d > 0.0, d, 1.0), 0.0)
        upper = inverse.astype(BF16).astype(F32)
        scales.append(dot(jnp.concatenate([upper, inverse - upper], axis=0).astype(BF16), expand, TN))
    sum_copies[1].wait_recv()
    for o in range(PER_DEV):
        here = slice(2 * o, 2 * o + 2)
        last_s[core, here] = (total_s[1, here] + sum_recv[1, here].astype(F32)).astype(BF16)
    last_copy.wait_recv()
    for o in range(PER_DEV):
        here = slice(2 * o, 2 * o + 2)
        numer = jnp.concatenate([last_s[side, here].reshape(BLOCK, half) for side in range(2)], axis=1)
        attended = (numer.astype(F32) * scales[o]).astype(BF16)
        base = jnp.concatenate([nodes_h[side, here].reshape(BLOCK, half) for side in range(2)], axis=1)
        mixed = base.astype(F32) + dot(attended, w_s[3])
        mean = jnp.mean(mixed * mixed, axis=1, keepdims=True)
        nodes_out[o * BLOCK : (o + 1) * BLOCK] = (
            mixed * lax.rsqrt(mean + 1e-05) * gain_node_ref[...][None]
        ).astype(BF16)
    for copy in sends:
        copy.wait_send()


def store_kernel(nodes_ref, edge_ref, nodes_out, edges_out, sem):
    slots = edge_ref.shape[0]
    copies = [pltpu.make_async_copy(nodes_ref, nodes_out, sem.at[slots])]
    for s in range(slots):
        copies.append(pltpu.make_async_copy(edge_ref.at[s], edges_out.at[s], sem.at[s]))
    for copy in copies:
        copy.start()
    for copy in copies:
        copy.wait()


def store_call(nodes_new, edges_new):
    vm = pl.BlockSpec(memory_space=pltpu.VMEM)
    hbm = pl.BlockSpec(memory_space=pl.ANY)
    return pl.pallas_call(
        store_kernel,
        in_specs=[vm, vm],
        out_specs=[hbm, hbm],
        out_shape=[
            jax.ShapeDtypeStruct(nodes_new.shape, BF16),
            jax.ShapeDtypeStruct(edges_new.shape, BF16),
        ],
        scratch_shapes=[pltpu.SemaphoreType.DMA((edges_new.shape[0] + 1,))],
        compiler_params=pltpu.CompilerParams(vmem_limit_bytes=1 * 1024 * 1024),
        name="store",
    )(
        pltpu.with_memory_space_constraint(nodes_new, pltpu.VMEM),
        pltpu.with_memory_space_constraint(edges_new, pltpu.VMEM),
    )


def on_device(
    nodes,
    w_query,
    w_key,
    w_value,
    w_out,
    w_edge_gate,
    w_edge_bias,
    w_edge_out,
    gain_node,
    gain_edge,
    edges,
    tile_list,
    tile_count,
):
    rows, width = nodes.shape
    slots = edges.shape[2]
    piece = rows // PIECES
    half = width // 2
    vm = pl.BlockSpec(memory_space=pltpu.VMEM)
    sm = pl.BlockSpec(memory_space=pltpu.SMEM)
    hbm = pl.BlockSpec(memory_space=pl.ANY)
    dma = pltpu.SemaphoreType.DMA
    v = pltpu.VMEM
    nodes_out, edges_out = pl.pallas_call(
        layer_kernel,
        in_specs=[sm, sm, sm] + [hbm] * 10,
        out_specs=[vm, vm],
        out_shape=[v((rows, width), BF16), v((slots, CH, BLOCK, BLOCK), BF16)],
        scratch_shapes=[
            v((2, PIECES, piece, half), BF16),
            v((HEADS, CH), BF16),
            v((HEADS, CH), BF16),
            v((HEADS, CH), F32),
            v((width,), F32),
            v((2, PIECES, piece, half), F32),
            dma((6,)),
            v((NY * PIECES, piece, half), BF16),
            v((NX * PIECES, piece, half), BF16),
            v((4 * PIECES, piece, half), BF16),
            v((2, 2, slots + 1, 2, piece, half), BF16),
            v((2, 2, slots + 1, 2, piece, half), BF16),
            v((2, 2, slots, piece, half), BF16),
            v((2, 2, slots, piece, half), BF16),
            v((slots, 2, 2, piece, half), BF16),
            v((slots, 2, 2, piece, half), BF16),
            v((slots, 2, piece, half), BF16),
            v((8, 128), jnp.int32),
            v((9, 8, 128), jnp.int32),
            pltpu.SMEM((9, 8, 128), jnp.int32),
            dma((2, 2, 3)),
            dma((2, 2, 3)),
            dma((3,)),
            dma((3,)),
            dma((2, 2, slots + 1)),
            dma((2, 2, slots + 1)),
            dma((2, 2, slots)),
            dma((2, 2, slots)),
            dma((slots,)),
            dma((slots,)),
            dma((9,)),
            dma((9,)),
            dma((slots,)),
            dma((slots,)),
            dma,
            v((4, width, width), BF16),
            v((2, slots, 2, piece, half), BF16),
            v((2, slots, 2, piece, half), BF16),
            v((slots, BLOCK, width), BF16),
            v((slots, BLOCK, width), BF16),
            v((slots, BLOCK, width), BF16),
            v((2 * HEADS * GROUP, CH * GROUP), BF16),
            v((CH * GROUP, 2 * HEADS * GROUP), BF16),
            v((slots, HEADS, BLOCK, BLOCK), F32),
            v((slots, HEADS, BLOCK, BLOCK), F32),
            v((slots, HEADS, BLOCK, BLOCK), BF16),
            v((HEADS, BLOCK, BLOCK), BF16),
            v((BLOCK, HEADS * BLOCK), BF16),
            v((CH * GROUP, 2 * BLOCK), F32),
            v((2, 2 * slots, piece, half), BF16),
            v((slots, HEADS, BLOCK), F32),
            dma((slots,)),
            dma((4,)),
            v((2 * slots, piece, half), BF16),
            v((2, 2 * slots, piece, half), BF16),
            v((2, PIECES, piece, half), BF16),
            v((2, PIECES, piece, half), BF16),
            v((PIECES, piece, half), BF16),
            v((2, PIECES, piece, half), BF16),
            v((N_COL, PER_DEV, HEADS, BLOCK), F32),
            v((N_COL, PER_DEV, HEADS, BLOCK), F32),
            dma((slots,)),
            dma((slots,)),
            dma((slots, 2)),
            dma((slots, 2)),
            dma((2,)),
            dma((2,)),
            dma((2,)),
            dma((N_COL,)),
            dma((N_COL,)),
        ],
        compiler_params=pltpu.CompilerParams(
            collective_id=0, has_side_effects=True, vmem_limit_bytes=48 * 1024 * 1024
        ),
        name="layer",
    )(
        tile_list.reshape(-1),
        tile_count.reshape(1),
        gain_edge,
        nodes.reshape(PIECES, piece, width),
        w_edge_bias.T,
        w_edge_gate.T,
        w_edge_out,
        gain_node,
        w_query,
        w_key,
        w_value,
        w_out,
        edges.reshape(slots, CH, BLOCK, BLOCK),
    )

    nodes_out, edges_out = store_call(nodes_out, edges_out)
    return (nodes_out, edges_out.reshape(edges.shape))


def solution(mesh):
    return jax.shard_map(
        on_device,
        mesh=mesh,
        in_specs=(
            P(("row", "col"), None),
            *[P()] * 9,
            P("row", "col", None, None, None, None),
            P("row", "col", None),
            P("row", "col"),
        ),
        out_specs=(P(("row", "col"), None), P("row", "col", None, None, None, None)),
        check_vma=False,
    )
```
